128 devices in a mesh: node: 16 (over z_hi, x, core), group: 8 (over z_lo, y).
Axes of the slice: x: 4, y: 4, z: 4 (z_hi: 2, z_lo: 2; z = z_hi * 2 + z_lo), core: 2. Of those that a mesh axis runs over, the one named last changes fastest.
Arguments:
- tokens: bfloat16 [49152, 5120], P(('node', 'group')), may hold values from -24 to 24
- w_codes: bfloat16 [5120, 2048], P('node'), may hold values from -4 to 4
- w_scale: bfloat16 [5120, 16], P('node'), may hold values from 0.0048828125 to 0.0390625
- gain: float32 [1024], replicated, may hold values from 0.5 to 1.5
- key_cot: bfloat16 [49152, 1024], P(('node', 'group')), may hold values from -8 to 8
- value_cot: bfloat16 [49152, 1024], P(('node', 'group')), may hold values from -6 to 6
- grad_scale: float32 [5120, 16], replicated, may hold values from 39.191837 to 391.91837
Outputs:
- keys: bfloat16 [49152, 1024], P(('node', 'group'))
- values: bfloat16 [49152, 1024], P(('node', 'group'))
- grad_tokens: bfloat16 [49152, 5120], P(('node', 'group'))
- grad_codes: float32 [5120, 2048], P(('node', 'group'))
- grad_gain: float32 [1024], replicated
The draws below stay inside these ranges and needn't reach their ends.
All inputs are finite; a program needn't handle non-finite values.
Results may differ from the reference program's by a relative error of at most 0.027.
Values may be sent and summed in bfloat16 or wider, within the bound.
No kernel may reach another device: no remote copies, remote signals or barrier semaphores. Data moves between devices by JAX's collectives and lax.ppermute only.
A program may use at most 256 MiB of HBM per device.

```python
import math
import jax
import jax.numpy as jnp
from jax import lax

D = 5120
KV = 1024
GROUP = 128
TOK_DEV = 384
TOKENS = 49152
N_NODE = 16
N_GROUP = 8


def draw_key_cot(key, part):
    key = jax.random.fold_in(key, 11)
    rows = jnp.arange(TOKENS, dtype=jnp.float32)[:, None]
    ramp = 0.5 + 1.5 * rows / TOKENS
    base = jax.random.truncated_normal(key, -4.0, 4.0, (TOKENS, KV), jnp.float32)
    return (base * ramp).astype(jnp.bfloat16)


def raised(array, own_key, source, target, shards_of, factor):
    owner, partner = [(jnp.arange(array.shape[dim]) // (array.shape[dim] // shards_of)).reshape([-1 if axis == dim else 1 for axis in range(array.ndim)]) for dim in (source, target)]
    chosen = jax.random.permutation(own_key, shards_of)[partner]
    strong = (owner == chosen) | (owner == (partner + shards_of // 2) % shards_of)
    return jnp.where(strong, factor * array, array)


def shard_levels(key, dims, split, smallest, top_value):
    factor_of = 1.0
    for position, blocks in split:
        heights = jax.random.uniform(jax.random.fold_in(jax.random.fold_in(key, 6), position), (blocks,), jnp.float32, smallest / len(split), top_value / len(split))
        factor_of = factor_of * jnp.repeat(jnp.exp(heights), dims[position] // blocks).reshape((-1,) + (1,) * (len(dims) - 1 - position))
    return factor_of


def bell_draw(key, dims, deviation, bound, shards=(), kind=jnp.bfloat16):
    drawn = jax.random.normal(key, dims, jnp.float32) * deviation
    if len(shards) > 0:
        drawn = shard_levels(key, dims, shards, -0.22, 0.18) * drawn
    return jnp.clip(drawn, min=-bound, max=bound).astype(kind)


def noise_with(stream_key, shape, deviation, bound, shards, heavy, kind=jnp.bfloat16):
    entries = deviation * jax.random.normal(stream_key, shape, jnp.float32)
    if shards:
        entries = entries * shard_levels(stream_key, shape, shards, -0.22, 0.18)
    return jnp.clip(raised(entries, jax.random.fold_in(stream_key, 3), *heavy), -bound, bound).astype(kind)


def setup_inputs(seed: int = 0) -> dict:
    seeds = jax.random.split(jax.random.key(seed), 8)
    return {
        "tokens": noise_with(seeds[0], (TOKENS, D), 1.0, 24.0, ((0, 128),), (0, 1, 128, 5.5)),
        "w_codes": bell_draw(seeds[1], (D, 2 * KV), 1.0, 4.0, ((0, 16),)),
        "w_scale": jnp.clip(jnp.exp(math.log(0.0390625) - 2.0794415 * jax.random.uniform(seeds[2], (D, 2 * KV // GROUP), jnp.float32) ** shard_levels(seeds[2], (D, 2 * KV // GROUP), ((0, 16),), -0.2, 0.2)), 0.0048828125, 0.0390625).astype(jnp.bfloat16),
        "gain": jnp.clip(1.0 + 0.1 * jax.random.normal(seeds[3], (KV,), jnp.float32), 0.5, 1.5),
        "key_cot": draw_key_cot(jax.random.fold_in(seeds[7], 71), 0),
        "value_cot": bell_draw(seeds[5], (TOKENS, KV), 1.0, 6.0, ((0, 128),)),
        "grad_scale": jnp.clip(jnp.exp(jax.random.uniform(seeds[6], (D, 2 * KV // GROUP), jnp.float32, math.log(39.191837), math.log(391.91837))), 39.191837, 391.91837),
    }


def dequantize(codes, scales):
    spread = jnp.repeat(scales.astype(jnp.float32), GROUP, axis=1)
    return (codes.astype(jnp.float32) * spread).astype(jnp.bfloat16)

def reference(tokens, w_codes, w_scale, gain, key_cot, value_cot, grad_scale):
    weight = dequantize(w_codes, w_scale)
    proj = jnp.dot(tokens, weight, preferred_element_type=jnp.float32)
    key_raw = proj[:, :KV]
    inverse = lax.rsqrt(lax.optimization_barrier(jnp.mean(key_raw * key_raw, axis=-1, keepdims=True)) + 1e-06)
    normed = key_raw * inverse
    keys = (normed * gain).astype(jnp.bfloat16)
    values = proj[:, KV:].astype(jnp.bfloat16)
    upstream = key_cot.astype(jnp.float32) * gain
    key_grad = inverse * (upstream - normed * lax.optimization_barrier(jnp.mean(upstream * normed, axis=-1, keepdims=True)))
    grad_out = jnp.concatenate([key_grad.astype(jnp.bfloat16), value_cot], axis=1)
    grad_tokens = lax.dot_general(grad_out, weight, (((1,), (1,)), ((), ())), preferred_element_type=jnp.float32).astype(jnp.bfloat16)
    grad_gain = lax.optimization_barrier(jnp.sum(key_cot.astype(jnp.float32) * normed, axis=0))
    spread = jnp.repeat(grad_scale, GROUP, axis=1)
    tok_blocks = jnp.swapaxes(tokens.reshape(N_NODE, N_GROUP, TOK_DEV, D), 0, 1)
    out_blocks = jnp.swapaxes(grad_out.reshape(N_NODE, N_GROUP, TOK_DEV, 2 * KV), 0, 1)

    def one_group(pair):

        def add_code(total, block):
            product = lax.dot_general(block[0], block[1], (((0,), (0,)), ((), ())), preferred_element_type=jnp.float32)
            coded = lax.optimization_barrier((product / spread).astype(jnp.bfloat16)).astype(jnp.float32)
            return (total + coded, None)
        total, unused = lax.scan(add_code, jnp.zeros((D, 2 * KV), jnp.float32), pair)
        return lax.optimization_barrier(total.astype(jnp.bfloat16)).astype(jnp.float32)
    partials = lax.map(one_group, (tok_blocks, out_blocks))
    grad_codes = lax.optimization_barrier(jnp.sum(partials, axis=0))
    return (keys, values, grad_tokens, grad_codes, grad_gain)
```

```python
import jax
import jax.numpy as jnp
from jax import lax
from jax.experimental import pallas as pl
from jax.experimental.pallas import tpu as pltpu
from jax.sharding import PartitionSpec as P

BF = jnp.bfloat16
F32 = jnp.float32
GROUP = 128
AXES = ("node", "group")
TOK = 384
ROWS = 320
SHARD = 640
D = 5120
KV = 1024
HALF = 512
QUART = 256
VMEM_LIMIT = 56 * 2**20


def coords(i):
    y, z_lo, core, x, z_hi = i % 4, (i // 4) % 2, (i // 8) % 2, (i // 16) % 4, i // 64
    return z_hi * 2 + z_lo, x, core, y


def flat(z, x, core, y):
    return (((z // 2 * 4 + x) * 2 + core) * 2 + z % 2) * 4 + y


def near(n, which):
    return n ^ 1 if which == 0 else 3 - n


def pairs_of(axis, step):
    out = []
    for i in range(128):
        z, x, core, y = coords(i)
        if axis == "core":
            out.append((i, flat(z, x, 1 - core, y)))
            continue
        which = step ^ core
        if axis == "x":
            out.append((i, flat(z, near(x, which), core, y)))
        if axis == "y":
            out.append((i, flat(z, x, core, near(y, which))))
        if axis == "z":
            out.append((i, flat(near(z, which), x, core, y)))
    return out


def pairs_zb():
    out = []
    for i in range(128):
        z, x, core, y = coords(i)
        out.append((i, flat(3 - z, x, core, y)))
    return out


def swap(v, axis, step=0):
    return lax.ppermute(v, AXES, pairs_of(axis, step))


def swap_zb(v):
    return lax.ppermute(v, AXES, pairs_zb())


def params():
    return pltpu.CompilerParams(vmem_limit_bytes=VMEM_LIMIT)


def cost(flops, nbytes):
    return pl.CostEstimate(flops=int(flops), bytes_accessed=int(nbytes), transcendentals=0)


def dequant_kernel(core_ref, own_ref, oth_ref, s_own_ref, s_oth_ref, ka, kb, va, vb):
    for c in (0, 1):

        @pl.when(core_ref[0] == c)
        def _():
            for r in (0, 1):
                codes = own_ref if r == c else oth_ref
                scale = s_own_ref if r == c else s_oth_ref
                for n, out in enumerate((ka, kb, va, vb)):
                    base = (n // 2) * 8 + c * 4 + (n % 2) * 2
                    for j in (0, 1):
                        b = base + j
                        out[r * ROWS : (r + 1) * ROWS, j * GROUP : (j + 1) * GROUP] = (
                            codes[:, b * GROUP : (b + 1) * GROUP].astype(F32)
                            * scale[:, b : b + 1].astype(F32)
                        ).astype(BF)


def dequant(core, own, oth, s_own, s_oth):
    vm = pl.BlockSpec(memory_space=pltpu.VMEM)
    return pl.pallas_call(
        dequant_kernel,
        grid_spec=pltpu.PrefetchScalarGridSpec(
            num_scalar_prefetch=1, grid=(), in_specs=[vm] * 4, out_specs=[vm] * 4
        ),
        out_shape=[jax.ShapeDtypeStruct((SHARD, QUART), BF)] * 4,
        compiler_params=params(),
        cost_estimate=cost(2e6, 4e6),
        name="dequant",
    )(core, own, oth, s_own, s_oth)


def dot(a, b):
    return jnp.dot(a, b, preferred_element_type=F32)


def fwd_early_kernel(ids, toa, tta, tob, ttb, wa, wb, out):
    @pl.when(pl.program_id(0) == 0)
    def _():
        out[...] = jnp.zeros_like(out)

    out[:TOK, :QUART] += dot(toa[...], wa[0])
    out[TOK:, :QUART] += dot(tta[...], wa[0])
    out[:TOK, QUART:] += dot(tob[...], wb[0])
    out[TOK:, QUART:] += dot(ttb[...], wb[0])


def tok_spec(offset):
    return pl.BlockSpec((TOK, SHARD), lambda j, ids: (0, ids[offset + j]))


def w_spec():
    return pl.BlockSpec((1, SHARD, QUART), lambda j, ids: (j, 0, 0))


def fwd_early(ids, t_own, t_oth, wa, wb):
    return pl.pallas_call(
        fwd_early_kernel,
        grid_spec=pltpu.PrefetchScalarGridSpec(
            num_scalar_prefetch=1,
            grid=(4,),
            in_specs=[tok_spec(0), tok_spec(0), tok_spec(4), tok_spec(4), w_spec(), w_spec()],
            out_specs=pl.BlockSpec((2 * TOK, HALF), lambda j, ids: (0, 0)),
        ),
        out_shape=jax.ShapeDtypeStruct((2 * TOK, HALF), F32),
        compiler_params=params(),
        cost_estimate=cost(2 * 768 * 2560 * 512, 12e6),
        name="key_projection_early",
    )(ids, t_own, t_oth, t_own, t_oth, wa, wb)


def fwd_late_kernel(ids, raw, toa, tta, tob, ttb, wa, wb, co, ct, gain, out, stats):
    @pl.when(pl.program_id(0) == 0)
    def _():
        out[...] = raw[...]

    out[:TOK, :QUART] += dot(toa[...], wa[0])
    out[TOK:, :QUART] += dot(tta[...], wa[0])
    out[:TOK, QUART:] += dot(tob[...], wb[0])
    out[TOK:, QUART:] += dot(ttb[...], wb[0])

    @pl.when(pl.program_id(0) == 3)
    def _():
        lane = lax.broadcasted_iota(jnp.int32, (TOK, GROUP), 1)
        for n, cot in enumerate((co, ct)):
            part = out[n * TOK : (n + 1) * TOK, :]
            square = jnp.sum(part * part, axis=1, keepdims=True)
            cross = jnp.sum(part * (cot[...].astype(F32) * gain[...]), axis=1, keepdims=True)
            stats[n * TOK : (n + 1) * TOK, :] = jnp.where(
                lane == 0, square, jnp.where(lane == 1, cross, 0.0)
            )


def fwd_late(ids, raw, t_own, t_oth, wa, wb, cot_own, cot_oth, gain):
    full = pl.BlockSpec((2 * TOK, HALF), lambda j, ids: (0, 0))
    cot = pl.BlockSpec((TOK, HALF), lambda j, ids: (0, ids[8]))
    return pl.pallas_call(
        fwd_late_kernel,
        grid_spec=pltpu.PrefetchScalarGridSpec(
            num_scalar_prefetch=1,
            grid=(4,),
            in_specs=[full, tok_spec(0), tok_spec(0), tok_spec(4), tok_spec(4), w_spec(), w_spec()]
            + [cot, cot, pl.BlockSpec((1, HALF), lambda j, ids: (0, ids[8]))],
            out_specs=[full, pl.BlockSpec((2 * TOK, GROUP), lambda j, ids: (0, 0))],
        ),
        out_shape=[
            jax.ShapeDtypeStruct((2 * TOK, HALF), F32),
            jax.ShapeDtypeStruct((2 * TOK, GROUP), F32),
        ],
        compiler_params=params(),
        cost_estimate=cost(2 * 768 * 2560 * 512, 14e6),
        name="key_projection_late",
    )(ids, raw, t_own, t_oth, t_own, t_oth, wa, wb, cot_own, cot_oth, gain)


def norm_kernel(ids, raw, mine, theirs, co, ct, gain, k_own, k_oth, g_own, g_oth, gsum):
    total = jnp.zeros((8, HALF), F32)
    for n, (cot, keys, grad) in enumerate(((co, k_own, g_own), (ct, k_oth, g_oth))):
        here = slice(n * TOK, (n + 1) * TOK)
        there = slice((1 - n) * TOK, (2 - n) * TOK)
        square = mine[here, 0:1] + theirs[there, 0:1]
        cross = mine[here, 1:2] + theirs[there, 1:2]
        inverse = lax.rsqrt(square * (1.0 / KV) + 1e-06)
        normed = raw[here, :] * inverse
        cotangent = cot[...].astype(F32)
        keys[...] = (normed * gain[...]).astype(BF)
        upstream = cotangent * gain[...]
        mean = cross * inverse * (1.0 / KV)
        grad[...] = (inverse * (upstream - normed * mean)).astype(BF)
        total += jnp.sum((cotangent * normed).reshape(TOK // 8, 8, HALF), axis=0)
    gsum[...] = jnp.broadcast_to(jnp.sum(total, axis=0, keepdims=True), (8, HALF))


def norm(ids, raw, mine, theirs, cot_own, cot_oth, gain):
    def whole(*shape):
        return pl.BlockSpec(shape, lambda j, ids: (0, 0))

    cot = pl.BlockSpec((TOK, HALF), lambda j, ids: (0, ids[8]))
    return pl.pallas_call(
        norm_kernel,
        grid_spec=pltpu.PrefetchScalarGridSpec(
            num_scalar_prefetch=1,
            grid=(1,),
            in_specs=[whole(2 * TOK, HALF), whole(2 * TOK, GROUP), whole(2 * TOK, GROUP)]
            + [cot, cot, pl.BlockSpec((1, HALF), lambda j, ids: (0, ids[8]))],
            out_specs=[whole(TOK, HALF)] * 4 + [whole(8, HALF)],
        ),
        out_shape=[jax.ShapeDtypeStruct((TOK, HALF), BF)] * 4
        + [jax.ShapeDtypeStruct((8, HALF), F32)],
        compiler_params=params(),
        cost_estimate=cost(8e6, 5e6),
        name="key_norm",
    )(ids, raw, mine, theirs, cot_own, cot_oth, gain)


def pick_early(w1, w2):
    return jnp.where(pl.program_id(0) < 4, w1[0], w2[0])


def pick_even(w1, w2):
    return jnp.where(pl.program_id(0) % 2 == 0, w1[0], w2[0])


def w_all_specs():
    first = pl.BlockSpec((1, SHARD, QUART), lambda j, ids: (jnp.minimum(j, 3), 0, 0))
    second = pl.BlockSpec((1, SHARD, QUART), lambda j, ids: (jnp.maximum(j - 4, 0), 0, 0))
    half = pl.BlockSpec((1, SHARD, QUART), lambda j, ids: (j // 2, 0, 0))
    return [first, second, half, half]


def fwd_value_kernel(ids, to, tt, a1, a2, b1, b2, v_own, v_oth, acc):
    wa, wb = pick_early(a1, a2), pick_even(b1, b2)

    @pl.when(pl.program_id(0) == 0)
    def _():
        acc[...] = jnp.zeros_like(acc)

    for n, tokens in enumerate((to, tt)):
        here = slice(n * TOK, (n + 1) * TOK)
        acc[here, :QUART] += dot(tokens[...], wa)
        acc[here, QUART:] += dot(tokens[...], wb)

    @pl.when(pl.program_id(0) == 7)
    def _():
        v_own[...] = acc[:TOK, :].astype(BF)
        v_oth[...] = acc[TOK:, :].astype(BF)


def fwd_value(ids, t_own, t_oth, weights):
    tok = pl.BlockSpec((TOK, SHARD), lambda j, ids: (0, ids[j]))
    out = pl.BlockSpec((TOK, HALF), lambda j, ids: (0, 0))
    return pl.pallas_call(
        fwd_value_kernel,
        grid_spec=pltpu.PrefetchScalarGridSpec(
            num_scalar_prefetch=1,
            grid=(8,),
            in_specs=[tok, tok] + w_all_specs(),
            out_specs=[out, out],
            scratch_shapes=[pltpu.VMEM((2 * TOK, HALF), F32)],
        ),
        out_shape=[jax.ShapeDtypeStruct((TOK, HALF), BF)] * 2,
        compiler_params=params(),
        cost_estimate=cost(2 * 768 * 5120 * 512, 14e6),
        name="value_projection",
    )(ids, t_own, t_oth, *weights)


def back(g_key, g_val, refs):
    ka = pick_early(refs[0], refs[1])
    kb = pick_even(refs[2], refs[3])
    va = pick_early(refs[4], refs[5])
    vb = pick_even(refs[6], refs[7])
    nt = (((1,), (1,)), ((), ()))
    total = lax.dot_general(g_key[:, :QUART], ka, nt, preferred_element_type=F32)
    total += lax.dot_general(g_key[:, QUART:], kb, nt, preferred_element_type=F32)
    total += lax.dot_general(g_val[:, :QUART], va, nt, preferred_element_type=F32)
    total += lax.dot_general(g_val[:, QUART:], vb, nt, preferred_element_type=F32)
    return total


def back_kernel(ids, g_key, g_val, *refs):
    refs[8][...] = back(g_key, g_val, refs).astype(BF)


def back_add_kernel(ids, g_key, g_val, *refs):
    refs[9][...] = (back(g_key, g_val, refs) + refs[8][...].astype(F32)).astype(BF)


def grad_tokens_of(ids, g_key, g_val, weights_k, weights_v, received=None):
    block = pl.BlockSpec((TOK, SHARD), lambda j, ids: (0, ids[j]))
    specs = [
        pl.BlockSpec((TOK, HALF), lambda j, ids: (0, 0)),
        pl.BlockSpec((TOK, HALF), lambda j, ids: (0, ids[8])),
    ]
    extra = [] if received is None else [received]
    return pl.pallas_call(
        back_kernel if received is None else back_add_kernel,
        grid_spec=pltpu.PrefetchScalarGridSpec(
            num_scalar_prefetch=1,
            grid=(8,),
            in_specs=specs + w_all_specs() * 2 + [block] * len(extra),
            out_specs=block,
        ),
        out_shape=jax.ShapeDtypeStruct((TOK, D), BF),
        compiler_params=params(),
        cost_estimate=cost(2 * 384 * 5120 * 1024, 16e6),
        name="token_gradient" if received is None else "token_gradient_sum",
    )(ids, g_key, g_val, *weights_k, *weights_v, *extra)


def codes_product(ids, to, tt, go, gt, scale, base, prod, width):
    tn = (((0,), (0,)), ((), ()))
    total = lax.dot_general(to[...], go[...], tn, preferred_element_type=F32)
    total += lax.dot_general(tt[...], gt[...], tn, preferred_element_type=F32)
    for j in range(width // GROUP):
        prod[:, j * GROUP : (j + 1) * GROUP] = (
            total[:, j * GROUP : (j + 1) * GROUP] / scale[:, base + j : base + j + 1]
        )


def piece(prod, offset):
    low = prod[pl.ds(pl.multiple_of(offset, 8), 40), :]
    high = prod[pl.ds(pl.multiple_of(offset + ROWS, 8), 40), :]
    return jnp.concatenate([low, high], axis=0).astype(BF)


def codes_y_kernel(base, width, ids, to, tt, go, gt, scale, keep, send, prod):
    codes_product(ids, to, tt, go, gt, scale, base, prod, width)
    k = pl.program_id(1)
    for m in (0, 1):
        z_slot = ids[8 + k * 2 + m]
        z_lo = ids[12 + m]
        for s in range(4):
            offset = z_lo * 160 + ids[14 + s] * 40
            out = keep if s < 2 else send
            out[s % 2, z_slot, 0] = piece(prod, offset)


def codes_x_kernel(base, width, ids, to, tt, go, gt, scale, keep, send, prod):
    codes_product(ids, to, tt, go, gt, scale, base, prod, width)
    k = pl.program_id(1)
    first = pl.program_id(0) < 2
    for m in (0, 1):
        z_slot = ids[8 + k * 2 + m]
        z_lo = ids[12 + m]
        for s in range(4):
            offset = z_lo * 160 + ids[14 + s] * 40
            value = piece(prod, offset)

            @pl.when(first)
            def _():
                send[0, s, z_slot] = value

            @pl.when(jnp.logical_not(first))
            def _():
                keep[0, s, z_slot] = value


def codes(kind, ids, t_own, t_oth, g_own, g_oth, scale, base, width, g_block):
    if kind == "y":
        order = lambda i: i
        shape = (2, 4, 4, 80, width)
        out_k = out_s = pl.BlockSpec((2, 4, 1, 80, width), lambda i, k, ids: (0, 0, i, 0, 0))
        body = codes_y_kernel
    else:
        order = lambda i: (i + 2) % 4
        shape = (2, 4, 4, 80, width)
        out_k = pl.BlockSpec((1, 4, 4, 80, width), lambda i, k, ids: (jnp.maximum(i - 2, 0), 0, 0, 0, 0))
        out_s = pl.BlockSpec((1, 4, 4, 80, width), lambda i, k, ids: (jnp.minimum(i, 1), 0, 0, 0, 0))
        body = codes_x_kernel
    tok = pl.BlockSpec((TOK, SHARD), lambda i, k, ids: (0, ids[order(i) * 2 + k]))
    grad = pl.BlockSpec((TOK, width), lambda i, k, ids: (0, g_block(ids)))
    return pl.pallas_call(
        lambda *refs: body(base, width, *refs),
        grid_spec=pltpu.PrefetchScalarGridSpec(
            num_scalar_prefetch=1,
            grid=(4, 2),
            in_specs=[tok, tok, grad, grad]
            + [pl.BlockSpec((SHARD, 8), lambda i, k, ids: (ids[order(i) * 2 + k], 0))],
            out_specs=[out_k, out_s],
            scratch_shapes=[pltpu.VMEM((SHARD, width), F32)],
        ),
        out_shape=[jax.ShapeDtypeStruct(shape, BF)] * 2,
        compiler_params=params(),
        cost_estimate=cost(2 * 768 * 5120 * width, 8e6 + 5120 * width * 2),
        name="weight_gradient_codes",
    )(ids, t_own, t_oth, g_own, g_oth, scale)


def f32(v):
    return v.astype(F32)


def reduce_axis(axis, keep, send):
    first = swap(send, axis, 0)
    second = swap((f32(keep[1]) + f32(first[1])).astype(BF), axis, 1)
    return f32(keep[0]) + f32(first[0]) + f32(second)


def reduce_all(order, keep, send):
    total = reduce_axis(order[0], keep, send)
    for axis in order[1:]:
        total = reduce_axis(axis, total[:2].astype(BF), total[2:].astype(BF))
    return total


def gather(ha, hb):
    g = swap_zb(ha)
    x1 = swap(hb, "x", 0)
    s1 = jnp.stack([ha, g])
    r1 = swap(s1, "x", 0)
    s2 = jnp.stack([hb, x1])
    q2 = swap(s2, "x", 1)
    c1 = jnp.concatenate([s1, r1])
    r2 = swap(c1, "x", 1)
    c2 = jnp.concatenate([s2, q2])
    rz = swap_zb(c2)
    return c1, r2, c2, rz


def on_device(tokens, w_codes, w_scale, gain, key_cot, value_cot, grad_scale):
    node, group = lax.axis_index("node"), lax.axis_index("group")
    z_hi, x, core = node // 8, (node // 2) % 4, node % 2
    z_lo, y = group // 4, group % 4
    z = z_hi * 2 + z_lo

    def ring(n):
        a, b = n ^ 1, 3 - n
        first, second = jnp.where(core == 0, a, b), jnp.where(core == 0, b, a)
        return [n, second, first, (n + 2) % 4]

    x_of, y_of, z_of = ring(x), ring(y), ring(z)
    gx = [x_of[0], x_of[2], x_of[1], x_of[3]]
    sid = {(dz, dx): (z_hi ^ dz) * 4 + gx[dx] for dz in (0, 1) for dx in range(4)}
    order = [(dz, dx) for dx in range(4) for dz in (0, 1)]
    as_ids = lambda values: jnp.stack([jnp.asarray(v, jnp.int32) for v in values])
    ids_all = as_ids([sid[o] for o in order] + [core])
    ids_early = as_ids([sid[o] for o in order[:4]] + [sid[(0, dx)] for dx in range(4)] + [core])
    ids_late = as_ids([sid[o] for o in order[4:]] + [sid[(1, dx)] for dx in range(4)] + [core])

    def slot_of(places, n):
        return sum(jnp.where(places[s] == n, s, 0) for s in range(4))

    z_slots = [slot_of(z_of, (z_hi ^ k) * 2 + (z_lo ^ m)) for k in (0, 1) for m in (0, 1)]
    ids_codes = as_ids(
        [(z_hi ^ k) * 4 + x_of[s] for s in range(4) for k in (0, 1)]
        + z_slots
        + [z_lo, z_lo ^ 1]
        + y_of
        + [core]
    )

    codes_oth = swap(w_codes, "core")
    scale_oth = swap(w_scale, "core")
    t_oth = swap(tokens, "core")
    vc_oth = swap(value_cot, "core")
    kc_oth = swap(key_cot, "core")
    core1 = as_ids([core])
    ka, kb, va, vb = dequant(core1, w_codes, codes_oth, w_scale, scale_oth)
    weights_k = gather(ka, kb)
    weights_v = gather(va, vb)

    scale_cols = jnp.concatenate(
        [
            lax.dynamic_slice_in_dim(grad_scale, core * 4, 4, axis=1),
            lax.dynamic_slice_in_dim(grad_scale, 8 + core * 4, 4, axis=1),
        ],
        axis=1,
    )
    v_keep, v_send = codes(
        "y", ids_codes, tokens, t_oth, value_cot, vc_oth, scale_cols, 4, HALF, lambda ids: ids[18]
    )
    sum_v = reduce_all(("y", "z", "x"), v_keep, v_send)

    gain2 = gain.reshape(1, KV)
    c1, r2, c2, rz = weights_k
    raw = fwd_early(ids_early, tokens, t_oth, c1, c2)
    raw, stats = fwd_late(ids_late, raw, tokens, t_oth, r2, rz, key_cot, kc_oth, gain2)
    stats_oth = swap(stats, "core")
    k_own, k_oth, g_own, g_oth, gsum = norm(ids_all, raw, stats, stats_oth, key_cot, kc_oth, gain2)

    a_keep, a_send = codes(
        "y", ids_codes, tokens, t_oth, g_own, g_oth, scale_cols, 0, QUART, lambda ids: 0
    )
    b_keep, b_send = codes(
        "x", ids_codes, tokens, t_oth, g_own, g_oth, scale_cols, 2, QUART, lambda ids: 1
    )
    sum_a = reduce_all(("y", "z", "x"), a_keep, a_send)
    sum_b = reduce_all(("x", "y", "z"), b_keep, b_send)

    for axis in ("x", "y", "z"):
        for step in (0, 1):
            gsum = gsum + swap(gsum, axis, step)
    gsum_oth = swap(gsum, "core")

    v_own, v_oth = fwd_value(ids_all, tokens, t_oth, weights_v)
    sent = grad_tokens_of(ids_all, g_oth, vc_oth, weights_k, weights_v)
    received = swap(sent, "core")
    grad_tokens = grad_tokens_of(ids_all, g_own, value_cot, weights_k, weights_v, received)

    def both(mine, theirs, axis):
        return jnp.where(
            core == 0,
            jnp.concatenate([mine, theirs], axis=axis),
            jnp.concatenate([theirs, mine], axis=axis),
        )

    keys = both(k_own, swap(k_oth, "core"), 1)
    values = both(v_own, swap(v_oth, "core"), 1)
    total = jnp.concatenate([sum_a, sum_b, sum_v], axis=1).reshape(2, 40, KV)
    mine = lax.dynamic_index_in_dim(total, core, 0, keepdims=False)
    theirs = swap(lax.dynamic_index_in_dim(total, 1 - core, 0, keepdims=False), "core")
    grad_codes = jnp.concatenate(
        [both(mine[:, :HALF], theirs[:, :HALF], 1), both(mine[:, HALF:], theirs[:, HALF:], 1)], axis=1
    )
    grad_gain = both(gsum[0], gsum_oth[0], 0)
    return (keys, values, grad_tokens, grad_codes, grad_gain)


def solution(mesh):
    rows = P(("node", "group"), None)
    in_specs = (rows, P("node", None), P("node", None), P(), rows, rows, P())
    out_specs = (rows, rows, rows, rows, P())
    return jax.shard_map(
        on_device, mesh=mesh, in_specs=in_specs, out_specs=out_specs, check_vma=False
    )
```

```python
import jax
import jax.numpy as jnp
from jax import lax
from jax.experimental import pallas as pl
from jax.experimental.pallas import tpu as pltpu
from jax.sharding import PartitionSpec as P

BF = jnp.bfloat16
F32 = jnp.float32
GROUP = 128
AXES = ("node", "group")
TOK = 384
ROWS = 320
SHARD = 640
D = 5120
KV = 1024
HALF = 512
QUART = 256
VMEM_LIMIT = 20 * 2**20
NT = (((1,), (1,)), ((), ()))
TN = (((0,), (0,)), ((), ()))


def coords(i):
    y, z_lo, core, x, z_hi = i % 4, (i // 4) % 2, (i // 8) % 2, (i // 16) % 4, i // 64
    return z_hi * 2 + z_lo, x, core, y


def flat(z, x, core, y):
    return (((z // 2 * 4 + x) * 2 + core) * 2 + z % 2) * 4 + y


def near(n, which):
    return n ^ 1 if which == 0 else 3 - n


def pairs_of(axis, step):
    out = []
    for i in range(128):
        z, x, core, y = coords(i)
        which = step ^ core
        if axis == "core":
            out.append((i, flat(z, x, 1 - core, y)))
        if axis == "x":
            out.append((i, flat(z, near(x, which), core, y)))
        if axis == "y":
            out.append((i, flat(z, x, core, near(y, which))))
        if axis == "z":
            out.append((i, flat(near(z, which), x, core, y)))
        if axis == "zb":
            out.append((i, flat(3 - z, x, core, y)))
    return out


def swap(v, axis, step=0):
    return lax.ppermute(v, AXES, pairs_of(axis, step))


def dot(a, b, dims=(((1,), (0,)), ((), ()))):
    return lax.dot_general(a, b, dims, preferred_element_type=F32)


def f32(v):
    return v.astype(F32)


def columns(n):
    return pl.ds(pl.multiple_of(n * SHARD, GROUP), SHARD)


class Chain:
    def __init__(self):
        self.last = None

    def __call__(self, name, body, ids, arrays, shapes, scratch, flops):
        vm = pl.BlockSpec(memory_space=pltpu.VMEM)
        n_in = len(arrays)
        extra = [] if self.last is None else [self.last]

        def kernel(*refs):
            body(refs[0], refs[1 : 1 + n_in], refs[1 + n_in + len(extra) :])

        out = pl.pallas_call(
            kernel,
            in_specs=[pl.BlockSpec(memory_space=pltpu.SMEM)]
            + [vm] * n_in
            + [pl.BlockSpec(memory_space=pl.ANY)] * len(extra),
            out_specs=[vm] * len(shapes),
            out_shape=[jax.ShapeDtypeStruct(s, t) for s, t in shapes],
            scratch_shapes=list(scratch),
            compiler_params=pltpu.CompilerParams(vmem_limit_bytes=VMEM_LIMIT),
            cost_estimate=pl.CostEstimate(flops=flops, bytes_accessed=1000, transcendentals=0),
            name=name,
        )(ids, *arrays, *extra)
        self.last = out[-1]
        return out


CORE = 8


def dequant_body(ids, ins, outs):
    own, oth, s_own, s_oth = ins
    for c in (0, 1):

        @pl.when(ids[CORE] == c)
        def _():
            for r in (0, 1):
                codes = own if r == c else oth
                scale = s_own if r == c else s_oth
                for n, out in enumerate(outs):
                    for j in (0, 1):
                        b = (n // 2) * 8 + c * 4 + (n % 2) * 2 + j
                        out[r * ROWS : (r + 1) * ROWS, j * GROUP : (j + 1) * GROUP] = (
                            f32(codes[:, b * GROUP : (b + 1) * GROUP]) * f32(scale[:, b : b + 1])
                        ).astype(BF)


def stack_body(ids, ins, outs):
    outs[0][0] = ins[0][...]
    outs[0][1] = ins[1][...]


def add_products(ids, tokens, out, pieces, first):
    fresh = [first, first]
    for ref, n, shard, half in pieces:
        cols = slice(half * QUART, (half + 1) * QUART)
        for t, tok in enumerate(tokens):
            here = slice(t * TOK, (t + 1) * TOK)
            value = dot(tok[:, columns(ids[shard])], ref[n])
            if fresh[half]:
                out[here, cols] = value
            else:
                out[here, cols] += value
        fresh[half] = False


def early_pieces(s1, r1, s2, q2):
    return [(s1, 0, 0, 0), (s1, 1, 4, 0), (r1, 0, 1, 0), (r1, 1, 5, 0)] + [
        (s2, 0, 0, 1), (s2, 1, 1, 1), (q2, 0, 2, 1), (q2, 1, 3, 1)
    ]


def late_pieces(q1, p1, za, zc):
    return [(q1, 0, 2, 0), (q1, 1, 6, 0), (p1, 0, 3, 0), (p1, 1, 7, 0)] + [
        (za, 0, 4, 1), (za, 1, 5, 1), (zc, 0, 6, 1), (zc, 1, 7, 1)
    ]


def early_body(ids, ins, outs):
    add_products(ids, ins[:2], outs[0], early_pieces(*ins[2:6]), True)


def cot_columns(ref, core):
    return ref[:, pl.ds(pl.multiple_of(core * HALF, GROUP), HALF)]


def late_body(ids, ins, outs):
    raw, cot_own, cot_oth, gain = ins[6:10]
    out, stats = outs
    out[...] = raw[...]
    add_products(ids, ins[:2], out, late_pieces(*ins[2:6]), False)
    lane = lax.broadcasted_iota(jnp.int32, (TOK, GROUP), 1)
    weight = cot_columns(gain, ids[CORE])
    for n, cot in enumerate((cot_own, cot_oth)):
        part = out[n * TOK : (n + 1) * TOK, :]
        square = jnp.sum(part * part, axis=1, keepdims=True)
        cross = jnp.sum(part * (f32(cot_columns(cot, ids[CORE])) * weight), axis=1, keepdims=True)
        stats[n * TOK : (n + 1) * TOK, :] = jnp.where(
            lane == 0, square, jnp.where(lane == 1, cross, 0.0)
        )


def norm_body(ids, ins, outs):
    raw, mine, theirs, cot_own, cot_oth, gain = ins
    gsum = outs[4]
    weight = cot_columns(gain, ids[CORE])
    total = jnp.zeros((8, HALF), F32)
    for n, cot in enumerate((cot_own, cot_oth)):
        here = slice(n * TOK, (n + 1) * TOK)
        there = slice((1 - n) * TOK, (2 - n) * TOK)
        square = mine[here, 0:1] + theirs[there, 0:1]
        cross = mine[here, 1:2] + theirs[there, 1:2]
        inverse = lax.rsqrt(square * (1.0 / KV) + 1e-06)
        normed = raw[here, :] * inverse
        cotangent = f32(cot_columns(cot, ids[CORE]))
        outs[n][...] = (normed * weight).astype(BF)
        mean = cross * inverse * (1.0 / KV)
        outs[2 + n][...] = (inverse * (cotangent * weight - normed * mean)).astype(BF)
        total += jnp.sum((cotangent * normed).reshape(TOK // 8, 8, HALF), axis=0)
    gsum[...] = jnp.broadcast_to(jnp.sum(total, axis=0, keepdims=True), (8, HALF))


def value_body(ids, ins, outs):
    acc = outs[2]
    add_products(ids, ins[:2], acc, early_pieces(*ins[2:6]), True)
    add_products(ids, ins[:2], acc, late_pieces(*ins[6:10]), False)
    outs[0][...] = acc[:TOK, :].astype(BF)
    outs[1][...] = acc[TOK:, :].astype(BF)


def back_body(ids, ins, outs):
    g_key, g_val = ins[:2]
    received = ins[18] if len(ins) > 18 else None
    grad = jnp.concatenate([g_key[...], cot_columns(g_val, ids[CORE])], axis=1)
    where = {}
    for part, refs in ((0, ins[2:10]), (1, ins[10:18])):
        for ref, n, shard, half in early_pieces(*refs[:4]) + late_pieces(*refs[4:]):
            where[shard, part * 2 + half] = (ref, n)
    for shard in range(8):
        weight = jnp.concatenate([where[shard, q][0][where[shard, q][1]] for q in range(4)], axis=1)
        value = dot(grad, weight, NT)
        if received is not None:
            value += f32(received[:, columns(ids[shard])])
        outs[0][:, columns(ids[shard])] = value.astype(BF)
    if received is not None:
        outs[1][...] = jnp.zeros_like(outs[1])


def piece(prod, offset):
    low = prod[pl.ds(pl.multiple_of(offset, 8), 40), :]
    high = prod[pl.ds(pl.multiple_of(offset + ROWS, 8), 40), :]
    return jnp.concatenate([low, high], axis=0).astype(BF)


def codes_body(kind, base, width, grads, ids, ins, outs):
    t_own, t_oth, g_own, g_oth, scale = ins
    keep, send, prod = outs
    g_own, g_oth = grads(ids, g_own), grads(ids, g_oth)

    def block_codes(near_half, pair, k):
        sx = pair + (0 if near_half else 2)
        block = ids[9 + sx * 2 + k]
        total = dot(t_own[:, columns(block)], g_own, TN) + dot(t_oth[:, columns(block)], g_oth, TN)
        rows = pl.ds(pl.multiple_of(block * SHARD, SHARD), SHARD)
        factor = scale[rows, base : base + width // GROUP]
        for j in range(width // GROUP):
            cols = slice(j * GROUP, (j + 1) * GROUP)
            prod[:, cols] = total[:, cols] * factor[:, j : j + 1]
        for m in (0, 1):
            z_slot = ids[17 + k * 2 + m]
            for s in range(4):
                value = piece(prod, ids[21 + m] * 160 + ids[23 + s] * 40)
                if kind == "y":
                    (keep if s < 2 else send)[s % 2, sx, z_slot] = value
                else:
                    (keep if near_half else send)[pair, s, z_slot] = value

    for near_half in (False, True):

        @pl.loop(0, 2)
        def _(pair):
            block_codes(near_half, pair, 0)
            block_codes(near_half, pair, 1)


def add2_body(ids, ins, outs):
    outs[0][...] = (f32(ins[0][1]) + f32(ins[1][1])).astype(BF)


def add3_body(ids, ins, outs):
    keep, first, second = ins
    for out, at in ((outs[0], 0), (outs[1], 2)):
        for s in (0, 1):
            out[s] = (f32(keep[0, at + s]) + f32(first[0, at + s]) + f32(second[at + s])).astype(BF)


def merge_body(ids, ins, outs):
    for n, (at, width) in enumerate(((0, QUART), (QUART, QUART), (HALF, HALF))):
        keep, first, second = ins[3 * n : 3 * n + 3]
        for s in range(4):
            outs[s // 2][s % 2, :, at : at + width] = (
                f32(keep[0, s]) + f32(first[0, s]) + f32(second[s])
            ).astype(BF)


def last_body(ids, ins, outs):
    keep, first, second = ins
    mine, theirs, total = outs
    total[...] = f32(keep[0]) + f32(first[0]) + f32(second[...])
    mine[...] = total[pl.ds(pl.multiple_of(ids[CORE] * 40, 8), 40), :]
    theirs[...] = total[pl.ds(pl.multiple_of(40 - ids[CORE] * 40, 8), 40), :]


def place_body(ids, ins, outs):
    mine, theirs = ins
    for c in (0, 1):

        @pl.when(ids[CORE] == c)
        def _():
            for n in range(4):
                source = mine if n % 2 == c else theirs
                outs[0][:, n * HALF : (n + 1) * HALF] = source[:, n // 2 * HALF : (n // 2 + 1) * HALF]


def plus_body(ids, ins, outs):
    outs[0][...] = ins[0][...] + ins[1][...]


def on_device(tokens, w_codes, w_scale, gain, key_cot, value_cot, grad_scale):
    node, group = lax.axis_index("node"), lax.axis_index("group")
    z_hi, x, core = node // 8, (node // 2) % 4, node % 2
    z_lo, y = group // 4, group % 4
    z = z_hi * 2 + z_lo

    def ring(n):
        a, b = n ^ 1, 3 - n
        first, second = jnp.where(core == 0, a, b), jnp.where(core == 0, b, a)
        return [n, second, first, (n + 2) % 4]

    x_of, y_of, z_of = ring(x), ring(y), ring(z)
    slot_of = lambda places, n: sum(jnp.where(places[s] == n, s, 0) for s in range(4))
    ids = jnp.stack(
        [
            jnp.asarray(v, jnp.int32)
            for v in [(z_hi ^ dz) * 4 + x_of[s] for dz in (0, 1) for s in (0, 2, 1, 3)]
            + [core]
            + [(z_hi ^ k) * 4 + x_of[s] for s in range(4) for k in (0, 1)]
            + [slot_of(z_of, (z_hi ^ k) * 2 + (z_lo ^ m)) for k in (0, 1) for m in (0, 1)]
            + [z_lo, z_lo ^ 1]
            + y_of
        ]
    )
    chain = Chain()

    def run(name, body, arrays, shapes, scratch=(), flops=1000):
        return chain(name, body, ids, arrays, shapes, scratch, flops)

    codes_oth = swap(w_codes, "core")
    scale_oth = swap(w_scale, "core")
    t_oth = swap(tokens, "core")
    vc_oth = swap(value_cot, "core")
    kc_oth = swap(key_cot, "core")
    both_t = [tokens, t_oth]
    gain2 = gain.reshape(1, KV)
    factors = 1.0 / jnp.concatenate(
        [
            lax.dynamic_slice_in_dim(grad_scale, core * 4, 4, axis=1),
            lax.dynamic_slice_in_dim(grad_scale, 8 + core * 4, 4, axis=1),
        ],
        axis=1,
    )

    def stack(a, b):
        return run("stack_shards", stack_body, [a, b], [((2, SHARD, QUART), BF)])[0]

    def codes(kind, base, width, grads, g_own, g_oth):
        return run(
            "gradient_codes",
            lambda *a: codes_body(kind, base, width, grads, *a),
            both_t + [g_own, g_oth, factors],
            [((2, 4, 4, 80, width), BF)] * 2,
            [pltpu.VMEM((SHARD, width), F32)],
            flops=4 * TOK * D * width,
        )

    def add2(keep, first):
        return run("add_two", add2_body, [keep, first], [(keep.shape[1:], BF)])[0]

    def add3(keep, first, second):
        shape = (2,) + keep.shape[2:]
        return run("add_three", add3_body, [keep, first, second], [(shape, BF)] * 2)

    def plus(a, b):
        return run("add_gain", plus_body, [a, b], [(a.shape, F32)])[0]

    ka, kb, va, vb = run(
        "dequantize", dequant_body, [w_codes, codes_oth, w_scale, scale_oth], [((SHARD, QUART), BF)] * 4
    )
    k_g = swap(ka, "zb")
    k_x = swap(kb, "x", 0)
    k_s2 = stack(kb, k_x)
    k_q2 = swap(k_s2, "x", 1)
    k_za = swap(k_s2, "zb")
    k_s1 = stack(ka, k_g)
    k_r1 = swap(k_s1, "x", 0)
    k_q1 = swap(k_s1, "x", 1)

    v_cols = lambda ids, ref: cot_columns(ref, ids[CORE])
    v_keep, v_send = codes("y", 4, HALF, v_cols, value_cot, vc_oth)
    v_first = swap(v_send, "y", 0)

    k_zc = swap(k_q2, "zb")
    k_p1 = swap(k_r1, "x", 1)
    k_early, k_late = [k_s1, k_r1, k_s2, k_q2], [k_q1, k_p1, k_za, k_zc]
    raw = run("key_projection_early", early_body, both_t + k_early, [((2 * TOK, HALF), F32)], flops=2 * TOK * D * HALF)[0]
    v_g = swap(va, "zb")
    v_x = swap(vb, "x", 0)
    raw, stats = run(
        "key_projection_late",
        late_body,
        both_t + k_late + [raw, key_cot, kc_oth, gain2],
        [((2 * TOK, HALF), F32), ((2 * TOK, GROUP), F32)],
        flops=2 * TOK * D * HALF,
    )
    stats_oth = swap(stats, "core")
    v_s2 = stack(vb, v_x)
    v_q2 = swap(v_s2, "x", 1)
    v_za = swap(v_s2, "zb")
    v_s1 = stack(va, v_g)
    k_own, k_oth, g_own, g_oth, gsum = run(
        "key_norm",
        norm_body,
        [raw, stats, stats_oth, key_cot, kc_oth, gain2],
        [((TOK, HALF), BF)] * 4 + [((8, HALF), F32)],
    )
    a_keep, a_send = codes("y", 0, QUART, lambda ids, ref: ref[:, :QUART], g_own, g_oth)
    a_first = swap(a_send, "y", 0)
    b_keep, b_send = codes("x", 2, QUART, lambda ids, ref: ref[:, QUART:], g_own, g_oth)
    b_first = swap(b_send, "x", 0)
    v_r1 = swap(v_s1, "x", 0)
    v_q1 = swap(v_s1, "x", 1)

    v_second = swap(add2(v_keep, v_first), "y", 1)
    gsum = plus(gsum, swap(gsum, "y", 0))
    v_zc = swap(v_q2, "zb")
    v_p1 = swap(v_r1, "x", 1)
    gsum = plus(gsum, swap(gsum, "y", 1))
    a_second = swap(add2(a_keep, a_first), "y", 1)
    b_second = swap(add2(b_keep, b_first), "x", 1)
    v_keep, v_send = add3(v_keep, v_first, v_second)
    v_first = swap(v_send, "x", 0)

    v_early, v_late = [v_s1, v_r1, v_s2, v_q2], [v_q1, v_p1, v_za, v_zc]
    v_own, v_oth = run(
        "value_projection",
        value_body,
        both_t + v_early + v_late,
        [((TOK, HALF), BF)] * 2,
        [pltpu.VMEM((2 * TOK, HALF), F32)],
        flops=4 * TOK * D * HALF,
    )
    a_keep, a_send = add3(a_keep, a_first, a_second)
    a_first = swap(a_send, "x", 0)
    b_keep, b_send = add3(b_keep, b_first, b_second)
    b_first = swap(b_send, "y", 0)
    v_second = swap(add2(v_keep, v_first), "x", 1)
    gsum = plus(gsum, swap(gsum, "x", 0))
    weights = k_early + k_late + v_early + v_late
    sent = run("token_gradient", back_body, [g_oth, vc_oth] + weights, [((TOK, D), BF)], flops=2 * TOK * D * KV)[0]
    received = swap(sent, "core")
    a_second = swap(add2(a_keep, a_first), "x", 1)
    b_second = swap(add2(b_keep, b_first), "y", 1)
    gsum = plus(gsum, swap(gsum, "x", 1))
    z_keep, z_send = run(
        "merge_sums",
        merge_body,
        [a_keep, a_first, a_second, b_keep, b_first, b_second, v_keep, v_first, v_second],
        [((2, 80, KV), BF)] * 2,
    )
    z_first = swap(z_send, "z", 0)
    gsum = plus(gsum, swap(gsum, "z", 0))
    grad_tokens, _ = run(
        "token_gradient_sum",
        back_body,
        [g_own, value_cot] + weights + [received],
        [((TOK, D), BF), ((8, GROUP), F32)],
        flops=2 * TOK * D * KV,
    )
    z_second = swap(add2(z_keep, z_first), "z", 1)
    gsum = plus(gsum, swap(gsum, "z", 1))
    gsum_oth = swap(gsum, "core")
    mine, theirs = run(
        "last_sum",
        last_body,
        [z_keep, z_first, z_second],
        [((40, KV), F32)] * 2,
        [pltpu.VMEM((80, KV), F32)],
    )
    grad_codes = run("place_codes", place_body, [mine, swap(theirs, "core")], [((40, 2 * KV), F32)])[0]

    def both(mine, theirs, axis):
        return jnp.where(
            core == 0,
            jnp.concatenate([mine, theirs], axis=axis),
            jnp.concatenate([theirs, mine], axis=axis),
        )

    keys = both(k_own, swap(k_oth, "core"), 1)
    values = both(v_own, swap(v_oth, "core"), 1)
    grad_gain = both(gsum[0], gsum_oth[0], 0)
    return (keys, values, grad_tokens, grad_codes, grad_gain)


def solution(mesh):
    rows = P(("node", "group"), None)
    in_specs = (rows, P("node", None), P("node", None), P(), rows, rows, P())
    out_specs = (rows, rows, rows, rows, P())
    return jax.shard_map(
        on_device, mesh=mesh, in_specs=in_specs, out_specs=out_specs, check_vma=False
    )
```

```python
import jax
import jax.numpy as jnp
from jax import lax
from jax.experimental import pallas as pl
from jax.experimental.pallas import tpu as pltpu
from jax.sharding import PartitionSpec as P

BF = jnp.bfloat16
F32 = jnp.float32
GROUP = 128
AXES = ("node", "group")
TOK = 384
ROWS = 320
SHARD = 640
D = 5120
KV = 1024
HALF = 512
QUART = 256
VMEM_LIMIT = 20 * 2**20
NT = (((1,), (1,)), ((), ()))
TN = (((0,), (0,)), ((), ()))


def coords(i):
    y, z_lo, core, x, z_hi = i % 4, (i // 4) % 2, (i // 8) % 2, (i // 16) % 4, i // 64
    return z_hi * 2 + z_lo, x, core, y


def flat(z, x, core, y):
    return (((z // 2 * 4 + x) * 2 + core) * 2 + z % 2) * 4 + y


def near(n, which):
    return n ^ 1 if which == 0 else 3 - n


def pairs_of(axis, step):
    out = []
    for i in range(128):
        z, x, core, y = coords(i)
        which = step ^ core
        if axis == "core":
            out.append((i, flat(z, x, 1 - core, y)))
        if axis == "x":
            out.append((i, flat(z, near(x, which), core, y)))
        if axis == "y":
            out.append((i, flat(z, x, core, near(y, which))))
        if axis == "z":
            out.append((i, flat(near(z, which), x, core, y)))
        if axis == "zb":
            out.append((i, flat(3 - z, x, core, y)))
        if axis == "x_far":
            out.append((i, flat(z, (x + 2) % 4, core, y)))
        if axis == "y_far":
            out.append((i, flat(z, x, core, (y + 2) % 4)))
        if axis == "z_far":
            out.append((i, flat((z + 2) % 4, x, core, y)))
    return out


def swap(v, axis, step=0):
    return lax.ppermute(v, AXES, pairs_of(axis, step))


def dot(a, b, dims=(((1,), (0,)), ((), ()))):
    return lax.dot_general(a, b, dims, preferred_element_type=F32)


def f32(v):
    return v.astype(F32)


def columns(n):
    return pl.ds(pl.multiple_of(n * SHARD, GROUP), SHARD)


class Chain:
    def __init__(self):
        self.last = None

    def __call__(self, name, body, ids, arrays, shapes, scratch, flops, after):
        vm = pl.BlockSpec(memory_space=pltpu.VMEM)
        n_in = len(arrays)
        extra = ([] if self.last is None else [self.last]) + list(after)

        def kernel(*refs):
            body(refs[0], refs[1 : 1 + n_in], refs[1 + n_in + len(extra) :])

        out = pl.pallas_call(
            kernel,
            in_specs=[pl.BlockSpec(memory_space=pltpu.SMEM)]
            + [vm] * n_in
            + [pl.BlockSpec(memory_space=pl.ANY)] * len(extra),
            out_specs=[vm] * len(shapes),
            out_shape=[jax.ShapeDtypeStruct(s, t) for s, t in shapes],
            scratch_shapes=list(scratch),
            compiler_params=pltpu.CompilerParams(vmem_limit_bytes=VMEM_LIMIT),
            cost_estimate=pl.CostEstimate(flops=flops, bytes_accessed=1000, transcendentals=0),
            name=name,
        )(ids, *arrays, *extra)
        self.last = out[-1]
        return out


CORE = 8


def dequant_body(ids, ins, outs):
    own, oth, s_own, s_oth = ins
    for c in (0, 1):

        @pl.when(ids[CORE] == c)
        def _():
            for r in (0, 1):
                codes = own if r == c else oth
                scale = s_own if r == c else s_oth
                for n, out in enumerate(outs):
                    for j in (0, 1):
                        b = (n // 2) * 8 + c * 4 + (n % 2) * 2 + j
                        out[r * ROWS : (r + 1) * ROWS, j * GROUP : (j + 1) * GROUP] = (
                            f32(codes[:, b * GROUP : (b + 1) * GROUP]) * f32(scale[:, b : b + 1])
                        ).astype(BF)


def stack_body(ids, ins, outs):
    outs[0][0] = ins[0][...]
    outs[0][1] = ins[1][...]


def join_body(ids, ins, outs):
    outs[0][0:2] = ins[0][...]
    outs[0][2:4] = ins[1][...]


def half_body(ids, ins, outs):
    outs[0][...] = cot_columns(ins[0], 1 - ids[CORE])
    outs[1][...] = cot_columns(ins[1], 1 - ids[CORE])


def add_products(ids, tokens, out, pieces, first):
    fresh = [first, first]
    for ref, n, shard, half in pieces:
        cols = slice(half * QUART, (half + 1) * QUART)
        for t, tok in enumerate(tokens):
            here = slice(t * TOK, (t + 1) * TOK)
            value = dot(tok[:, columns(ids[shard])], ref[n])
            if fresh[half]:
                out[here, cols] = value
            else:
                out[here, cols] += value
        fresh[half] = False


def early_pieces(s1, r1, s2, q2):
    return [(s1, 0, 0, 0), (s1, 1, 4, 0), (r1, 0, 1, 0), (r1, 1, 5, 0)] + [
        (s2, 0, 0, 1), (s2, 1, 1, 1), (q2, 0, 2, 1), (q2, 1, 3, 1)
    ]


def late_pieces(q1, p1, za, zc):
    return [(q1, 0, 2, 0), (q1, 1, 6, 0), (p1, 0, 3, 0), (p1, 1, 7, 0)] + [
        (za, 0, 4, 1), (za, 1, 5, 1), (zc, 0, 6, 1), (zc, 1, 7, 1)
    ]


def early_body(ids, ins, outs):
    add_products(ids, ins[:2], outs[0], early_pieces(*ins[2:6]), True)


def cot_columns(ref, core):
    return ref[:, pl.ds(pl.multiple_of(core * HALF, GROUP), HALF)]


def late_body(ids, ins, outs):
    raw, cot_own, cot_oth, gain = ins[6:10]
    out, stats = outs
    out[...] = raw[...]
    add_products(ids, ins[:2], out, late_pieces(*ins[2:6]), False)
    lane = lax.broadcasted_iota(jnp.int32, (TOK, GROUP), 1)
    weight = cot_columns(gain, ids[CORE])
    for n, cot in enumerate((cot_columns(cot_own, ids[CORE]), cot_oth[...])):
        part = out[n * TOK : (n + 1) * TOK, :]
        square = jnp.sum(part * part, axis=1, keepdims=True)
        cross = jnp.sum(part * (f32(cot) * weight), axis=1, keepdims=True)
        stats[n * TOK : (n + 1) * TOK, :] = jnp.where(
            lane == 0, square, jnp.where(lane == 1, cross, 0.0)
        )


def norm_body(ids, ins, outs):
    raw, mine, theirs, cot_own, cot_oth, gain = ins
    gsum = outs[4]
    weight = cot_columns(gain, ids[CORE])
    total = jnp.zeros((8, HALF), F32)
    for n, cot in enumerate((cot_columns(cot_own, ids[CORE]), cot_oth[...])):
        here = slice(n * TOK, (n + 1) * TOK)
        there = slice((1 - n) * TOK, (2 - n) * TOK)
        square = mine[here, 0:1] + theirs[there, 0:1]
        cross = mine[here, 1:2] + theirs[there, 1:2]
        inverse = lax.rsqrt(square * (1.0 / KV) + 1e-06)
        normed = raw[here, :] * inverse
        cotangent = f32(cot)
        outs[n][...] = (normed * weight).astype(BF)
        mean = cross * inverse * (1.0 / KV)
        outs[2 + n][...] = (inverse * (cotangent * weight - normed * mean)).astype(BF)
        total += jnp.sum((cotangent * normed).reshape(TOK // 8, 8, HALF), axis=0)
    gsum[...] = jnp.broadcast_to(jnp.sum(total, axis=0, keepdims=True), (8, HALF))


def value_body(numbers, ids, ins, outs):
    acc = outs[2]
    pieces = [(ins[2 + r], n, shard, half) for r, n, shard, half in numbers]
    add_products(ids, ins[:2], acc, pieces, True)
    outs[0][...] = acc[:TOK, :].astype(BF)
    outs[1][...] = acc[TOK:, :].astype(BF)


def back_body(numbers, ids, ins, outs):
    g_key, g_val = ins[:2]
    own = len(ins) > 16
    grad = jnp.concatenate([g_key[...], cot_columns(g_val, ids[CORE]) if own else g_val[...]], axis=1)
    where = {}
    for ref, n, shard, half in early_pieces(*ins[2:6]) + late_pieces(*ins[6:10]):
        where[shard, half] = (ref, n)
    for r, n, shard, half in numbers:
        where[shard, 2 + half] = (ins[10 + r], n)
    for shard in range(8):
        weight = jnp.concatenate([where[shard, q][0][where[shard, q][1]] for q in range(4)], axis=1)
        value = dot(grad, weight, NT)
        if own:
            value += f32(ins[16][:, columns(ids[shard])])
        outs[0][:, columns(ids[shard])] = value.astype(BF)
    if own:
        outs[1][...] = jnp.zeros_like(outs[1])


def piece(prod, offset, extra):
    low = prod[pl.ds(pl.multiple_of(offset, 8), 40), :]
    high = prod[pl.ds(pl.multiple_of(offset + ROWS, 8), 40), :]
    return jnp.concatenate([low, high] + extra, axis=0).astype(BF)


def two_rows(total):
    row = lax.broadcasted_iota(jnp.int32, (16, total.shape[1]), 0)
    high = f32(total.astype(BF))
    return jnp.where(row == 0, high, jnp.where(row == 1, total - high, 0.0))


def with_gain(total):
    return jnp.concatenate(
        [total[:80], two_rows(jnp.sum(total[80:], axis=0, keepdims=True))], axis=0
    ).astype(BF)


def codes_body(kind, base, width, grads, ids, ins, outs):
    t_own, t_oth, g_own, g_oth, scale = ins[:5]
    keep, send, prod = outs
    g_own, g_oth = grads(ids, g_own, g_oth)
    extra = [two_rows(ins[5][0:1, base * GROUP : base * GROUP + width])] if len(ins) > 5 else []

    def block_codes(near_half, pair, k):
        sx = pair + (0 if near_half else 2)
        block = ids[9 + sx * 2 + k]
        total = dot(t_own[:, columns(block)], g_own, TN) + dot(t_oth[:, columns(block)], g_oth, TN)
        rows = pl.ds(pl.multiple_of(block * SHARD, SHARD), SHARD)
        factor = scale[rows, base : base + width // GROUP]
        for j in range(width // GROUP):
            cols = slice(j * GROUP, (j + 1) * GROUP)
            prod[:, cols] = total[:, cols] * factor[:, j : j + 1]
        for m in (0, 1):
            z_slot = ids[17 + k * 2 + m]
            for s in range(4):
                value = piece(prod, ids[21 + m] * 160 + ids[23 + s] * 40, extra)
                if kind == "y":
                    (keep if s < 2 else send)[s % 2, sx, z_slot] = value
                else:
                    (keep if near_half else send)[pair, s, z_slot] = value

    for near_half in (False, True):

        @pl.loop(0, 2)
        def _(pair):
            block_codes(near_half, pair, 0)
            block_codes(near_half, pair, 1)


def summed(parts, at, gains):
    total = f32(parts[0][at])
    for part in parts[1:]:
        total += f32(part[at])
    return with_gain(total) if gains else total.astype(BF)


def add2_body(gains, ids, ins, outs):
    keep, first = ins[0].at[1], ins[1].at[1]
    for i in range(4):
        for j in range(4):
            outs[0][i, j] = summed([keep, first], (i, j), gains)


def add3_body(gains, ids, ins, outs):
    keep, first, second = ins[0].at[0], ins[1].at[0], ins[2]
    for i in range(4):
        for j in range(4):
            outs[i][j] = summed([keep, first, second], (i, j), gains)


def add3_both_body(ids, ins, outs):
    for n, (at, rows, width) in enumerate(((0, 96, QUART), (QUART, 80, HALF))):
        keep, first, second = ins[3 * n].at[0], ins[3 * n + 1].at[0], ins[3 * n + 2]
        for i in range(4):
            for j in range(4):
                value = summed([keep, first, second], (i, j), rows > 80)
                outs[i][j, :rows, at : at + width] = value
    for i in range(4):
        for j in range(4):
            outs[i][j, 80:, QUART:] = jnp.zeros((16, HALF), BF)


def merge_body(ids, ins, outs):
    for s in range(4):
        outs[s][:, :QUART] = summed([p.at[:, :, :QUART] for p in ins[:4]], s, True)
        outs[s][:, QUART:HALF] = summed(ins[4:], s, True)
        outs[s][:, HALF:] = summed([p.at[:, :, QUART:] for p in ins[:4]], s, False)


def last_body(ids, ins, outs):
    mine, theirs, total = outs
    total[...] = f32(ins[0][...]) + f32(ins[1][...]) + f32(ins[2][...]) + f32(ins[3][...])
    gain = jnp.broadcast_to(jnp.sum(total[80:, :], axis=0, keepdims=True), (8, KV))
    for out, core in ((mine, ids[CORE]), (theirs, 1 - ids[CORE])):
        out[:40, :] = total[pl.ds(pl.multiple_of(core * 40, 8), 40), :]
        out[40:, :] = gain


def halves_body(ids, ins, outs):
    for c in (0, 1):

        @pl.when(ids[CORE] == c)
        def _():
            outs[0][:, c * HALF : (c + 1) * HALF] = ins[0][...]
            outs[0][:, (1 - c) * HALF : (2 - c) * HALF] = ins[1][...]


def place_body(ids, ins, outs):
    mine, theirs = ins
    for c in (0, 1):

        @pl.when(ids[CORE] == c)
        def _():
            for n in range(4):
                source = mine if n % 2 == c else theirs
                outs[0][:, n * HALF : (n + 1) * HALF] = source[:40, n // 2 * HALF : (n // 2 + 1) * HALF]
            for n in range(2):
                source = mine if n == c else theirs
                outs[1][:, n * HALF : (n + 1) * HALF] = source[40:, :HALF]


def on_device(tokens, w_codes, w_scale, gain, key_cot, value_cot, grad_scale):
    node, group = lax.axis_index("node"), lax.axis_index("group")
    z_hi, x, core = node // 8, (node // 2) % 4, node % 2
    z_lo, y = group // 4, group % 4
    z = z_hi * 2 + z_lo

    def ring(n):
        a, b = n ^ 1, 3 - n
        first, second = jnp.where(core == 0, a, b), jnp.where(core == 0, b, a)
        return [n, second, first, (n + 2) % 4]

    x_of, y_of, z_of = ring(x), ring(y), ring(z)
    slot_of = lambda places, n: sum(jnp.where(places[s] == n, s, 0) for s in range(4))
    ids = jnp.stack(
        [
            jnp.asarray(v, jnp.int32)
            for v in [(z_hi ^ dz) * 4 + x_of[s] for dz in (0, 1) for s in (0, 2, 1, 3)]
            + [core]
            + [(z_hi ^ k) * 4 + x_of[s] for s in range(4) for k in (0, 1)]
            + [slot_of(z_of, (z_hi ^ k) * 2 + (z_lo ^ m)) for k in (0, 1) for m in (0, 1)]
            + [z_lo, z_lo ^ 1]
            + y_of
        ]
    )
    chain = Chain()

    def run(name, body, arrays, shapes, scratch=(), flops=1000, after=()):
        return chain(name, body, ids, arrays, shapes, scratch, flops, after)

    def codes(kind, base, width, rows, grads, arrays, after=()):
        return run(
            "gradient_codes",
            lambda *a: codes_body(kind, base, width, grads, *a),
            both_t + arrays,
            [((2, 4, 4, rows, width), BF)] * 2,
            [pltpu.VMEM((SHARD, width), F32)],
            flops=4 * TOK * D * width,
            after=after,
        )

    def add2(keep, first, after=()):
        gains = keep.shape[-2] > 80
        body = lambda *a: add2_body(gains, *a)
        return run("add_two", body, [keep, first], [(keep.shape[1:], BF)], after=after)[0]

    def add3(keep, first, second):
        gains = keep.shape[-2] > 80
        body = lambda *a: add3_body(gains, *a)
        return run("add_three", body, [keep, first, second], [(keep.shape[2:], BF)] * 4)

    def direct(axis, slots):
        return [
            slots[0],
            swap(slots[1], axis, 1),
            swap(slots[2], axis, 0),
            swap(slots[3], axis + "_far"),
        ]

    codes_oth = swap(w_codes, "core")
    scale_oth = swap(w_scale, "core")
    t_oth = swap(tokens, "core")
    both_t = [tokens, t_oth]
    gain2 = gain.reshape(1, KV)
    factors = 1.0 / jnp.concatenate(
        [
            lax.dynamic_slice_in_dim(grad_scale, core * 4, 4, axis=1),
            lax.dynamic_slice_in_dim(grad_scale, 8 + core * 4, 4, axis=1),
        ],
        axis=1,
    )
    vc_send, kc_send = run("halves", half_body, [value_cot, key_cot], [((TOK, HALF), BF)] * 2)
    vc_oth, kc_oth = swap(vc_send, "core"), swap(kc_send, "core")

    def stack(a, b, after=()):
        return run("stack_shards", stack_body, [a, b], [((2, SHARD, QUART), BF)], after=after)[0]

    ka, kb, va, vb = run(
        "dequantize", dequant_body, [w_codes, codes_oth, w_scale, scale_oth], [((SHARD, QUART), BF)] * 4
    )
    k_g = swap(ka, "zb")
    k_x = swap(kb, "x", 0)
    v_cols = lambda ids, own, oth: (cot_columns(own, ids[CORE]), oth[...])
    v_keep, v_send = codes("y", 4, HALF, 80, v_cols, [value_cot, vc_oth, factors], [kc_oth])
    v_first = swap(v_send, "y", 0)
    k_s2 = stack(kb, k_x)
    k_q2 = swap(k_s2, "x", 1)
    k_za = swap(k_s2, "zb")
    k_s1 = stack(ka, k_g)
    k_r1 = swap(k_s1, "x", 0)
    k_q1 = swap(k_s1, "x", 1)

    k_zc = swap(k_q2, "zb")
    k_p1 = swap(k_r1, "x", 1)
    k_early, k_late = [k_s1, k_r1, k_s2, k_q2], [k_q1, k_p1, k_za, k_zc]
    raw = run(
        "key_projection_early",
        early_body,
        both_t + k_early,
        [((2 * TOK, HALF), F32)],
    )[0]
    v_x = swap(vb, "x", 0)
    v_s2 = stack(vb, v_x, [k_za, k_q1])
    v_q2 = swap(v_s2, "x", 1)
    raw, stats = run(
        "key_projection_late",
        late_body,
        both_t + k_late + [raw, key_cot, kc_oth, gain2],
        [((2 * TOK, HALF), F32), ((2 * TOK, GROUP), F32)],
    )
    stats_oth = swap(stats, "core")
    v_g = swap(va, "zb")
    v_za = swap(v_s2, "zb")
    k_own, k_oth, g_own, g_oth, gsum = run(
        "key_norm",
        norm_body,
        [raw, stats, stats_oth, key_cot, kc_oth, gain2],
        [((TOK, HALF), BF)] * 4 + [((8, HALF), F32)],
    )
    a_cols = lambda ids, own, oth: (own[:, :QUART], oth[:, :QUART])
    a_keep, a_send = codes("y", 0, QUART, 96, a_cols, [g_own, g_oth, factors, gsum])
    a_first = swap(a_send, "y", 0)
    v_s1 = stack(va, v_g, [v_q2])
    v_r1 = swap(v_s1, "x", 0)
    v_zc = swap(v_q2, "zb")
    b_cols = lambda ids, own, oth: (own[:, QUART:], oth[:, QUART:])
    b_keep, b_send = codes("x", 2, QUART, 96, b_cols, [g_own, g_oth, factors, gsum])
    b_first = swap(b_send, "x", 0)
    v_second = swap(add2(v_keep, v_first), "y", 1)
    v_c1 = run("join_shards", join_body, [v_s1, v_r1], [((4, SHARD, QUART), BF)])[0]
    v_r2 = swap(v_c1, "x", 1)

    a_second = swap(add2(a_keep, a_first, [v_za, v_zc]), "y", 1)
    b_second = swap(add2(b_keep, b_first, [v_r2]), "x", 1)
    v_pieces = [(v_c1, n, s, 0) for n, s in enumerate((0, 4, 1, 5))]
    v_pieces += [(v_r2, n, s, 0) for n, s in enumerate((2, 6, 3, 7))]
    v_pieces += [(r, n, s, 1) for r, n, s in ((v_s2, 0, 0), (v_s2, 1, 1), (v_q2, 0, 2), (v_q2, 1, 3))]
    v_pieces += [(r, n, s, 1) for r, n, s in ((v_za, 0, 4), (v_za, 1, 5), (v_zc, 0, 6), (v_zc, 1, 7))]
    v_weights = [v_c1, v_r2, v_s2, v_q2, v_za, v_zc]
    numbers = [(next(i for i, w in enumerate(v_weights) if w is r), n, s, h) for r, n, s, h in v_pieces]
    join = lambda own, oth: run("join_halves", halves_body, [own, oth], [((TOK, KV), BF)])[0]
    keys = join(k_own, swap(k_oth, "core"))
    weights = k_early + k_late + v_weights
    sent = run(
        "token_gradient",
        lambda *a: back_body(numbers, *a),
        [g_oth, vc_oth] + weights,
        [((TOK, D), BF)],
        flops=8 * TOK * D * KV,
    )[0]
    received = swap(sent, "core")
    av_slots = run(
        "add_three",
        add3_both_body,
        [a_keep, a_first, a_second, v_keep, v_first, v_second],
        [((4, 96, QUART + HALF), BF)] * 4,
    )
    av_parts = direct("x", av_slots)
    b_parts = direct("y", add3(b_keep, b_first, b_second))
    grad_tokens, _ = run(
        "token_gradient_sum",
        lambda *a: back_body(numbers, *a),
        [g_own, value_cot] + weights + [received],
        [((TOK, D), BF), ((8, GROUP), F32)],
        flops=8 * TOK * D * KV,
    )
    z_slots = run("merge_sums", merge_body, av_parts + b_parts, [((96, KV), BF)] * 4)
    z_parts = direct("z", z_slots)
    v_own, v_oth = run(
        "value_projection",
        lambda *a: value_body(numbers, *a),
        both_t + v_weights,
        [((TOK, HALF), BF)] * 2,
        [pltpu.VMEM((2 * TOK, HALF), F32)],
        flops=4 * TOK * D * HALF,
    )
    mine, theirs = run(
        "last_sum", last_body, z_parts, [((48, KV), F32)] * 2, [pltpu.VMEM((96, KV), F32)]
    )
    theirs = swap(theirs, "core")
    values = join(v_own, swap(v_oth, "core"))
    grad_codes, grad_gain = run(
        "place_codes", place_body, [mine, theirs], [((40, 2 * KV), F32), ((8, KV), F32)]
    )

    return (keys, values, grad_tokens, grad_codes, grad_gain[0])


def solution(mesh):
    rows = P(("node", "group"), None)
    in_specs = (rows, P("node", None), P("node", None), P(), rows, rows, P())
    out_specs = (rows, rows, rows, rows, P())
    return jax.shard_map(
        on_device, mesh=mesh, in_specs=in_specs, out_specs=out_specs, check_vma=False
    )
```

```python
import jax
import jax.numpy as jnp
from jax import lax
from jax.experimental import pallas as pl
from jax.experimental.pallas import tpu as pltpu
from jax.sharding import PartitionSpec as P

BF = jnp.bfloat16
F32 = jnp.float32
GROUP = 128
AXES = ("node", "group")
TOK = 384
ROWS = 320
SHARD = 640
D = 5120
KV = 1024
HALF = 512
QUART = 256
VMEM_LIMIT = 20 * 2**20
COVER = 10**11
NT = (((1,), (1,)), ((), ()))
TN = (((0,), (0,)), ((), ()))


def coords(i):
    y, z_lo, core, x, z_hi = i % 4, (i // 4) % 2, (i // 8) % 2, (i // 16) % 4, i // 64
    return z_hi * 2 + z_lo, x, core, y


def flat(z, x, core, y):
    return (((z // 2 * 4 + x) * 2 + core) * 2 + z % 2) * 4 + y


def near(n, which):
    return n ^ 1 if which == 0 else 3 - n


def pairs_of(axis, step):
    out = []
    for i in range(128):
        z, x, core, y = coords(i)
        which = step ^ core
        if axis == "core":
            out.append((i, flat(z, x, 1 - core, y)))
        if axis == "x":
            out.append((i, flat(z, near(x, which), core, y)))
        if axis == "y":
            out.append((i, flat(z, x, core, near(y, which))))
        if axis == "z":
            out.append((i, flat(near(z, which), x, core, y)))
        if axis == "zb":
            out.append((i, flat(3 - z, x, core, y)))
        if axis == "x_far":
            out.append((i, flat(z, (x + 2) % 4, core, y)))
        if axis == "y_far":
            out.append((i, flat(z, x, core, (y + 2) % 4)))
        if axis == "z_far":
            out.append((i, flat((z + 2) % 4, x, core, y)))
    return out


def swap(v, axis, step=0):
    return lax.ppermute(v, AXES, pairs_of(axis, step))


def dot(a, b, dims=(((1,), (0,)), ((), ()))):
    return lax.dot_general(a, b, dims, preferred_element_type=F32)


def f32(v):
    return v.astype(F32)


def columns(n):
    return pl.ds(pl.multiple_of(n * SHARD, GROUP), SHARD)


class Chain:
    def __init__(self):
        self.last = None

    def __call__(self, name, body, ids, arrays, shapes, scratch, flops, after):
        vm = pl.BlockSpec(memory_space=pltpu.VMEM)
        n_in = len(arrays)
        extra = ([] if self.last is None else [self.last]) + list(after)

        def kernel(*refs):
            body(refs[0], refs[1 : 1 + n_in], refs[1 + n_in + len(extra) :])

        out = pl.pallas_call(
            kernel,
            in_specs=[pl.BlockSpec(memory_space=pltpu.SMEM)]
            + [vm] * n_in
            + [pl.BlockSpec(memory_space=pl.ANY)] * len(extra),
            out_specs=[vm] * len(shapes),
            out_shape=[jax.ShapeDtypeStruct(s, t) for s, t in shapes],
            scratch_shapes=list(scratch),
            compiler_params=pltpu.CompilerParams(vmem_limit_bytes=VMEM_LIMIT),
            cost_estimate=pl.CostEstimate(flops=flops, bytes_accessed=1000, transcendentals=0),
            name=name,
        )(ids, *arrays, *extra)
        self.last = out[-1]
        return out


CORE = 8


def dequant_body(first, ids, ins, outs):
    own, oth, s_own, s_oth = ins
    for c in (0, 1):

        @pl.when(ids[CORE] == c)
        def _():
            for r in (0, 1):
                codes = own if r == c else oth
                scale = s_own if r == c else s_oth
                for j in range(4):
                    b = first + c * 4 + j
                    outs[0][r * ROWS : (r + 1) * ROWS, j * GROUP : (j + 1) * GROUP] = (
                        f32(codes[:, b * GROUP : (b + 1) * GROUP]) * f32(scale[:, b : b + 1])
                    ).astype(BF)


def half_body(ids, ins, outs):
    outs[0][...] = cot_columns(ins[0], 1 - ids[CORE])
    outs[1][...] = cot_columns(ins[1], 1 - ids[CORE])


def cot_columns(ref, core):
    return ref[:, pl.ds(pl.multiple_of(core * HALF, GROUP), HALF)]


def key_body(ids, ins, outs):
    t_own, t_oth, weight, cot_own, cot_oth, gain = ins
    out, stats = outs
    lane = lax.broadcasted_iota(jnp.int32, (TOK, GROUP), 1)
    gains = cot_columns(gain, ids[CORE])
    for n, (tok, cot) in enumerate(((t_own, cot_columns(cot_own, ids[CORE])), (t_oth, cot_oth[...]))):
        here = slice(n * TOK, (n + 1) * TOK)
        out[here, :] = dot(tok[...], weight[...])
        part = out[here, :]
        square = jnp.sum(part * part, axis=1, keepdims=True)
        cross = jnp.sum(part * (f32(cot) * gains), axis=1, keepdims=True)
        stats[here, :] = jnp.where(lane == 0, square, jnp.where(lane == 1, cross, 0.0))


def norm_body(ids, ins, outs):
    raw, mine, theirs, cot_own, cot_oth, gain = ins
    gsum = outs[4]
    weight = cot_columns(gain, ids[CORE])
    total = jnp.zeros((8, HALF), F32)
    for n, cot in enumerate((cot_columns(cot_own, ids[CORE]), cot_oth[...])):
        here = slice(n * TOK, (n + 1) * TOK)
        there = slice((1 - n) * TOK, (2 - n) * TOK)
        square = mine[here, 0:1] + theirs[there, 0:1]
        cross = mine[here, 1:2] + theirs[there, 1:2]
        inverse = lax.rsqrt(square * (1.0 / KV) + 1e-06)
        normed = raw[here, :] * inverse
        cotangent = f32(cot)
        outs[n][...] = (normed * weight).astype(BF)
        mean = cross * inverse * (1.0 / KV)
        outs[2 + n][...] = (inverse * (cotangent * weight - normed * mean)).astype(BF)
        total += jnp.sum((cotangent * normed).reshape(TOK // 8, 8, HALF), axis=0)
    gsum[...] = jnp.broadcast_to(jnp.sum(total, axis=0, keepdims=True), (8, HALF))


def value_body(ids, ins, outs):
    for n in (0, 1):
        outs[n][...] = dot(ins[n][...], ins[2][...]).astype(BF)


def back_body(ids, ins, outs):
    g_key, g_val, w_key, w_val = ins[:4]
    own = len(ins) > 4
    grad = jnp.concatenate([g_key[...], cot_columns(g_val, ids[CORE]) if own else g_val[...]], axis=1)
    for n in range(D // SHARD):
        rows = slice(n * SHARD, (n + 1) * SHARD)
        value = dot(grad, jnp.concatenate([w_key[rows, :], w_val[rows, :]], axis=1), NT)
        if own:
            value += f32(ins[4][:, rows])
        outs[0][:, rows] = value.astype(BF)
    if own:
        outs[1][...] = jnp.zeros_like(outs[1])


def piece(prod, offset, extra):
    low = prod[pl.ds(pl.multiple_of(offset, 8), 40), :]
    high = prod[pl.ds(pl.multiple_of(offset + ROWS, 8), 40), :]
    return jnp.concatenate([low, high] + extra, axis=0).astype(BF)


def two_rows(total):
    row = lax.broadcasted_iota(jnp.int32, (16, total.shape[1]), 0)
    high = f32(total.astype(BF))
    return jnp.where(row == 0, high, jnp.where(row == 1, total - high, 0.0))


def with_gain(total):
    return jnp.concatenate(
        [total[:80], two_rows(jnp.sum(total[80:], axis=0, keepdims=True))], axis=0
    ).astype(BF)


def codes_body(kind, base, width, grads, ids, ins, outs):
    t_own, t_oth, g_own, g_oth, scale = ins[:5]
    keep, send, prod = outs
    g_own, g_oth = grads(ids, g_own, g_oth)
    extra = [two_rows(ins[5][0:1, base * GROUP : base * GROUP + width])] if len(ins) > 5 else []

    def block_codes(near_half, pair, k):
        sx = pair + (0 if near_half else 2)
        block = ids[9 + sx * 2 + k]
        total = dot(t_own[:, columns(block)], g_own, TN) + dot(t_oth[:, columns(block)], g_oth, TN)
        rows = pl.ds(pl.multiple_of(block * SHARD, SHARD), SHARD)
        factor = scale[rows, base : base + width // GROUP]
        for j in range(width // GROUP):
            cols = slice(j * GROUP, (j + 1) * GROUP)
            prod[:, cols] = total[:, cols] * factor[:, j : j + 1]
        for m in (0, 1):
            z_slot = ids[17 + k * 2 + m]
            for s in range(4):
                value = piece(prod, ids[21 + m] * 160 + ids[23 + s] * 40, extra)
                if kind == "y":
                    (keep if s < 2 else send)[s % 2, sx, z_slot] = value
                else:
                    (keep if near_half else send)[pair, s, z_slot] = value

    for near_half in (False, True):

        @pl.loop(0, 2)
        def _(pair):
            block_codes(near_half, pair, 0)
            block_codes(near_half, pair, 1)


def summed(parts, at, gains):
    total = f32(parts[0][at])
    for part in parts[1:]:
        total += f32(part[at])
    return with_gain(total) if gains else total.astype(BF)


def add2_body(gains, ids, ins, outs):
    keep, first = ins[0].at[1], ins[1].at[1]
    for i in range(4):
        if keep.shape[0] == 4 and len(keep.shape) == 4:
            for j in range(4):
                outs[0][i, j] = summed([keep, first], (i, j), gains)
        else:
            outs[0][i] = summed([keep, first], i, gains)


def add3_body(gains, ids, ins, outs):
    keep, first, second = ins[0].at[0], ins[1].at[0], ins[2]
    for i in range(4):
        for j in range(4):
            outs[i // 2][i % 2, j] = summed([keep, first, second], (i, j), gains)


def merge_body(ids, ins, outs):
    for n, (at, width) in enumerate(((0, QUART), (QUART, QUART), (HALF, HALF))):
        keep, first, second = ins[3 * n].at[0], ins[3 * n + 1].at[0], ins[3 * n + 2]
        rows = 80 if n == 2 else 96
        for s in range(4):
            outs[s][:rows, at : at + width] = summed([keep, first, second], s, n < 2)
            if n == 2:
                outs[s][80:, at : at + width] = jnp.zeros((16, width), BF)


def last_body(ids, ins, outs):
    mine, theirs, total = outs
    total[...] = f32(ins[0][...]) + f32(ins[1][...]) + f32(ins[2][...]) + f32(ins[3][...])
    gain = jnp.broadcast_to(jnp.sum(total[80:, :], axis=0, keepdims=True), (8, KV))
    for out, core in ((mine, ids[CORE]), (theirs, 1 - ids[CORE])):
        out[:40, :] = total[pl.ds(pl.multiple_of(core * 40, 8), 40), :]
        out[40:, :] = gain


def halves_body(ids, ins, outs):
    for c in (0, 1):

        @pl.when(ids[CORE] == c)
        def _():
            outs[0][:, c * HALF : (c + 1) * HALF] = ins[0][...]
            outs[0][:, (1 - c) * HALF : (2 - c) * HALF] = ins[1][...]


def place_body(ids, ins, outs):
    mine, theirs = ins
    for c in (0, 1):

        @pl.when(ids[CORE] == c)
        def _():
            for n in range(4):
                source = mine if n % 2 == c else theirs
                outs[0][:, n * HALF : (n + 1) * HALF] = source[:40, n // 2 * HALF : (n // 2 + 1) * HALF]
            for n in range(2):
                source = mine if n == c else theirs
                outs[1][:, n * HALF : (n + 1) * HALF] = source[40:, :HALF]


def on_device(tokens, w_codes, w_scale, gain, key_cot, value_cot, grad_scale):
    node, group = lax.axis_index("node"), lax.axis_index("group")
    z_hi, x, core = node // 8, (node // 2) % 4, node % 2
    z_lo, y = group // 4, group % 4
    z = z_hi * 2 + z_lo

    def ring(n):
        a, b = n ^ 1, 3 - n
        first, second = jnp.where(core == 0, a, b), jnp.where(core == 0, b, a)
        return [n, second, first, (n + 2) % 4]

    x_of, y_of, z_of = ring(x), ring(y), ring(z)
    slot_of = lambda places, n: sum(jnp.where(places[s] == n, s, 0) for s in range(4))
    ids = jnp.stack(
        [
            jnp.asarray(v, jnp.int32)
            for v in [(z_hi ^ dz) * 4 + x_of[s] for dz in (0, 1) for s in (0, 2, 1, 3)]
            + [core]
            + [(z_hi ^ k) * 4 + x_of[s] for s in range(4) for k in (0, 1)]
            + [slot_of(z_of, (z_hi ^ k) * 2 + (z_lo ^ m)) for k in (0, 1) for m in (0, 1)]
            + [z_lo, z_lo ^ 1]
            + y_of
        ]
    )
    chain = Chain()

    def run(name, body, arrays, shapes, scratch=(), flops=1000, after=()):
        return chain(name, body, ids, arrays, shapes, scratch, flops, after)

    def codes(kind, base, width, rows, grads, arrays, after=()):
        return run(
            "gradient_codes",
            lambda *a: codes_body(kind, base, width, grads, *a),
            both_t + arrays,
            [((2, 4, 4, rows, width), BF)] * 2,
            [pltpu.VMEM((SHARD, width), F32)],
            flops=COVER,
            after=after,
        )

    def add2(keep, first, after=()):
        gains = keep.shape[-2] > 80
        body = lambda *a: add2_body(gains, *a)
        return run("add_two", body, [keep, first], [(keep.shape[1:], BF)], after=after)[0]

    def add3(keep, first, second):
        gains = keep.shape[-2] > 80
        body = lambda *a: add3_body(gains, *a)
        shape = (2,) + keep.shape[2:]
        return run("add_three", body, [keep, first, second], [(shape, BF)] * 2)

    def direct(axis, slots):
        return [
            slots[0],
            swap(slots[1], axis, 1),
            swap(slots[2], axis, 0),
            swap(slots[3], axis + "_far"),
        ]

    codes_oth = swap(w_codes, "core")
    scale_oth = swap(w_scale, "core")
    t_oth = swap(tokens, "core")
    both_t = [tokens, t_oth]
    gain2 = gain.reshape(1, KV)
    factors = 1.0 / jnp.concatenate(
        [
            lax.dynamic_slice_in_dim(grad_scale, core * 4, 4, axis=1),
            lax.dynamic_slice_in_dim(grad_scale, 8 + core * 4, 4, axis=1),
        ],
        axis=1,
    )
    vc_send, kc_send = run("halves", half_body, [value_cot, key_cot], [((TOK, HALF), BF)] * 2)
    vc_oth, kc_oth = swap(vc_send, "core"), swap(kc_send, "core")

    def shards(first):
        local = run(
            "dequantize",
            lambda *a: dequant_body(first, *a),
            [w_codes, codes_oth, w_scale, scale_oth],
            [((SHARD, HALF), BF)],
        )[0]
        same_core = [list(range(c, 16, 2)) for c in (0, 1)]
        return lax.all_gather(local, "node", axis_index_groups=same_core, axis=0, tiled=True)

    join = lambda own, oth: run("join_halves", halves_body, [own, oth], [((TOK, KV), BF)])[0]
    w_key = shards(0)

    v_cols = lambda ids, own, oth: (cot_columns(own, ids[CORE]), oth[...])
    v_keep, v_send = codes("y", 4, HALF, 80, v_cols, [value_cot, vc_oth, factors], [kc_oth])
    v_first = swap(v_send, "y", 0)
    w_val = shards(8)
    raw, stats = run(
        "key_projection",
        key_body,
        both_t + [w_key, key_cot, kc_oth, gain2],
        [((2 * TOK, HALF), F32), ((2 * TOK, GROUP), F32)],
        flops=COVER,
    )
    stats_oth = swap(stats, "core")
    v_second = swap(add2(v_keep, v_first), "y", 1)
    k_own, k_oth, g_own, g_oth, gsum = run(
        "key_norm",
        norm_body,
        [raw, stats, stats_oth, key_cot, kc_oth, gain2],
        [((TOK, HALF), BF)] * 4 + [((8, HALF), F32)],
    )
    a_cols = lambda ids, own, oth: (own[:, :QUART], oth[:, :QUART])
    a_keep, a_send = codes("y", 0, QUART, 96, a_cols, [g_own, g_oth, factors, gsum])
    a_first = swap(a_send, "y", 0)
    b_cols = lambda ids, own, oth: (own[:, QUART:], oth[:, QUART:])
    b_keep, b_send = codes("x", 2, QUART, 96, b_cols, [g_own, g_oth, factors, gsum])
    b_first = swap(b_send, "x", 0)
    v_keep, v_send = add3(v_keep, v_first, v_second)
    v_first = swap(v_send, "x", 0)
    keys = join(k_own, swap(k_oth, "core"))

    a_second = swap(add2(a_keep, a_first), "y", 1)
    b_second = swap(add2(b_keep, b_first), "x", 1)
    v_second = swap(add2(v_keep, v_first), "x", 1)
    sent = run(
        "token_gradient", back_body, [g_oth, vc_oth, w_key, w_val], [((TOK, D), BF)], flops=COVER
    )[0]
    received = swap(sent, "core")
    a_keep, a_send = add3(a_keep, a_first, a_second)
    a_first = swap(a_send, "x", 0)
    b_keep, b_send = add3(b_keep, b_first, b_second)
    b_first = swap(b_send, "y", 0)
    v_own, v_oth = run(
        "value_projection",
        value_body,
        both_t + [w_val],
        [((TOK, HALF), BF)] * 2,
        flops=COVER,
    )
    a_second = swap(add2(a_keep, a_first), "x", 1)
    b_second = swap(add2(b_keep, b_first), "y", 1)
    grad_tokens, _ = run(
        "token_gradient_sum",
        back_body,
        [g_own, value_cot, w_key, w_val, received],
        [((TOK, D), BF), ((8, GROUP), F32)],
        flops=COVER,
    )
    z_slots = run(
        "merge_sums",
        merge_body,
        [a_keep, a_first, a_second, b_keep, b_first, b_second, v_keep, v_first, v_second],
        [((96, KV), BF)] * 4,
    )
    z_parts = direct("z", z_slots)
    values = join(v_own, swap(v_oth, "core"))
    mine, theirs = run(
        "last_sum", last_body, z_parts, [((48, KV), F32)] * 2, [pltpu.VMEM((96, KV), F32)]
    )
    theirs = swap(theirs, "core")
    grad_codes, grad_gain = run(
        "place_codes", place_body, [mine, theirs], [((40, 2 * KV), F32), ((8, KV), F32)]
    )
    return (keys, values, grad_tokens, grad_codes, grad_gain[0])


def solution(mesh):
    rows = P(("node", "group"), None)
    in_specs = (rows, P("node", None), P("node", None), P(), rows, rows, P())
    out_specs = (rows, rows, rows, rows, P())
    return jax.shard_map(
        on_device, mesh=mesh, in_specs=in_specs, out_specs=out_specs, check_vma=False
    )
```

```python
import jax
import jax.numpy as jnp
from jax import lax
from jax.experimental import pallas as pl
from jax.experimental.pallas import tpu as pltpu
from jax.sharding import PartitionSpec as P

BF = jnp.bfloat16
F32 = jnp.float32
GROUP = 128
AXES = ("node", "group")
TOK = 384
ROWS = 320
SHARD = 640
D = 5120
KV = 1024
HALF = 512
QUART = 256
VMEM_LIMIT = 20 * 2**20
COVER = 10**11
NT = (((1,), (1,)), ((), ()))
TN = (((0,), (0,)), ((), ()))


def coords(i):
    y, z_lo, core, x, z_hi = i % 4, (i // 4) % 2, (i // 8) % 2, (i // 16) % 4, i // 64
    return z_hi * 2 + z_lo, x, core, y


def flat(z, x, core, y):
    return (((z // 2 * 4 + x) * 2 + core) * 2 + z % 2) * 4 + y


def near(n, which):
    return n ^ 1 if which == 0 else 3 - n


def pairs_of(axis, step):
    out = []
    for i in range(128):
        z, x, core, y = coords(i)
        which = step ^ core
        if axis == "core":
            out.append((i, flat(z, x, 1 - core, y)))
        if axis == "x":
            out.append((i, flat(z, near(x, which), core, y)))
        if axis == "y":
            out.append((i, flat(z, x, core, near(y, which))))
        if axis == "z":
            out.append((i, flat(near(z, which), x, core, y)))
        if axis == "zb":
            out.append((i, flat(3 - z, x, core, y)))
        if axis == "za":
            out.append((i, flat(z ^ 1, x, core, y)))
        if axis == "x_far":
            out.append((i, flat(z, (x + 2) % 4, core, y)))
        if axis == "y_far":
            out.append((i, flat(z, x, core, (y + 2) % 4)))
        if axis == "z_far":
            out.append((i, flat((z + 2) % 4, x, core, y)))
    return out


def swap(v, axis, step=0):
    return lax.ppermute(v, AXES, pairs_of(axis, step))


def dot(a, b, dims=(((1,), (0,)), ((), ()))):
    return lax.dot_general(a, b, dims, preferred_element_type=F32)


def f32(v):
    return v.astype(F32)


def columns(n):
    return pl.ds(pl.multiple_of(n * SHARD, GROUP), SHARD)


class Chain:
    def __init__(self):
        self.last = None

    def __call__(self, name, body, ids, arrays, shapes, scratch, flops, after):
        vm = pl.BlockSpec(memory_space=pltpu.VMEM)
        n_in = len(arrays)
        extra = ([] if self.last is None else [self.last]) + list(after)

        def kernel(*refs):
            body(refs[0], refs[1 : 1 + n_in], refs[1 + n_in + len(extra) :])

        out = pl.pallas_call(
            kernel,
            in_specs=[pl.BlockSpec(memory_space=pltpu.SMEM)]
            + [vm] * n_in
            + [pl.BlockSpec(memory_space=pl.ANY)] * len(extra),
            out_specs=[vm] * len(shapes),
            out_shape=[jax.ShapeDtypeStruct(s, t) for s, t in shapes],
            scratch_shapes=list(scratch),
            compiler_params=pltpu.CompilerParams(vmem_limit_bytes=VMEM_LIMIT),
            cost_estimate=pl.CostEstimate(flops=flops, bytes_accessed=1000, transcendentals=0),
            name=name,
        )(ids, *arrays, *extra)
        self.last = out[-1]
        return out


CORE = 8
Z_LO = 21


def dequant_body(first, ids, ins, outs):
    own, oth, s_own, s_oth = ins
    for c in (0, 1):

        @pl.when(ids[CORE] == c)
        def _():
            for r in (0, 1):
                codes = own if r == c else oth
                scale = s_own if r == c else s_oth
                per = 4 // len(outs)
                for j in range(4):
                    b = first + c * 4 + j
                    at = j % per * GROUP
                    outs[j // per][r * ROWS : (r + 1) * ROWS, at : at + GROUP] = (
                        f32(codes[:, b * GROUP : (b + 1) * GROUP]) * f32(scale[:, b : b + 1])
                    ).astype(BF)


def stack_body(ids, ins, outs):
    outs[0][0] = ins[0][...]
    outs[0][1] = ins[1][...]


def stack_half_body(ids, ins, outs):
    outs[0][0] = ins[0][...]
    outs[0][1] = ins[1][...]
    cols = pl.ds(pl.multiple_of((1 - ids[Z_LO]) * QUART, GROUP), QUART)
    outs[1][0] = ins[0][:, cols]
    outs[1][1] = ins[1][:, cols]


def cut_half_body(ids, ins, outs):
    cols = pl.ds(pl.multiple_of((1 - ids[Z_LO]) * QUART, GROUP), QUART)
    outs[0][...] = ins[0][:, :, cols]


def half_body(ids, ins, outs):
    outs[0][...] = cot_columns(ins[0], 1 - ids[CORE])
    outs[1][...] = cot_columns(ins[1], 1 - ids[CORE])


def cot_columns(ref, core):
    return ref[:, pl.ds(pl.multiple_of(core * HALF, GROUP), HALF)]


def add_products(ids, tokens, out, pieces, first):
    fresh = [first, first]
    for ref, n, shard, half in pieces:
        cols = slice(half * QUART, (half + 1) * QUART)
        for t, tok in enumerate(tokens):
            here = slice(t * TOK, (t + 1) * TOK)
            value = dot(tok[:, columns(ids[shard])], ref[n])
            if fresh[half]:
                out[here, cols] = value
            else:
                out[here, cols] += value
        fresh[half] = False


def early_pieces(s1, r1, s2, q2):
    return [(s1, 0, 0, 0), (s1, 1, 4, 0), (r1, 0, 1, 0), (r1, 1, 5, 0)] + [
        (s2, 0, 0, 1), (s2, 1, 1, 1), (q2, 0, 2, 1), (q2, 1, 3, 1)
    ]


def late_pieces(q1, p1, za, zc):
    return [(q1, 0, 2, 0), (q1, 1, 6, 0), (p1, 0, 3, 0), (p1, 1, 7, 0)] + [
        (za, 0, 4, 1), (za, 1, 5, 1), (zc, 0, 6, 1), (zc, 1, 7, 1)
    ]


def value_shard(ids, refs, shard):
    s2, q2, zs, zq, os, oq = refs
    x_slot = shard % 4
    if shard < 4:
        return (s2 if x_slot < 2 else q2)[x_slot % 2]
    mine = (zs if x_slot < 2 else zq)[x_slot % 2]
    other = (os if x_slot < 2 else oq)[x_slot % 2]
    even = ids[Z_LO] == 0
    return jnp.concatenate([jnp.where(even, mine, other), jnp.where(even, other, mine)], axis=1)


def early_body(ids, ins, outs):
    add_products(ids, ins[:2], outs[0], early_pieces(*ins[2:6]), True)


def late_body(ids, ins, outs):
    raw, cot_own, cot_oth, gain = ins[6:10]
    out, stats = outs
    out[...] = raw[...]
    add_products(ids, ins[:2], out, late_pieces(*ins[2:6]), False)
    lane = lax.broadcasted_iota(jnp.int32, (TOK, GROUP), 1)
    gains = cot_columns(gain, ids[CORE])
    for n, cot in enumerate((cot_columns(cot_own, ids[CORE]), cot_oth[...])):
        here = slice(n * TOK, (n + 1) * TOK)
        part = out[here, :]
        square = jnp.sum(part * part, axis=1, keepdims=True)
        cross = jnp.sum(part * (f32(cot) * gains), axis=1, keepdims=True)
        stats[here, :] = jnp.where(lane == 0, square, jnp.where(lane == 1, cross, 0.0))


def norm_body(ids, ins, outs):
    raw, mine, theirs, cot_own, cot_oth, gain = ins
    gsum = outs[4]
    weight = cot_columns(gain, ids[CORE])
    total = jnp.zeros((8, HALF), F32)
    for n, cot in enumerate((cot_columns(cot_own, ids[CORE]), cot_oth[...])):
        here = slice(n * TOK, (n + 1) * TOK)
        there = slice((1 - n) * TOK, (2 - n) * TOK)
        square = mine[here, 0:1] + theirs[there, 0:1]
        cross = mine[here, 1:2] + theirs[there, 1:2]
        inverse = lax.rsqrt(square * (1.0 / KV) + 1e-06)
        normed = raw[here, :] * inverse
        cotangent = f32(cot)
        outs[n][...] = (normed * weight).astype(BF)
        mean = cross * inverse * (1.0 / KV)
        outs[2 + n][...] = (inverse * (cotangent * weight - normed * mean)).astype(BF)
        total += jnp.sum((cotangent * normed).reshape(TOK // 8, 8, HALF), axis=0)
    gsum[...] = jnp.broadcast_to(jnp.sum(total, axis=0, keepdims=True), (8, HALF))


def value_body(ids, ins, outs):
    acc = outs[2]
    for shard in range(8):
        weight = value_shard(ids, ins[2:8], shard)
        for n in (0, 1):
            here = slice(n * TOK, (n + 1) * TOK)
            value = dot(ins[n][:, columns(ids[shard])], weight)
            if shard == 0:
                acc[here, :] = value
            else:
                acc[here, :] += value
    outs[0][...] = acc[:TOK, :].astype(BF)
    outs[1][...] = acc[TOK:, :].astype(BF)


def back_body(ids, ins, outs):
    g_key, g_val = ins[:2]
    own = len(ins) > 16
    grad = jnp.concatenate([g_key[...], cot_columns(g_val, ids[CORE]) if own else g_val[...]], axis=1)
    where = {}
    for ref, n, shard, half in early_pieces(*ins[2:6]) + late_pieces(*ins[6:10]):
        where[shard, half] = ref[n]
    for shard in range(8):
        parts = [where[shard, 0], where[shard, 1], value_shard(ids, ins[10:16], shard)]
        value = dot(grad, jnp.concatenate(parts, axis=1), NT)
        if own:
            value += f32(ins[16][:, columns(ids[shard])])
        outs[0][:, columns(ids[shard])] = value.astype(BF)
    if own:
        outs[1][...] = jnp.zeros_like(outs[1])


def piece(prod, offset, extra):
    low = prod[pl.ds(pl.multiple_of(offset, 8), 40), :]
    high = prod[pl.ds(pl.multiple_of(offset + ROWS, 8), 40), :]
    return jnp.concatenate([low, high] + extra, axis=0).astype(BF)


def two_rows(total):
    row = lax.broadcasted_iota(jnp.int32, (16, total.shape[1]), 0)
    high = f32(total.astype(BF))
    return jnp.where(row == 0, high, jnp.where(row == 1, total - high, 0.0))


def with_gain(total):
    return jnp.concatenate(
        [total[:80], two_rows(jnp.sum(total[80:], axis=0, keepdims=True))], axis=0
    ).astype(BF)


def codes_body(kind, base, width, grads, ids, ins, outs):
    t_own, t_oth, g_own, g_oth, scale = ins[:5]
    keep, send, prod = outs
    g_own, g_oth = grads(ids, g_own, g_oth)
    extra = [two_rows(ins[5][0:1, base * GROUP : base * GROUP + width])] if len(ins) > 5 else []

    def block_codes(near_half, pair, k):
        sx = pair + (0 if near_half else 2)
        block = ids[9 + sx * 2 + k]
        total = dot(t_own[:, columns(block)], g_own, TN) + dot(t_oth[:, columns(block)], g_oth, TN)
        rows = pl.ds(pl.multiple_of(block * SHARD, SHARD), SHARD)
        factor = scale[rows, base : base + width // GROUP]
        for j in range(width // GROUP):
            cols = slice(j * GROUP, (j + 1) * GROUP)
            prod[:, cols] = total[:, cols] * factor[:, j : j + 1]
        for m in (0, 1):
            z_slot = ids[17 + k * 2 + m]
            for s in range(4):
                value = piece(prod, ids[21 + m] * 160 + ids[23 + s] * 40, extra)
                if kind == "y":
                    (keep if s < 2 else send)[s % 2, sx, z_slot] = value
                else:
                    (keep if near_half else send)[pair, s, z_slot] = value

    for near_half in (False, True):

        @pl.loop(0, 2)
        def _(pair):
            block_codes(near_half, pair, 0)
            block_codes(near_half, pair, 1)


def summed(parts, at, gains):
    total = f32(parts[0][at])
    for part in parts[1:]:
        total += f32(part[at])
    return with_gain(total) if gains else total.astype(BF)


def add2_body(gains, ids, ins, outs):
    keep, first = ins[0].at[1], ins[1].at[1]
    for i in range(4):
        if keep.shape[0] == 4 and len(keep.shape) == 4:
            for j in range(4):
                outs[0][i, j] = summed([keep, first], (i, j), gains)
        else:
            outs[0][i] = summed([keep, first], i, gains)


def add3_body(gains, ids, ins, outs):
    keep, first, second = ins[0].at[0], ins[1].at[0], ins[2]
    for i in range(4):
        for j in range(4):
            outs[i // 2][i % 2, j] = summed([keep, first, second], (i, j), gains)


def merge_body(ids, ins, outs):
    for n, (at, width) in enumerate(((0, QUART), (QUART, QUART), (HALF, HALF))):
        keep, first, second = ins[3 * n].at[0], ins[3 * n + 1].at[0], ins[3 * n + 2]
        rows = 80 if n == 2 else 96
        for s in range(4):
            outs[s][:rows, at : at + width] = summed([keep, first, second], s, n < 2)
            if n == 2:
                outs[s][80:, at : at + width] = jnp.zeros((16, width), BF)


def last_body(ids, ins, outs):
    mine, theirs, total = outs
    total[...] = f32(ins[0][...]) + f32(ins[1][...]) + f32(ins[2][...]) + f32(ins[3][...])
    gain = jnp.broadcast_to(jnp.sum(total[80:, :], axis=0, keepdims=True), (8, KV))
    for out, core in ((mine, ids[CORE]), (theirs, 1 - ids[CORE])):
        out[:40, :] = total[pl.ds(pl.multiple_of(core * 40, 8), 40), :]
        out[40:, :] = gain


def halves_body(ids, ins, outs):
    for c in (0, 1):

        @pl.when(ids[CORE] == c)
        def _():
            outs[0][:, c * HALF : (c + 1) * HALF] = ins[0][...]
            outs[0][:, (1 - c) * HALF : (2 - c) * HALF] = ins[1][...]


def place_body(ids, ins, outs):
    mine, theirs = ins
    for c in (0, 1):

        @pl.when(ids[CORE] == c)
        def _():
            for n in range(4):
                source = mine if n % 2 == c else theirs
                outs[0][:, n * HALF : (n + 1) * HALF] = source[:40, n // 2 * HALF : (n // 2 + 1) * HALF]
            for n in range(2):
                source = mine if n == c else theirs
                outs[1][:, n * HALF : (n + 1) * HALF] = source[40:, :HALF]


def on_device(tokens, w_codes, w_scale, gain, key_cot, value_cot, grad_scale):
    node, group = lax.axis_index("node"), lax.axis_index("group")
    z_hi, x, core = node // 8, (node // 2) % 4, node % 2
    z_lo, y = group // 4, group % 4
    z = z_hi * 2 + z_lo

    def ring(n):
        a, b = n ^ 1, 3 - n
        first, second = jnp.where(core == 0, a, b), jnp.where(core == 0, b, a)
        return [n, second, first, (n + 2) % 4]

    x_of, y_of, z_of = ring(x), ring(y), ring(z)
    slot_of = lambda places, n: sum(jnp.where(places[s] == n, s, 0) for s in range(4))
    ids = jnp.stack(
        [
            jnp.asarray(v, jnp.int32)
            for v in [(z_hi ^ dz) * 4 + x_of[s] for dz in (0, 1) for s in (0, 2, 1, 3)]
            + [core]
            + [(z_hi ^ k) * 4 + x_of[s] for s in range(4) for k in (0, 1)]
            + [slot_of(z_of, (z_hi ^ k) * 2 + (z_lo ^ m)) for k in (0, 1) for m in (0, 1)]
            + [z_lo, z_lo ^ 1]
            + y_of
        ]
    )
    chain = Chain()

    def run(name, body, arrays, shapes, scratch=(), flops=1000, after=()):
        return chain(name, body, ids, arrays, shapes, scratch, flops, after)

    def codes(kind, base, width, rows, grads, arrays, after=()):
        return run(
            "gradient_codes",
            lambda *a: codes_body(kind, base, width, grads, *a),
            both_t + arrays,
            [((2, 4, 4, rows, width), BF)] * 2,
            [pltpu.VMEM((SHARD, width), F32)],
            flops=COVER,
            after=after,
        )

    def add2(keep, first, after=()):
        gains = keep.shape[-2] > 80
        body = lambda *a: add2_body(gains, *a)
        return run("add_two", body, [keep, first], [(keep.shape[1:], BF)], after=after)[0]

    def add3(keep, first, second, after=()):
        gains = keep.shape[-2] > 80
        body = lambda *a: add3_body(gains, *a)
        shape = (2,) + keep.shape[2:]
        return run("add_three", body, [keep, first, second], [(shape, BF)] * 2, after=after)

    def direct(axis, slots):
        return [
            slots[0],
            swap(slots[1], axis, 1),
            swap(slots[2], axis, 0),
            swap(slots[3], axis + "_far"),
        ]

    codes_oth = swap(w_codes, "core")
    scale_oth = swap(w_scale, "core")
    t_oth = swap(tokens, "core")
    both_t = [tokens, t_oth]
    gain2 = gain.reshape(1, KV)
    factors = 1.0 / jnp.concatenate(
        [
            lax.dynamic_slice_in_dim(grad_scale, core * 4, 4, axis=1),
            lax.dynamic_slice_in_dim(grad_scale, 8 + core * 4, 4, axis=1),
        ],
        axis=1,
    )
    vc_send, kc_send = run("halves", half_body, [value_cot, key_cot], [((TOK, HALF), BF)] * 2)
    vc_oth, kc_oth = swap(vc_send, "core"), swap(kc_send, "core")

    def shards(first, widths, after=()):
        return run(
            "dequantize",
            lambda *a: dequant_body(first, *a),
            [w_codes, codes_oth, w_scale, scale_oth],
            [((SHARD, w), BF) for w in widths],
            after=after,
        )

    def stack(a, b):
        return run("stack_shards", stack_body, [a, b], [((2, SHARD, QUART), BF)])[0]

    join = lambda own, oth: run("join_halves", halves_body, [own, oth], [((TOK, KV), BF)])[0]

    ka, kb = shards(0, [QUART, QUART])
    k_g = swap(ka, "zb")
    k_x = swap(kb, "x", 0)
    v_cols = lambda ids, own, oth: (cot_columns(own, ids[CORE]), oth[...])
    v_keep, v_send = codes("y", 4, HALF, 80, v_cols, [value_cot, vc_oth, factors], [kc_oth])
    v_first = swap(v_send, "y", 0)
    k_s2 = stack(kb, k_x)
    k_q2 = swap(k_s2, "x", 1)
    k_za = swap(k_s2, "zb")
    k_s1 = stack(ka, k_g)
    k_r1 = swap(k_s1, "x", 0)
    k_q1 = swap(k_s1, "x", 1)
    k_zc = swap(k_q2, "zb")
    k_p1 = swap(k_r1, "x", 1)
    k_early, k_late = [k_s1, k_r1, k_s2, k_q2], [k_q1, k_p1, k_za, k_zc]
    raw = run(
        "key_projection_early", early_body, both_t + k_early, [((2 * TOK, HALF), F32)], flops=COVER
    )[0]
    vw = shards(8, [HALF], [k_za, k_q1])[0]
    v_x = swap(vw, "x", 0)
    raw, stats = run(
        "key_projection_late",
        late_body,
        both_t + k_late + [raw, key_cot, kc_oth, gain2],
        [((2 * TOK, HALF), F32), ((2 * TOK, GROUP), F32)],
        flops=COVER,
    )
    stats_oth = swap(stats, "core")
    v_s2, v_h2 = run(
        "stack_shards",
        stack_half_body,
        [vw, v_x],
        [((2, SHARD, HALF), BF), ((2, SHARD, QUART), BF)],
    )
    v_q2 = swap(v_s2, "x", 1)
    v_zs = swap(v_h2, "zb")
    v_second = swap(add2(v_keep, v_first), "y", 1)
    k_own, k_oth, g_own, g_oth, gsum = run(
        "key_norm",
        norm_body,
        [raw, stats, stats_oth, key_cot, kc_oth, gain2],
        [((TOK, HALF), BF)] * 4 + [((8, HALF), F32)],
    )
    a_cols = lambda ids, own, oth: (own[:, :QUART], oth[:, :QUART])
    a_keep, a_send = codes("y", 0, QUART, 96, a_cols, [g_own, g_oth, factors, gsum])
    a_first = swap(a_send, "y", 0)
    v_os = swap(v_zs, "za")
    b_cols = lambda ids, own, oth: (own[:, QUART:], oth[:, QUART:])
    b_keep, b_send = codes("x", 2, QUART, 96, b_cols, [g_own, g_oth, factors, gsum])
    b_first = swap(b_send, "x", 0)
    v_keep, v_send = add3(v_keep, v_first, v_second, [v_zs])
    v_first = swap(v_send, "x", 0)
    v_hq = run("cut_columns", cut_half_body, [v_q2], [((2, SHARD, QUART), BF)])[0]
    v_zq = swap(v_hq, "zb")
    v_oq = swap(v_zq, "za")
    keys = join(k_own, swap(k_oth, "core"))

    a_second = swap(add2(a_keep, a_first), "y", 1)
    b_second = swap(add2(b_keep, b_first), "x", 1)
    v_second = swap(add2(v_keep, v_first), "x", 1)
    v_weights = [v_s2, v_q2, v_zs, v_zq, v_os, v_oq]
    weights = k_early + k_late + v_weights
    sent = run(
        "token_gradient", back_body, [g_oth, vc_oth] + weights, [((TOK, D), BF)], flops=COVER
    )[0]
    received = swap(sent, "core")
    a_keep, a_send = add3(a_keep, a_first, a_second)
    a_first = swap(a_send, "x", 0)
    b_keep, b_send = add3(b_keep, b_first, b_second)
    b_first = swap(b_send, "y", 0)
    v_own, v_oth = run(
        "value_projection",
        value_body,
        both_t + v_weights,
        [((TOK, HALF), BF)] * 2,
        [pltpu.VMEM((2 * TOK, HALF), F32)],
        flops=COVER,
    )
    a_second = swap(add2(a_keep, a_first), "x", 1)
    b_second = swap(add2(b_keep, b_first), "y", 1)
    grad_tokens, _ = run(
        "token_gradient_sum",
        back_body,
        [g_own, value_cot] + weights + [received],
        [((TOK, D), BF), ((8, GROUP), F32)],
        flops=COVER,
    )
    z_slots = run(
        "merge_sums",
        merge_body,
        [a_keep, a_first, a_second, b_keep, b_first, b_second, v_keep, v_first, v_second],
        [((96, KV), BF)] * 4,
    )
    z_parts = direct("z", z_slots)
    values = join(v_own, swap(v_oth, "core"))
    mine, theirs = run(
        "last_sum", last_body, z_parts, [((48, KV), F32)] * 2, [pltpu.VMEM((96, KV), F32)]
    )
    theirs = swap(theirs, "core")
    grad_codes, grad_gain = run(
        "place_codes", place_body, [mine, theirs], [((40, 2 * KV), F32), ((8, KV), F32)]
    )
    return (keys, values, grad_tokens, grad_codes, grad_gain[0])


def solution(mesh):
    rows = P(("node", "group"), None)
    in_specs = (rows, P("node", None), P("node", None), P(), rows, rows, P())
    out_specs = (rows, rows, rows, rows, P())
    return jax.shard_map(
        on_device, mesh=mesh, in_specs=in_specs, out_specs=out_specs, check_vma=False
    )
```

```python
import jax
import jax.numpy as jnp
from jax import lax
from jax.experimental import pallas as pl
from jax.experimental.pallas import tpu as pltpu
from jax.sharding import PartitionSpec as P

BF = jnp.bfloat16
F32 = jnp.float32
GROUP = 128
AXES = ("node", "group")
TOK = 384
ROWS = 320
SHARD = 640
D = 5120
KV = 1024
HALF = 512
QUART = 256
VMEM_LIMIT = 20 * 2**20
COVER = 10**11
SMALL = 6 * 10**9
NT = (((1,), (1,)), ((), ()))
TN = (((0,), (0,)), ((), ()))


def coords(i):
    y, z_lo, core, x, z_hi = i % 4, (i // 4) % 2, (i // 8) % 2, (i // 16) % 4, i // 64
    return z_hi * 2 + z_lo, x, core, y


def flat(z, x, core, y):
    return (((z // 2 * 4 + x) * 2 + core) * 2 + z % 2) * 4 + y


def near(n, which):
    return n ^ 1 if which == 0 else 3 - n


def pairs_of(axis, step):
    out = []
    for i in range(128):
        z, x, core, y = coords(i)
        which = step ^ core
        if axis == "core":
            out.append((i, flat(z, x, 1 - core, y)))
        if axis == "x":
            out.append((i, flat(z, near(x, which), core, y)))
        if axis == "y":
            out.append((i, flat(z, x, core, near(y, which))))
        if axis == "z":
            out.append((i, flat(near(z, which), x, core, y)))
        if axis == "zb":
            out.append((i, flat(3 - z, x, core, y)))
        if axis == "za":
            out.append((i, flat(z ^ 1, x, core, y)))
        if axis == "x_far":
            out.append((i, flat(z, (x + 2) % 4, core, y)))
        if axis == "y_far":
            out.append((i, flat(z, x, core, (y + 2) % 4)))
        if axis == "z_far":
            out.append((i, flat((z + 2) % 4, x, core, y)))
    return out


def swap(v, axis, step=0):
    return lax.ppermute(v, AXES, pairs_of(axis, step))


def dot(a, b, dims=(((1,), (0,)), ((), ()))):
    return lax.dot_general(a, b, dims, preferred_element_type=F32)


def f32(v):
    return v.astype(F32)


def columns(n):
    return pl.ds(pl.multiple_of(n * SHARD, GROUP), SHARD)


class Chain:
    def __init__(self):
        self.last = None

    def __call__(self, name, body, ids, arrays, shapes, scratch, flops, after):
        vm = pl.BlockSpec(memory_space=pltpu.VMEM)
        n_in = len(arrays)
        extra = ([] if self.last is None else [self.last]) + list(after)

        def kernel(*refs):
            body(refs[0], refs[1 : 1 + n_in], refs[1 + n_in + len(extra) :])

        out = pl.pallas_call(
            kernel,
            in_specs=[pl.BlockSpec(memory_space=pltpu.SMEM)]
            + [vm] * n_in
            + [pl.BlockSpec(memory_space=pl.ANY)] * len(extra),
            out_specs=[vm] * len(shapes),
            out_shape=[jax.ShapeDtypeStruct(s, t) for s, t in shapes],
            scratch_shapes=list(scratch),
            compiler_params=pltpu.CompilerParams(vmem_limit_bytes=VMEM_LIMIT),
            cost_estimate=pl.CostEstimate(flops=flops, bytes_accessed=1000, transcendentals=0),
            name=name,
        )(ids, *arrays, *extra)
        self.last = out[-1]
        return out


CORE = 8
Z_LO = 21


def dequant_body(ids, ins, outs):
    codes, scale = ins
    for c in (0, 1):

        @pl.when(ids[CORE] == c)
        def _():
            for n, out in enumerate(outs):
                for j in range(8):
                    b = j // 4 * 8 + (c ^ n) * 4 + j % 4
                    out[:, j * GROUP : (j + 1) * GROUP] = (
                        f32(codes[:, b * GROUP : (b + 1) * GROUP]) * f32(scale[:, b : b + 1])
                    ).astype(BF)


def assemble_body(ids, ins, outs):
    for c in (0, 1):

        @pl.when(ids[CORE] == c)
        def _():
            for r in (0, 1):
                rows = slice(r * ROWS, (r + 1) * ROWS)
                source = ins[r ^ c]
                if len(outs) == 2:
                    outs[0][rows, :] = source[:, :QUART]
                    outs[1][rows, :] = source[:, QUART:HALF]
                else:
                    outs[0][rows, :] = source[:, HALF:]


def stack_body(ids, ins, outs):
    outs[0][0] = ins[0][...]
    outs[0][1] = ins[1][...]


def pass_body(ids, ins, outs):
    outs[0][...] = ins[0][...]


def stack_half_body(ids, ins, outs):
    outs[0][0] = ins[0][...]
    outs[0][1] = ins[1][...]
    cols = pl.ds(pl.multiple_of((1 - ids[Z_LO]) * QUART, GROUP), QUART)
    outs[1][0] = ins[0][:, cols]
    outs[1][1] = ins[1][:, cols]


def half_body(ids, ins, outs):
    outs[0][0] = cot_columns(ins[0], 1 - ids[CORE])
    outs[0][1] = cot_columns(ins[1], 1 - ids[CORE])


def cot_columns(ref, core):
    return ref[:, pl.ds(pl.multiple_of(core * HALF, GROUP), HALF)]


def add_products(ids, tokens, out, pieces, first):
    fresh = [first, first]
    for ref, n, shard, half in pieces:
        cols = slice(half * QUART, (half + 1) * QUART)
        for t, tok in enumerate(tokens):
            here = slice(t * TOK, (t + 1) * TOK)
            value = dot(tok[:, columns(ids[shard])], ref[n])
            if fresh[half]:
                out[here, cols] = value
            else:
                out[here, cols] += value
        fresh[half] = False


def early_pieces(s1, r1, s2, q2):
    return [(s1, 0, 0, 0), (s1, 1, 4, 0), (r1, 0, 1, 0), (r1, 1, 5, 0)] + [
        (s2, 0, 0, 1), (s2, 1, 1, 1), (q2, 0, 2, 1), (q2, 1, 3, 1)
    ]


def late_pieces(q1, p1, za, zc):
    return [(q1, 0, 2, 0), (q1, 1, 6, 0), (p1, 0, 3, 0), (p1, 1, 7, 0)] + [
        (za, 0, 4, 1), (za, 1, 5, 1), (zc, 0, 6, 1), (zc, 1, 7, 1)
    ]


def value_shard(ids, refs, shard):
    s2, q2, zs, os, zq = refs
    x_slot = shard % 4
    if shard < 4:
        return (s2 if x_slot < 2 else q2)[x_slot % 2]
    if x_slot > 1:
        return zq[x_slot % 2]
    mine, other = zs[x_slot], os[x_slot]
    even = ids[Z_LO] == 0
    return jnp.concatenate([jnp.where(even, mine, other), jnp.where(even, other, mine)], axis=1)


def early_body(ids, ins, outs):
    add_products(ids, ins[:2], outs[0], early_pieces(*ins[2:6]), True)


def late_body(ids, ins, outs):
    raw, cot_own, cot_oth, gain = ins[6:10]
    out, stats = outs
    out[...] = raw[...]
    add_products(ids, ins[:2], out, late_pieces(*ins[2:6]), False)
    lane = lax.broadcasted_iota(jnp.int32, (TOK, GROUP), 1)
    gains = cot_columns(gain, ids[CORE])
    for n, cot in enumerate((cot_columns(cot_own, ids[CORE]), cot_oth[1])):
        here = slice(n * TOK, (n + 1) * TOK)
        part = out[here, :]
        square = jnp.sum(part * part, axis=1, keepdims=True)
        cross = jnp.sum(part * (f32(cot) * gains), axis=1, keepdims=True)
        stats[here, :] = jnp.where(lane == 0, square, jnp.where(lane == 1, cross, 0.0))


def norm_body(ids, ins, outs):
    raw, mine, theirs, cot_own, cot_oth, gain = ins
    gsum = outs[4]
    weight = cot_columns(gain, ids[CORE])
    total = jnp.zeros((8, HALF), F32)
    for n, cot in enumerate((cot_columns(cot_own, ids[CORE]), cot_oth[1])):
        here = slice(n * TOK, (n + 1) * TOK)
        there = slice((1 - n) * TOK, (2 - n) * TOK)
        square = mine[here, 0:1] + theirs[there, 0:1]
        cross = mine[here, 1:2] + theirs[there, 1:2]
        inverse = lax.rsqrt(square * (1.0 / KV) + 1e-06)
        normed = raw[here, :] * inverse
        cotangent = f32(cot)
        outs[n][...] = (normed * weight).astype(BF)
        mean = cross * inverse * (1.0 / KV)
        outs[2 + n][...] = (inverse * (cotangent * weight - normed * mean)).astype(BF)
        total += jnp.sum((cotangent * normed).reshape(TOK // 8, 8, HALF), axis=0)
    gsum[...] = jnp.broadcast_to(jnp.sum(total, axis=0, keepdims=True), (8, HALF))


def value_body(ids, ins, outs):
    acc = outs[2]
    for shard in range(8):
        weight = value_shard(ids, ins[2:7], shard)
        for n in (0, 1):
            here = slice(n * TOK, (n + 1) * TOK)
            value = dot(ins[n][:, columns(ids[shard])], weight)
            if shard == 0:
                acc[here, :] = value
            else:
                acc[here, :] += value
    outs[0][...] = acc[:TOK, :].astype(BF)
    outs[1][...] = acc[TOK:, :].astype(BF)


def back_body(ids, ins, outs):
    g_key, g_val = ins[:2]
    own = len(ins) > 15
    grad = jnp.concatenate([g_key[...], cot_columns(g_val, ids[CORE]) if own else g_val[0]], axis=1)
    where = {}
    for ref, n, shard, half in early_pieces(*ins[2:6]) + late_pieces(*ins[6:10]):
        where[shard, half] = ref[n]
    for shard in range(8):
        parts = [where[shard, 0], where[shard, 1], value_shard(ids, ins[10:15], shard)]
        value = dot(grad, jnp.concatenate(parts, axis=1), NT)
        if own:
            value += f32(ins[15][:, columns(ids[shard])])
        outs[0][:, columns(ids[shard])] = value.astype(BF)
    if own:
        outs[1][...] = jnp.zeros_like(outs[1])


def piece(prod, offset, extra):
    low = prod[pl.ds(pl.multiple_of(offset, 8), 40), :]
    high = prod[pl.ds(pl.multiple_of(offset + ROWS, 8), 40), :]
    return jnp.concatenate([low, high] + extra, axis=0).astype(BF)


def two_rows(total):
    row = lax.broadcasted_iota(jnp.int32, (16, total.shape[1]), 0)
    high = f32(total.astype(BF))
    return jnp.where(row == 0, high, jnp.where(row == 1, total - high, 0.0))


def with_gain(total):
    return jnp.concatenate(
        [total[:80], two_rows(jnp.sum(total[80:], axis=0, keepdims=True))], axis=0
    ).astype(BF)


def codes_body(kind, base, width, grads, ids, ins, outs):
    t_own, t_oth, g_own, g_oth, scale = ins[:5]
    keep, send, prod = outs
    g_own, g_oth = grads(ids, g_own, g_oth)
    extra = [two_rows(ins[5][0:1, base * GROUP : base * GROUP + width])] if len(ins) > 5 else []

    def block_codes(near_half, pair, k):
        sx = pair + (0 if near_half else 2)
        block = ids[9 + sx * 2 + k]
        total = dot(t_own[:, columns(block)], g_own, TN) + dot(t_oth[:, columns(block)], g_oth, TN)
        rows = pl.ds(pl.multiple_of(block * SHARD, SHARD), SHARD)
        factor = scale[rows, base : base + width // GROUP]
        for j in range(width // GROUP):
            cols = slice(j * GROUP, (j + 1) * GROUP)
            prod[:, cols] = total[:, cols] * factor[:, j : j + 1]
        for m in (0, 1):
            z_slot = ids[17 + k * 2 + m]
            for s in range(4):
                value = piece(prod, ids[21 + m] * 160 + ids[23 + s] * 40, extra)
                if kind == "y":
                    (keep if s < 2 else send)[s % 2, sx, z_slot] = value
                else:
                    (keep if near_half else send)[pair, s, z_slot] = value

    for near_half in (False, True):

        @pl.loop(0, 2)
        def _(pair):
            block_codes(near_half, pair, 0)
            block_codes(near_half, pair, 1)


def summed(parts, at, gains):
    total = f32(parts[0][at])
    for part in parts[1:]:
        total += f32(part[at])
    return with_gain(total) if gains else total.astype(BF)


def add2_body(gains, ids, ins, outs):
    keep, first = ins[0].at[1], ins[1].at[1]
    for i in range(4):
        if keep.shape[0] == 4 and len(keep.shape) == 4:
            for j in range(4):
                outs[0][i, j] = summed([keep, first], (i, j), gains)
        else:
            outs[0][i] = summed([keep, first], i, gains)


def add3_body(gains, ids, ins, outs):
    keep, first, second = ins[0].at[0], ins[1].at[0], ins[2]
    for i in range(4):
        for j in range(4):
            outs[i // 2][i % 2, j] = summed([keep, first, second], (i, j), gains)


def merge_body(ids, ins, outs):
    for n, (at, width) in enumerate(((0, QUART), (QUART, QUART), (HALF, HALF))):
        keep, first, second = ins[3 * n].at[0], ins[3 * n + 1].at[0], ins[3 * n + 2]
        rows = 80 if n == 2 else 96
        for s in range(4):
            outs[s][:rows, at : at + width] = summed([keep, first, second], s, n < 2)
            if n == 2:
                outs[s][80:, at : at + width] = jnp.zeros((16, width), BF)


def last_body(ids, ins, outs):
    mine, theirs, total = outs
    total[...] = f32(ins[0][...]) + f32(ins[1][...]) + f32(ins[2][...]) + f32(ins[3][...])
    gain = jnp.broadcast_to(jnp.sum(total[80:, :], axis=0, keepdims=True), (8, KV))
    for out, core in ((mine, ids[CORE]), (theirs, 1 - ids[CORE])):
        out[:40, :] = total[pl.ds(pl.multiple_of(core * 40, 8), 40), :]
        out[40:, :] = gain


def halves_body(ids, ins, outs):
    for c in (0, 1):

        @pl.when(ids[CORE] == c)
        def _():
            outs[0][:, c * HALF : (c + 1) * HALF] = ins[0][...]
            outs[0][:, (1 - c) * HALF : (2 - c) * HALF] = ins[1][...]


def place_body(ids, ins, outs):
    mine, theirs = ins
    for c in (0, 1):

        @pl.when(ids[CORE] == c)
        def _():
            for n in range(4):
                source = mine if n % 2 == c else theirs
                outs[0][:, n * HALF : (n + 1) * HALF] = source[:40, n // 2 * HALF : (n // 2 + 1) * HALF]
            for n in range(2):
                source = mine if n == c else theirs
                outs[1][:, n * HALF : (n + 1) * HALF] = source[40:, :HALF]


def on_device(tokens, w_codes, w_scale, gain, key_cot, value_cot, grad_scale):
    node, group = lax.axis_index("node"), lax.axis_index("group")
    z_hi, x, core = node // 8, (node // 2) % 4, node % 2
    z_lo, y = group // 4, group % 4
    z = z_hi * 2 + z_lo

    def ring(n):
        a, b = n ^ 1, 3 - n
        first, second = jnp.where(core == 0, a, b), jnp.where(core == 0, b, a)
        return [n, second, first, (n + 2) % 4]

    x_of, y_of, z_of = ring(x), ring(y), ring(z)
    slot_of = lambda places, n: sum(jnp.where(places[s] == n, s, 0) for s in range(4))
    ids = jnp.stack(
        [
            jnp.asarray(v, jnp.int32)
            for v in [(z_hi ^ dz) * 4 + x_of[s] for dz in (0, 1) for s in (0, 2, 1, 3)]
            + [core]
            + [(z_hi ^ k) * 4 + x_of[s] for s in range(4) for k in (0, 1)]
            + [slot_of(z_of, (z_hi ^ k) * 2 + (z_lo ^ m)) for k in (0, 1) for m in (0, 1)]
            + [z_lo, z_lo ^ 1]
            + y_of
        ]
    )
    chain = Chain()

    def run(name, body, arrays, shapes, scratch=(), flops=1000, after=()):
        return chain(name, body, ids, arrays, shapes, scratch, flops, after)

    def codes(kind, base, width, rows, grads, arrays, after=()):
        return run(
            "gradient_codes",
            lambda *a: codes_body(kind, base, width, grads, *a),
            both_t + arrays,
            [((2, 4, 4, rows, width), BF)] * 2,
            [pltpu.VMEM((SHARD, width), F32)],
            flops=SMALL if base == 0 else COVER,
            after=after,
        )

    def add2(keep, first, after=()):
        gains = keep.shape[-2] > 80
        body = lambda *a: add2_body(gains, *a)
        return run("add_two", body, [keep, first], [(keep.shape[1:], BF)], after=after)[0]

    def add3(keep, first, second, after=()):
        gains = keep.shape[-2] > 80
        body = lambda *a: add3_body(gains, *a)
        shape = (2,) + keep.shape[2:]
        return run("add_three", body, [keep, first, second], [(shape, BF)] * 2, after=after)

    def direct(axis, slots):
        return [
            slots[0],
            swap(slots[1], axis, 1),
            swap(slots[2], axis, 0),
            swap(slots[3], axis + "_far"),
        ]

    w_mine, w_send = run("dequantize", dequant_body, [w_codes, w_scale], [((ROWS, KV), BF)] * 2)
    w_came = swap(w_send, "core")
    t_oth = swap(tokens, "core")
    both_t = [tokens, t_oth]
    gain2 = gain.reshape(1, KV)
    factors = 1.0 / jnp.concatenate(
        [
            lax.dynamic_slice_in_dim(grad_scale, core * 4, 4, axis=1),
            lax.dynamic_slice_in_dim(grad_scale, 8 + core * 4, 4, axis=1),
        ],
        axis=1,
    )
    cots = swap(run("halves", half_body, [value_cot, key_cot], [((2, TOK, HALF), BF)])[0], "core")

    def stack(a, b, after):
        return run("stack_shards", stack_body, [a, b], [((2, SHARD, QUART), BF)], after=after)[0]

    join = lambda own, oth: run("join_halves", halves_body, [own, oth], [((TOK, KV), BF)])[0]

    ka, kb = run("assemble", assemble_body, [w_mine, w_came], [((SHARD, QUART), BF)] * 2)
    k_g = swap(ka, "zb")
    k_x = swap(kb, "x", 0)
    k_s2 = stack(kb, k_x, [cots])
    k_q2 = swap(k_s2, "x", 1)
    k_za = swap(k_s2, "zb")
    k_s1 = stack(ka, k_g, [t_oth])
    k_r1 = swap(k_s1, "x", 0)
    k_q1 = swap(k_s1, "x", 1)
    v_cols = lambda ids, own, oth: (cot_columns(own, ids[CORE]), oth[0])
    v_keep, v_send = codes("y", 4, HALF, 80, v_cols, [value_cot, cots, factors])
    v_first = swap(v_send, "y", 0)
    k_q2 = run("pass_shards", pass_body, [k_q2], [((2, SHARD, QUART), BF)])[0]
    k_zc = swap(k_q2, "zb")
    k_p1 = swap(k_r1, "x", 1)
    k_early, k_late = [k_s1, k_r1, k_s2, k_q2], [k_q1, k_p1, k_za, k_zc]
    raw = run(
        "key_projection_early",
        early_body,
        both_t + k_early,
        [((2 * TOK, HALF), F32)],
        flops=3 * SMALL,
        after=[k_za],
    )[0]
    vw = run(
        "assemble", assemble_body, [w_mine, w_came], [((SHARD, HALF), BF)], after=[k_q1]
    )[0]
    v_x = swap(vw, "x", 0)
    raw, stats = run(
        "key_projection_late",
        late_body,
        both_t + k_late + [raw, key_cot, cots, gain2],
        [((2 * TOK, HALF), F32), ((2 * TOK, GROUP), F32)],
        flops=SMALL,
    )
    stats_oth = swap(stats, "core")
    v_s2, v_h2 = run(
        "stack_shards",
        stack_half_body,
        [vw, v_x],
        [((2, SHARD, HALF), BF), ((2, SHARD, QUART), BF)],
    )
    v_q2 = swap(v_s2, "x", 1)
    v_zs = swap(v_h2, "zb")
    k_own, k_oth, g_own, g_oth, gsum = run(
        "key_norm",
        norm_body,
        [raw, stats, stats_oth, key_cot, cots, gain2],
        [((TOK, HALF), BF)] * 4 + [((8, HALF), F32)],
    )
    a_cols = lambda ids, own, oth: (own[:, :QUART], oth[:, :QUART])
    a_keep, a_send = codes("y", 0, QUART, 96, a_cols, [g_own, g_oth, factors, gsum])
    a_first = swap(a_send, "y", 0)
    v_second = swap(add2(v_keep, v_first), "y", 1)
    v_os = swap(v_zs, "za")
    b_cols = lambda ids, own, oth: (own[:, QUART:], oth[:, QUART:])
    b_keep, b_send = codes("x", 2, QUART, 96, b_cols, [g_own, g_oth, factors, gsum])
    b_first = swap(b_send, "x", 0)
    v_zq = swap(v_q2, "zb")
    a_second = swap(add2(a_keep, a_first, [v_zs, v_q2]), "y", 1)
    b_second = swap(add2(b_keep, b_first), "x", 1)
    v_keep, v_send = add3(v_keep, v_first, v_second)
    v_first = swap(v_send, "x", 0)
    keys = join(k_own, swap(k_oth, "core"))
    v_weights = [v_s2, v_q2, v_zs, v_os, v_zq]
    weights = k_early + k_late + v_weights
    sent = run(
        "token_gradient", back_body, [g_oth, cots] + weights, [((TOK, D), BF)], flops=COVER
    )[0]
    received = swap(sent, "core")
    a_keep, a_send = add3(a_keep, a_first, a_second)
    a_first = swap(a_send, "x", 0)
    b_keep, b_send = add3(b_keep, b_first, b_second)
    b_first = swap(b_send, "y", 0)
    v_own, v_oth = run(
        "value_projection",
        value_body,
        both_t + v_weights,
        [((TOK, HALF), BF)] * 2,
        [pltpu.VMEM((2 * TOK, HALF), F32)],
        flops=COVER,
    )
    a_second = swap(add2(a_keep, a_first), "x", 1)
    b_second = swap(add2(b_keep, b_first), "y", 1)
    v_second = swap(add2(v_keep, v_first), "x", 1)
    grad_tokens, _ = run(
        "token_gradient_sum",
        back_body,
        [g_own, value_cot] + weights + [received],
        [((TOK, D), BF), ((8, GROUP), F32)],
        flops=COVER,
    )
    z_slots = run(
        "merge_sums",
        merge_body,
        [a_keep, a_first, a_second, b_keep, b_first, b_second, v_keep, v_first, v_second],
        [((96, KV), BF)] * 4,
    )
    z_parts = direct("z", z_slots)
    values = join(v_own, swap(v_oth, "core"))
    mine, theirs = run(
        "last_sum", last_body, z_parts, [((48, KV), F32)] * 2, [pltpu.VMEM((96, KV), F32)]
    )
    theirs = swap(theirs, "core")
    grad_codes, grad_gain = run(
        "place_codes", place_body, [mine, theirs], [((40, 2 * KV), F32), ((8, KV), F32)]
    )
    return (keys, values, grad_tokens, grad_codes, grad_gain[0])


def solution(mesh):
    rows = P(("node", "group"), None)
    in_specs = (rows, P("node", None), P("node", None), P(), rows, rows, P())
    out_specs = (rows, rows, rows, rows, P())
    return jax.shard_map(
        on_device, mesh=mesh, in_specs=in_specs, out_specs=out_specs, check_vma=False
    )
```

```python
import jax
import jax.numpy as jnp
from jax import lax
from jax.experimental import pallas as pl
from jax.experimental.pallas import tpu as pltpu
from jax.sharding import PartitionSpec as P

BF = jnp.bfloat16
F32 = jnp.float32
GROUP = 128
AXES = ("node", "group")
TOK = 384
ROWS = 320
SHARD = 640
D = 5120
KV = 1024
HALF = 512
QUART = 256
VMEM_LIMIT = 20 * 2**20
COVER = 10**11
SMALL = 6 * 10**9
NT = (((1,), (1,)), ((), ()))
TN = (((0,), (0,)), ((), ()))


def coords(i):
    y, z_lo, core, x, z_hi = i % 4, (i // 4) % 2, (i // 8) % 2, (i // 16) % 4, i // 64
    return z_hi * 2 + z_lo, x, core, y


def flat(z, x, core, y):
    return (((z // 2 * 4 + x) * 2 + core) * 2 + z % 2) * 4 + y


def near(n, which):
    return n ^ 1 if which == 0 else 3 - n


def pairs_of(axis, step):
    out = []
    for i in range(128):
        z, x, core, y = coords(i)
        which = step ^ core
        if axis == "core":
            out.append((i, flat(z, x, 1 - core, y)))
        if axis == "x":
            out.append((i, flat(z, near(x, which), core, y)))
        if axis == "y":
            out.append((i, flat(z, x, core, near(y, which))))
        if axis == "z":
            out.append((i, flat(near(z, which), x, core, y)))
        if axis == "zb":
            out.append((i, flat(3 - z, x, core, y)))
        if axis == "za":
            out.append((i, flat(z ^ 1, x, core, y)))
        if axis == "x_far":
            out.append((i, flat(z, (x + 2) % 4, core, y)))
        if axis == "y_far":
            out.append((i, flat(z, x, core, (y + 2) % 4)))
        if axis == "z_far":
            out.append((i, flat((z + 2) % 4, x, core, y)))
    return out


def swap(v, axis, step=0):
    return lax.ppermute(v, AXES, pairs_of(axis, step))


def dot(a, b, dims=(((1,), (0,)), ((), ()))):
    return lax.dot_general(a, b, dims, preferred_element_type=F32)


def f32(v):
    return v.astype(F32)


def columns(n):
    return pl.ds(pl.multiple_of(n * SHARD, GROUP), SHARD)


class Chain:
    def __init__(self):
        self.last = None

    def __call__(self, name, body, ids, arrays, shapes, scratch, flops, after):
        vm = pl.BlockSpec(memory_space=pltpu.VMEM)
        n_in = len(arrays)
        extra = ([] if self.last is None else [self.last]) + list(after)

        def kernel(*refs):
            body(refs[0], refs[1 : 1 + n_in], refs[1 + n_in + len(extra) :])

        out = pl.pallas_call(
            kernel,
            in_specs=[pl.BlockSpec(memory_space=pltpu.SMEM)]
            + [vm] * n_in
            + [pl.BlockSpec(memory_space=pl.ANY)] * len(extra),
            out_specs=[vm] * len(shapes),
            out_shape=[jax.ShapeDtypeStruct(s, t) for s, t in shapes],
            scratch_shapes=list(scratch),
            compiler_params=pltpu.CompilerParams(vmem_limit_bytes=VMEM_LIMIT),
            cost_estimate=pl.CostEstimate(flops=flops, bytes_accessed=1000, transcendentals=0),
            name=name,
        )(ids, *arrays, *extra)
        self.last = out[-1]
        return out


CORE = 8
Z_LO = 21


def dequant_body(ids, ins, outs):
    codes, scale = ins
    for c in (0, 1):

        @pl.when(ids[CORE] == c)
        def _():
            for n, out in enumerate(outs):
                for j in range(8):
                    b = j // 4 * 8 + (c ^ n) * 4 + j % 4
                    out[:, j * GROUP : (j + 1) * GROUP] = (
                        f32(codes[:, b * GROUP : (b + 1) * GROUP]) * f32(scale[:, b : b + 1])
                    ).astype(BF)


def assemble_body(ids, ins, outs):
    for c in (0, 1):

        @pl.when(ids[CORE] == c)
        def _():
            for r in (0, 1):
                rows = slice(r * ROWS, (r + 1) * ROWS)
                source = ins[r ^ c]
                if len(outs) == 2:
                    outs[0][rows, :] = source[:, :QUART]
                    outs[1][rows, :] = source[:, QUART:HALF]
                else:
                    outs[0][rows, :] = source[:, HALF:]


def stack_body(ids, ins, outs):
    outs[0][0] = ins[0][...]
    outs[0][1] = ins[1][...]


def pass_body(ids, ins, outs):
    outs[0][...] = ins[0][...]


def stack_half_body(ids, ins, outs):
    outs[0][0] = ins[0][...]
    outs[0][1] = ins[1][...]
    cols = pl.ds(pl.multiple_of((1 - ids[Z_LO]) * QUART, GROUP), QUART)
    outs[1][0] = ins[0][:, cols]
    outs[1][1] = ins[1][:, cols]


def half_body(ids, ins, outs):
    outs[0][0] = cot_columns(ins[0], 1 - ids[CORE])
    outs[0][1] = cot_columns(ins[1], 1 - ids[CORE])


def cot_columns(ref, core):
    return ref[:, pl.ds(pl.multiple_of(core * HALF, GROUP), HALF)]


def add_products(ids, tokens, out, pieces, first):
    fresh = [first, first]
    for ref, n, shard, half in pieces:
        cols = slice(half * QUART, (half + 1) * QUART)
        for t, tok in enumerate(tokens):
            here = slice(t * TOK, (t + 1) * TOK)
            value = dot(tok[:, columns(ids[shard])], ref[n])
            if fresh[half]:
                out[here, cols] = value
            else:
                out[here, cols] += value
        fresh[half] = False


def early_pieces(s1, r1, s2, q2):
    return [(s1, 0, 0, 0), (s1, 1, 4, 0), (r1, 0, 1, 0), (r1, 1, 5, 0)] + [
        (s2, 0, 0, 1), (s2, 1, 1, 1), (q2, 0, 2, 1), (q2, 1, 3, 1)
    ]


def late_pieces(q1, p1, za, zc):
    return [(q1, 0, 2, 0), (q1, 1, 6, 0), (p1, 0, 3, 0), (p1, 1, 7, 0)] + [
        (za, 0, 4, 1), (za, 1, 5, 1), (zc, 0, 6, 1), (zc, 1, 7, 1)
    ]


def value_shard(ids, refs, shard):
    s2, q2, zs, os, zq = refs
    x_slot = shard % 4
    if shard < 4:
        return (s2 if x_slot < 2 else q2)[x_slot % 2]
    if x_slot > 1:
        return zq[x_slot % 2]
    mine, other = zs[x_slot], os[x_slot]
    even = ids[Z_LO] == 0
    return jnp.concatenate([jnp.where(even, mine, other), jnp.where(even, other, mine)], axis=1)


def early_body(ids, ins, outs):
    add_products(ids, ins[:2], outs[0], early_pieces(*ins[2:6]), True)


def late_body(ids, ins, outs):
    raw, cot_own, cot_oth, gain = ins[6:10]
    out, stats = outs
    out[...] = raw[...]
    add_products(ids, ins[:2], out, late_pieces(*ins[2:6]), False)
    lane = lax.broadcasted_iota(jnp.int32, (TOK, GROUP), 1)
    gains = cot_columns(gain, ids[CORE])
    for n, cot in enumerate((cot_columns(cot_own, ids[CORE]), cot_oth[1])):
        here = slice(n * TOK, (n + 1) * TOK)
        part = out[here, :]
        square = jnp.sum(part * part, axis=1, keepdims=True)
        cross = jnp.sum(part * (f32(cot) * gains), axis=1, keepdims=True)
        stats[here, :] = jnp.where(lane == 0, square, jnp.where(lane == 1, cross, 0.0))


def norm_body(ids, ins, outs):
    raw, mine, theirs, cot_own, cot_oth, gain = ins
    gsum = outs[4]
    weight = cot_columns(gain, ids[CORE])
    total = jnp.zeros((8, HALF), F32)
    for n, cot in enumerate((cot_columns(cot_own, ids[CORE]), cot_oth[1])):
        here = slice(n * TOK, (n + 1) * TOK)
        there = slice((1 - n) * TOK, (2 - n) * TOK)
        square = mine[here, 0:1] + theirs[there, 0:1]
        cross = mine[here, 1:2] + theirs[there, 1:2]
        inverse = lax.rsqrt(square * (1.0 / KV) + 1e-06)
        normed = raw[here, :] * inverse
        cotangent = f32(cot)
        outs[n][...] = (normed * weight).astype(BF)
        mean = cross * inverse * (1.0 / KV)
        outs[2 + n][...] = (inverse * (cotangent * weight - normed * mean)).astype(BF)
        total += jnp.sum((cotangent * normed).reshape(TOK // 8, 8, HALF), axis=0)
    gsum[...] = jnp.broadcast_to(jnp.sum(total, axis=0, keepdims=True), (8, HALF))


def value_body(ids, ins, outs):
    acc = outs[2]
    for shard in range(8):
        weight = value_shard(ids, ins[2:7], shard)
        for n in (0, 1):
            here = slice(n * TOK, (n + 1) * TOK)
            value = dot(ins[n][:, columns(ids[shard])], weight)
            if shard == 0:
                acc[here, :] = value
            else:
                acc[here, :] += value
    outs[0][...] = acc[:TOK, :].astype(BF)
    outs[1][...] = acc[TOK:, :].astype(BF)


def back_body(ids, ins, outs):
    g_key, g_val = ins[:2]
    own = len(ins) > 15
    grad = jnp.concatenate([g_key[...], cot_columns(g_val, ids[CORE]) if own else g_val[0]], axis=1)
    where = {}
    for ref, n, shard, half in early_pieces(*ins[2:6]) + late_pieces(*ins[6:10]):
        where[shard, half] = ref[n]
    for shard in range(8):
        parts = [where[shard, 0], where[shard, 1], value_shard(ids, ins[10:15], shard)]
        value = dot(grad, jnp.concatenate(parts, axis=1), NT)
        if own:
            value += f32(ins[15][:, columns(ids[shard])])
        outs[0][:, columns(ids[shard])] = value.astype(BF)
    if own:
        outs[1][...] = jnp.zeros_like(outs[1])


def piece(prod, offset, extra):
    low = prod[pl.ds(pl.multiple_of(offset, 8), 40), :]
    high = prod[pl.ds(pl.multiple_of(offset + ROWS, 8), 40), :]
    return jnp.concatenate([low, high] + extra, axis=0).astype(BF)


def two_rows(total):
    row = lax.broadcasted_iota(jnp.int32, (16, total.shape[1]), 0)
    high = f32(total.astype(BF))
    return jnp.where(row == 0, high, jnp.where(row == 1, total - high, 0.0))


def with_gain(total):
    return jnp.concatenate(
        [total[:80], two_rows(jnp.sum(total[80:], axis=0, keepdims=True))], axis=0
    ).astype(BF)


def codes_body(kind, base, width, grads, ids, ins, outs):
    t_own, t_oth, g_own, g_oth, scale = ins[:5]
    keep, send, prod = outs
    g_own, g_oth = grads(ids, g_own, g_oth)
    extra = [two_rows(ins[5][0:1, base * GROUP : base * GROUP + width])] if len(ins) > 5 else []

    def block_codes(near_half, pair, k):
        sx = pair + (0 if near_half else 2)
        block = ids[9 + sx * 2 + k]
        total = dot(t_own[:, columns(block)], g_own, TN) + dot(t_oth[:, columns(block)], g_oth, TN)
        rows = pl.ds(pl.multiple_of(block * SHARD, SHARD), SHARD)
        factor = scale[rows, base : base + width // GROUP]
        for j in range(width // GROUP):
            cols = slice(j * GROUP, (j + 1) * GROUP)
            prod[:, cols] = total[:, cols] * factor[:, j : j + 1]
        for m in (0, 1):
            z_slot = ids[17 + k * 2 + m]
            for s in range(4):
                value = piece(prod, ids[21 + m] * 160 + ids[23 + s] * 40, extra)
                if kind == "y":
                    (keep if s < 2 else send)[s % 2, sx, z_slot] = value
                else:
                    (keep if near_half else send)[pair, s, z_slot] = value

    for near_half in (False, True):

        @pl.loop(0, 2)
        def _(pair):
            block_codes(near_half, pair, 0)
            block_codes(near_half, pair, 1)


def summed(parts, at, gains):
    total = f32(parts[0][at])
    for part in parts[1:]:
        total += f32(part[at])
    return with_gain(total) if gains else total.astype(BF)


def add2_body(gains, ids, ins, outs):
    keep, first = ins[0].at[1], ins[1].at[1]
    for i in range(4):
        if keep.shape[0] == 4 and len(keep.shape) == 4:
            for j in range(4):
                outs[0][i, j] = summed([keep, first], (i, j), gains)
        else:
            outs[0][i] = summed([keep, first], i, gains)


def add3_body(gains, ids, ins, outs):
    keep, first, second = ins[0].at[0], ins[1].at[0], ins[2]
    for i in range(4):
        for j in range(4):
            outs[i // 2][i % 2, j] = summed([keep, first, second], (i, j), gains)


def merge_body(ids, ins, outs):
    for n, (at, width) in enumerate(((0, QUART), (QUART, QUART), (HALF, HALF))):
        keep, first, second = ins[3 * n].at[0], ins[3 * n + 1].at[0], ins[3 * n + 2]
        rows = 80 if n == 2 else 96
        for s in range(4):
            outs[s][:rows, at : at + width] = summed([keep, first, second], s, n < 2)
            if n == 2:
                outs[s][80:, at : at + width] = jnp.zeros((16, width), BF)


def last_body(ids, ins, outs):
    mine, theirs, total = outs
    total[...] = f32(ins[0][...]) + f32(ins[1][...]) + f32(ins[2][...]) + f32(ins[3][...])
    gain = jnp.broadcast_to(jnp.sum(total[80:, :], axis=0, keepdims=True), (8, KV))
    for out, core in ((mine, ids[CORE]), (theirs, 1 - ids[CORE])):
        out[:40, :] = total[pl.ds(pl.multiple_of(core * 40, 8), 40), :]
        out[40:, :] = gain


def halves_body(ids, ins, outs):
    for c in (0, 1):

        @pl.when(ids[CORE] == c)
        def _():
            outs[0][:, c * HALF : (c + 1) * HALF] = ins[0][...]
            outs[0][:, (1 - c) * HALF : (2 - c) * HALF] = ins[1][...]


def place_body(ids, ins, outs):
    mine, theirs = ins
    for c in (0, 1):

        @pl.when(ids[CORE] == c)
        def _():
            for n in range(4):
                source = mine if n % 2 == c else theirs
                outs[0][:, n * HALF : (n + 1) * HALF] = source[:40, n // 2 * HALF : (n // 2 + 1) * HALF]
            for n in range(2):
                source = mine if n == c else theirs
                outs[1][:, n * HALF : (n + 1) * HALF] = source[40:41, :HALF]


def on_device(tokens, w_codes, w_scale, gain, key_cot, value_cot, grad_scale):
    node, group = lax.axis_index("node"), lax.axis_index("group")
    z_hi, x, core = node // 8, (node // 2) % 4, node % 2
    z_lo, y = group // 4, group % 4
    z = z_hi * 2 + z_lo

    def ring(n):
        a, b = n ^ 1, 3 - n
        first, second = jnp.where(core == 0, a, b), jnp.where(core == 0, b, a)
        return [n, second, first, (n + 2) % 4]

    x_of, y_of, z_of = ring(x), ring(y), ring(z)
    slot_of = lambda places, n: sum(jnp.where(places[s] == n, s, 0) for s in range(4))
    ids = jnp.stack(
        [
            jnp.asarray(v, jnp.int32)
            for v in [(z_hi ^ dz) * 4 + x_of[s] for dz in (0, 1) for s in (0, 2, 1, 3)]
            + [core]
            + [(z_hi ^ k) * 4 + x_of[s] for s in range(4) for k in (0, 1)]
            + [slot_of(z_of, (z_hi ^ k) * 2 + (z_lo ^ m)) for k in (0, 1) for m in (0, 1)]
            + [z_lo, z_lo ^ 1]
            + y_of
        ]
    )
    chain = Chain()

    def run(name, body, arrays, shapes, scratch=(), flops=1000, after=()):
        return chain(name, body, ids, arrays, shapes, scratch, flops, after)

    def codes(kind, base, width, rows, grads, arrays, after=()):
        return run(
            "gradient_codes",
            lambda *a: codes_body(kind, base, width, grads, *a),
            both_t + arrays,
            [((2, 4, 4, rows, width), BF)] * 2,
            [pltpu.VMEM((SHARD, width), F32)],
            flops=SMALL if base == 0 else COVER,
            after=after,
        )

    def add2(keep, first, after=()):
        gains = keep.shape[-2] > 80
        body = lambda *a: add2_body(gains, *a)
        return run("add_two", body, [keep, first], [(keep.shape[1:], BF)], after=after)[0]

    def add3(keep, first, second, after=()):
        gains = keep.shape[-2] > 80
        body = lambda *a: add3_body(gains, *a)
        shape = (2,) + keep.shape[2:]
        return run("add_three", body, [keep, first, second], [(shape, BF)] * 2, after=after)

    def direct(axis, slots):
        return [
            slots[0],
            swap(slots[1], axis, 1),
            swap(slots[2], axis, 0),
            swap(slots[3], axis + "_far"),
        ]

    w_mine, w_send = run("dequantize", dequant_body, [w_codes, w_scale], [((ROWS, KV), BF)] * 2)
    w_came = swap(w_send, "core")
    t_oth = swap(tokens, "core")
    both_t = [tokens, t_oth]
    gain2 = gain.reshape(1, KV)
    factors = 1.0 / jnp.concatenate(
        [
            lax.dynamic_slice_in_dim(grad_scale, core * 4, 4, axis=1),
            lax.dynamic_slice_in_dim(grad_scale, 8 + core * 4, 4, axis=1),
        ],
        axis=1,
    )
    cots = swap(run("halves", half_body, [value_cot, key_cot], [((2, TOK, HALF), BF)])[0], "core")

    def stack(a, b, after):
        return run("stack_shards", stack_body, [a, b], [((2, SHARD, QUART), BF)], after=after)[0]

    join = lambda own, oth: run("join_halves", halves_body, [own, oth], [((TOK, KV), BF)])[0]

    ka, kb = run("assemble", assemble_body, [w_mine, w_came], [((SHARD, QUART), BF)] * 2)
    k_g = swap(ka, "zb")
    k_x = swap(kb, "x", 0)
    k_s2 = stack(kb, k_x, [cots])
    k_q2 = swap(k_s2, "x", 1)
    k_za = swap(k_s2, "zb")
    k_s1 = stack(ka, k_g, [t_oth])
    k_r1 = swap(k_s1, "x", 0)
    k_q1 = swap(k_s1, "x", 1)
    v_cols = lambda ids, own, oth: (cot_columns(own, ids[CORE]), oth[0])
    v_keep, v_send = codes("y", 4, HALF, 80, v_cols, [value_cot, cots, factors])
    v_first = swap(v_send, "y", 0)
    k_q2 = run("pass_shards", pass_body, [k_q2], [((2, SHARD, QUART), BF)])[0]
    k_zc = swap(k_q2, "zb")
    k_p1 = swap(k_r1, "x", 1)
    k_early, k_late = [k_s1, k_r1, k_s2, k_q2], [k_q1, k_p1, k_za, k_zc]
    raw = run(
        "key_projection_early",
        early_body,
        both_t + k_early,
        [((2 * TOK, HALF), F32)],
        flops=3 * SMALL,
        after=[k_za],
    )[0]
    vw = run(
        "assemble", assemble_body, [w_mine, w_came], [((SHARD, HALF), BF)], after=[k_q1]
    )[0]
    v_x = swap(vw, "x", 0)
    raw, stats = run(
        "key_projection_late",
        late_body,
        both_t + k_late + [raw, key_cot, cots, gain2],
        [((2 * TOK, HALF), F32), ((2 * TOK, GROUP), F32)],
        flops=SMALL,
    )
    stats_oth = swap(stats, "core")
    v_s2, v_h2 = run(
        "stack_shards",
        stack_half_body,
        [vw, v_x],
        [((2, SHARD, HALF), BF), ((2, SHARD, QUART), BF)],
    )
    v_q2 = swap(v_s2, "x", 1)
    v_zs = swap(v_h2, "zb")
    k_own, k_oth, g_own, g_oth, gsum = run(
        "key_norm",
        norm_body,
        [raw, stats, stats_oth, key_cot, cots, gain2],
        [((TOK, HALF), BF)] * 4 + [((8, HALF), F32)],
    )
    a_cols = lambda ids, own, oth: (own[:, :QUART], oth[:, :QUART])
    a_keep, a_send = codes("y", 0, QUART, 96, a_cols, [g_own, g_oth, factors, gsum])
    a_first = swap(a_send, "y", 0)
    v_second = swap(add2(v_keep, v_first), "y", 1)
    v_os = swap(v_zs, "za")
    b_cols = lambda ids, own, oth: (own[:, QUART:], oth[:, QUART:])
    b_keep, b_send = codes("x", 2, QUART, 96, b_cols, [g_own, g_oth, factors, gsum], [v_zs, v_q2])
    b_first = swap(b_send, "x", 0)
    v_zq = swap(v_q2, "zb")
    a_second = swap(add2(a_keep, a_first), "y", 1)
    b_second = swap(add2(b_keep, b_first), "x", 1)
    keys = join(k_own, swap(k_oth, "core"))
    v_weights = [v_s2, v_q2, v_zs, v_os, v_zq]
    weights = k_early + k_late + v_weights
    a_keep, a_send = add3(a_keep, a_first, a_second)
    a_first = swap(a_send, "x", 0)
    v_keep, v_send = add3(v_keep, v_first, v_second)
    v_first = swap(v_send, "x", 0)
    b_keep, b_send = add3(b_keep, b_first, b_second)
    b_first = swap(b_send, "y", 0)
    sent = run(
        "token_gradient", back_body, [g_oth, cots] + weights, [((TOK, D), BF)], flops=COVER
    )[0]
    received = swap(sent, "core")
    a_second = swap(add2(a_keep, a_first), "x", 1)
    b_second = swap(add2(b_keep, b_first), "y", 1)
    v_second = swap(add2(v_keep, v_first), "x", 1)
    v_own, v_oth = run(
        "value_projection",
        value_body,
        both_t + v_weights,
        [((TOK, HALF), BF)] * 2,
        [pltpu.VMEM((2 * TOK, HALF), F32)],
        flops=COVER,
    )
    z_slots = run(
        "merge_sums",
        merge_body,
        [a_keep, a_first, a_second, b_keep, b_first, b_second, v_keep, v_first, v_second],
        [((96, KV), BF)] * 4,
    )
    z_parts = direct("z", z_slots)
    grad_tokens, _ = run(
        "token_gradient_sum",
        back_body,
        [g_own, value_cot] + weights + [received],
        [((TOK, D), BF), ((8, GROUP), F32)],
        flops=COVER,
    )
    values = join(v_own, swap(v_oth, "core"))
    mine, theirs = run(
        "last_sum", last_body, z_parts, [((48, KV), F32)] * 2, [pltpu.VMEM((96, KV), F32)]
    )
    theirs = swap(theirs, "core")
    grad_codes, grad_gain = run(
        "place_codes", place_body, [mine, theirs], [((40, 2 * KV), F32), ((1, KV), F32)]
    )
    return (keys, values, grad_tokens, grad_codes, grad_gain.reshape(KV))


def solution(mesh):
    rows = P(("node", "group"), None)
    in_specs = (rows, P("node", None), P("node", None), P(), rows, rows, P())
    out_specs = (rows, rows, rows, rows, P())
    return jax.shard_map(
        on_device, mesh=mesh, in_specs=in_specs, out_specs=out_specs, check_vma=False
    )
```

```python
import jax
import jax.numpy as jnp
from jax import lax
from jax.experimental import pallas as pl
from jax.experimental.pallas import tpu as pltpu
from jax.sharding import PartitionSpec as P

BF = jnp.bfloat16
F32 = jnp.float32
GROUP = 128
AXES = ("node", "group")
TOK = 384
ROWS = 320
SHARD = 640
D = 5120
KV = 1024
HALF = 512
QUART = 256
VMEM_LIMIT = 20 * 2**20
COVER = 10**11
SMALL = 6 * 10**9
EARLY = 2 * 10**9
NT = (((1,), (1,)), ((), ()))
TN = (((0,), (0,)), ((), ()))


def coords(i):
    y, z_lo, core, x, z_hi = i % 4, (i // 4) % 2, (i // 8) % 2, (i // 16) % 4, i // 64
    return z_hi * 2 + z_lo, x, core, y


def flat(z, x, core, y):
    return (((z // 2 * 4 + x) * 2 + core) * 2 + z % 2) * 4 + y


def near(n, which):
    return n ^ 1 if which == 0 else 3 - n


def pairs_of(axis, step):
    out = []
    for i in range(128):
        z, x, core, y = coords(i)
        which = step ^ core
        if axis == "core":
            out.append((i, flat(z, x, 1 - core, y)))
        if axis == "x":
            out.append((i, flat(z, near(x, which), core, y)))
        if axis == "y":
            out.append((i, flat(z, x, core, near(y, which))))
        if axis == "z":
            out.append((i, flat(near(z, which), x, core, y)))
        if axis == "zb":
            out.append((i, flat(3 - z, x, core, y)))
        if axis == "za":
            out.append((i, flat(z ^ 1, x, core, y)))
        if axis == "x_far":
            out.append((i, flat(z, (x + 2) % 4, core, y)))
        if axis == "y_far":
            out.append((i, flat(z, x, core, (y + 2) % 4)))
        if axis == "z_far":
            out.append((i, flat((z + 2) % 4, x, core, y)))
    return out


def swap(v, axis, step=0):
    return lax.ppermute(v, AXES, pairs_of(axis, step))


def dot(a, b, dims=(((1,), (0,)), ((), ()))):
    return lax.dot_general(a, b, dims, preferred_element_type=F32)


def f32(v):
    return v.astype(F32)


def columns(n):
    return pl.ds(pl.multiple_of(n * SHARD, GROUP), SHARD)


class Chain:
    def __init__(self):
        self.last = None

    def __call__(self, name, body, ids, arrays, shapes, scratch, flops, after):
        vm = pl.BlockSpec(memory_space=pltpu.VMEM)
        n_in = len(arrays)
        extra = ([] if self.last is None else [self.last]) + list(after)

        def kernel(*refs):
            body(refs[0], refs[1 : 1 + n_in], refs[1 + n_in + len(extra) :])

        out = pl.pallas_call(
            kernel,
            in_specs=[pl.BlockSpec(memory_space=pltpu.SMEM)]
            + [vm] * n_in
            + [pl.BlockSpec(memory_space=pl.ANY)] * len(extra),
            out_specs=[vm] * len(shapes),
            out_shape=[jax.ShapeDtypeStruct(s, t) for s, t in shapes],
            scratch_shapes=list(scratch),
            compiler_params=pltpu.CompilerParams(vmem_limit_bytes=VMEM_LIMIT),
            cost_estimate=pl.CostEstimate(flops=flops, bytes_accessed=1000, transcendentals=0),
            name=name,
        )(ids, *arrays, *extra)
        self.last = out[-1]
        return out


CORE = 8
Z_LO = 21


def dequant_body(ids, ins, outs):
    codes, scale = ins
    for c in (0, 1):

        @pl.when(ids[CORE] == c)
        def _():
            for n, out in enumerate(outs):
                for j in range(8):
                    b = j // 4 * 8 + (c ^ n) * 4 + j % 4
                    out[:, j * GROUP : (j + 1) * GROUP] = (
                        f32(codes[:, b * GROUP : (b + 1) * GROUP]) * f32(scale[:, b : b + 1])
                    ).astype(BF)


def assemble_body(ids, ins, outs):
    for c in (0, 1):

        @pl.when(ids[CORE] == c)
        def _():
            for r in (0, 1):
                rows = slice(r * ROWS, (r + 1) * ROWS)
                source = ins[r ^ c]
                if len(outs) == 2:
                    outs[0][rows, :] = source[:, :QUART]
                    outs[1][rows, :] = source[:, QUART:HALF]
                else:
                    outs[0][rows, :] = source[:, HALF:]


def stack_body(ids, ins, outs):
    outs[0][0] = ins[0][...]
    outs[0][1] = ins[1][...]


def pass_body(ids, ins, outs):
    outs[0][...] = ins[0][...]


def stack_half_body(ids, ins, outs):
    outs[0][0] = ins[0][...]
    outs[0][1] = ins[1][...]
    cols = pl.ds(pl.multiple_of((1 - ids[Z_LO]) * QUART, GROUP), QUART)
    outs[1][0] = ins[0][:, cols]
    outs[1][1] = ins[1][:, cols]


def half_body(ids, ins, outs):
    outs[0][0] = cot_columns(ins[0], 1 - ids[CORE])
    outs[0][1] = cot_columns(ins[1], 1 - ids[CORE])


def cot_columns(ref, core):
    return ref[:, pl.ds(pl.multiple_of(core * HALF, GROUP), HALF)]


def add_products(ids, tokens, out, pieces, first):
    fresh = [first, first]
    for ref, n, shard, half in pieces:
        cols = slice(half * QUART, (half + 1) * QUART)
        for t, tok in enumerate(tokens):
            here = slice(t * TOK, (t + 1) * TOK)
            value = dot(tok[:, columns(ids[shard])], ref[n])
            if fresh[half]:
                out[here, cols] = value
            else:
                out[here, cols] += value
        fresh[half] = False


def early_pieces(s1, r1, s2, q2):
    return [(s1, 0, 0, 0), (s1, 1, 4, 0), (r1, 0, 1, 0), (r1, 1, 5, 0)] + [
        (s2, 0, 0, 1), (s2, 1, 1, 1), (q2, 0, 2, 1), (q2, 1, 3, 1)
    ]


def late_pieces(q1, p1, za, zc):
    return [(q1, 0, 2, 0), (q1, 1, 6, 0), (p1, 0, 3, 0), (p1, 1, 7, 0)] + [
        (za, 0, 4, 1), (za, 1, 5, 1), (zc, 0, 6, 1), (zc, 1, 7, 1)
    ]


def value_shard(ids, refs, shard):
    s2, q2, zs, os, zq = refs
    x_slot = shard % 4
    if shard < 4:
        return (s2 if x_slot < 2 else q2)[x_slot % 2]
    if x_slot > 1:
        return zq[x_slot % 2]
    mine, other = zs[x_slot], os[x_slot]
    even = ids[Z_LO] == 0
    return jnp.concatenate([jnp.where(even, mine, other), jnp.where(even, other, mine)], axis=1)


def early_body(ids, ins, outs):
    add_products(ids, ins[:2], outs[0], early_pieces(*ins[2:6]), True)


def late_body(ids, ins, outs):
    raw, cot_own, cot_oth, gain = ins[6:10]
    out, stats = outs
    out[...] = raw[...]
    add_products(ids, ins[:2], out, late_pieces(*ins[2:6]), False)
    lane = lax.broadcasted_iota(jnp.int32, (TOK, GROUP), 1)
    gains = cot_columns(gain, ids[CORE])
    for n, cot in enumerate((cot_columns(cot_own, ids[CORE]), cot_oth[1])):
        here = slice(n * TOK, (n + 1) * TOK)
        part = out[here, :]
        square = jnp.sum(part * part, axis=1, keepdims=True)
        cross = jnp.sum(part * (f32(cot) * gains), axis=1, keepdims=True)
        stats[here, :] = jnp.where(lane == 0, square, jnp.where(lane == 1, cross, 0.0))


def norm_body(ids, ins, outs):
    raw, mine, theirs, cot_own, cot_oth, gain = ins
    gsum = outs[4]
    weight = cot_columns(gain, ids[CORE])
    total = jnp.zeros((8, HALF), F32)
    for n, cot in enumerate((cot_columns(cot_own, ids[CORE]), cot_oth[1])):
        here = slice(n * TOK, (n + 1) * TOK)
        there = slice((1 - n) * TOK, (2 - n) * TOK)
        square = mine[here, 0:1] + theirs[there, 0:1]
        cross = mine[here, 1:2] + theirs[there, 1:2]
        inverse = lax.rsqrt(square * (1.0 / KV) + 1e-06)
        normed = raw[here, :] * inverse
        cotangent = f32(cot)
        outs[n][...] = (normed * weight).astype(BF)
        mean = cross * inverse * (1.0 / KV)
        outs[2 + n][...] = (inverse * (cotangent * weight - normed * mean)).astype(BF)
        total += jnp.sum((cotangent * normed).reshape(TOK // 8, 8, HALF), axis=0)
    gsum[...] = jnp.broadcast_to(jnp.sum(total, axis=0, keepdims=True), (8, HALF))


def value_body(part, ids, ins, outs):
    refs = (*ins[2:4], None, None, None) if part == 0 else (None, None, *ins[2:5])
    total = outs[2 * part]
    for shard in range(4 * part, 4 * part + 4):
        weight = value_shard(ids, refs, shard)
        for n in (0, 1):
            here = slice(n * TOK, (n + 1) * TOK)
            value = dot(ins[n][:, columns(ids[shard])], weight)
            if shard == 0:
                total[here, :] = value
            elif shard == 4:
                total[here, :] = ins[5][here, :] + value
            else:
                total[here, :] += value
    if part == 1:
        outs[0][...] = total[:TOK, :].astype(BF)
        outs[1][...] = total[TOK:, :].astype(BF)


def back_body(part, ids, ins, outs):
    g_key, g_val = ins[:2]
    own = part == 2
    refs = [(*ins[10:12], None, None, None), (None, None, *ins[10:13]), ins[10:15]][part]
    grad = jnp.concatenate([g_key[...], cot_columns(g_val, ids[CORE]) if own else g_val[0]], axis=1)
    where = {}
    for ref, n, shard, half in early_pieces(*ins[2:6]) + late_pieces(*ins[6:10]):
        where[shard, half] = (ref, n)
    for shard in range(8) if own else range(4 * part, 4 * part + 4):
        parts = [where[shard, h][0][where[shard, h][1]] for h in (0, 1)]
        parts.append(value_shard(ids, refs, shard))
        value = dot(grad, jnp.concatenate(parts, axis=1), NT)
        cols = columns(lax.rem(ids[shard], 4) if part == 0 else ids[shard])
        if own:
            value += f32(ins[15][:, cols])
        outs[0][:, cols] = value.astype(BF)
    if part == 1:
        near_cols = pl.ds(pl.multiple_of((ids[0] // 4) * (D // 2), GROUP), D // 2)
        outs[0][:, near_cols] = ins[13][...]
    if own:
        outs[1][...] = jnp.zeros_like(outs[1])


def piece(prod, offset, extra):
    low = prod[pl.ds(pl.multiple_of(offset, 8), 40), :]
    high = prod[pl.ds(pl.multiple_of(offset + ROWS, 8), 40), :]
    return jnp.concatenate([low, high] + extra, axis=0).astype(BF)


def two_rows(total):
    row = lax.broadcasted_iota(jnp.int32, (16, total.shape[1]), 0)
    high = f32(total.astype(BF))
    return jnp.where(row == 0, high, jnp.where(row == 1, total - high, 0.0))


def with_gain(total):
    return jnp.concatenate(
        [total[:80], two_rows(jnp.sum(total[80:], axis=0, keepdims=True))], axis=0
    ).astype(BF)


def codes_body(kind, base, width, grads, ids, ins, outs):
    t_own, t_oth, g_own, g_oth, scale = ins[:5]
    keep, send, prod = outs
    g_own, g_oth = grads(ids, g_own, g_oth)
    extra = [two_rows(ins[5][0:1, base * GROUP : base * GROUP + width])] if len(ins) > 5 else []

    def block_codes(near_half, pair, k):
        sx = pair + (0 if near_half else 2)
        block = ids[9 + sx * 2 + k]
        total = dot(t_own[:, columns(block)], g_own, TN) + dot(t_oth[:, columns(block)], g_oth, TN)
        rows = pl.ds(pl.multiple_of(block * SHARD, SHARD), SHARD)
        factor = scale[rows, base : base + width // GROUP]
        for j in range(width // GROUP):
            cols = slice(j * GROUP, (j + 1) * GROUP)
            prod[:, cols] = total[:, cols] * factor[:, j : j + 1]
        for m in (0, 1):
            z_slot = ids[17 + k * 2 + m]
            for s in range(4):
                value = piece(prod, ids[21 + m] * 160 + ids[23 + s] * 40, extra)
                if kind == "y":
                    (keep if s < 2 else send)[s % 2, sx, z_slot] = value
                else:
                    (keep if near_half else send)[pair, s, z_slot] = value

    for near_half in (False, True):

        @pl.loop(0, 2)
        def _(pair):
            block_codes(near_half, pair, 0)
            block_codes(near_half, pair, 1)


def summed(parts, at, gains):
    total = f32(parts[0][at])
    for part in parts[1:]:
        total += f32(part[at])
    return with_gain(total) if gains else total.astype(BF)


def add2_body(gains, ids, ins, outs):
    keep, first = ins[0].at[1], ins[1].at[1]
    for i in range(4):
        if keep.shape[0] == 4 and len(keep.shape) == 4:
            for j in range(4):
                outs[0][i, j] = summed([keep, first], (i, j), gains)
        else:
            outs[0][i] = summed([keep, first], i, gains)


def add3_body(gains, ids, ins, outs):
    keep, first, second = ins[0].at[0], ins[1].at[0], ins[2]
    for i in range(4):
        for j in range(4):
            outs[i // 2][i % 2, j] = summed([keep, first, second], (i, j), gains)


def merge_body(ids, ins, outs):
    for n, (at, width) in enumerate(((0, QUART), (QUART, QUART), (HALF, HALF))):
        keep, first, second = ins[3 * n].at[0], ins[3 * n + 1].at[0], ins[3 * n + 2]
        rows = 80 if n == 2 else 96
        for s in range(4):
            outs[s][:rows, at : at + width] = summed([keep, first, second], s, n < 2)
            if n == 2:
                outs[s][80:, at : at + width] = jnp.zeros((16, width), BF)


def last_body(ids, ins, outs):
    mine, theirs, total = outs
    total[...] = f32(ins[0][...]) + f32(ins[1][...]) + f32(ins[2][...]) + f32(ins[3][...])
    gain = jnp.broadcast_to(jnp.sum(total[80:, :], axis=0, keepdims=True), (8, KV))
    for out, core in ((mine, ids[CORE]), (theirs, 1 - ids[CORE])):
        out[:40, :] = total[pl.ds(pl.multiple_of(core * 40, 8), 40), :]
        out[40:, :] = gain


def halves_body(ids, ins, outs):
    for c in (0, 1):

        @pl.when(ids[CORE] == c)
        def _():
            outs[0][:, c * HALF : (c + 1) * HALF] = ins[0][...]
            outs[0][:, (1 - c) * HALF : (2 - c) * HALF] = ins[1][...]


def place_body(ids, ins, outs):
    mine, theirs = ins
    for c in (0, 1):

        @pl.when(ids[CORE] == c)
        def _():
            for n in range(4):
                source = mine if n % 2 == c else theirs
                outs[0][:, n * HALF : (n + 1) * HALF] = source[:40, n // 2 * HALF : (n // 2 + 1) * HALF]
            for n in range(2):
                source = mine if n == c else theirs
                outs[1][:, n * HALF : (n + 1) * HALF] = source[40:41, :HALF]


def on_device(tokens, w_codes, w_scale, gain, key_cot, value_cot, grad_scale):
    node, group = lax.axis_index("node"), lax.axis_index("group")
    z_hi, x, core = node // 8, (node // 2) % 4, node % 2
    z_lo, y = group // 4, group % 4
    z = z_hi * 2 + z_lo

    def ring(n):
        a, b = n ^ 1, 3 - n
        first, second = jnp.where(core == 0, a, b), jnp.where(core == 0, b, a)
        return [n, second, first, (n + 2) % 4]

    x_of, y_of, z_of = ring(x), ring(y), ring(z)
    slot_of = lambda places, n: sum(jnp.where(places[s] == n, s, 0) for s in range(4))
    ids = jnp.stack(
        [
            jnp.asarray(v, jnp.int32)
            for v in [(z_hi ^ dz) * 4 + x_of[s] for dz in (0, 1) for s in (0, 2, 1, 3)]
            + [core]
            + [(z_hi ^ k) * 4 + x_of[s] for s in range(4) for k in (0, 1)]
            + [slot_of(z_of, (z_hi ^ k) * 2 + (z_lo ^ m)) for k in (0, 1) for m in (0, 1)]
            + [z_lo, z_lo ^ 1]
            + y_of
        ]
    )
    chain = Chain()

    def run(name, body, arrays, shapes, scratch=(), flops=1000, after=()):
        return chain(name, body, ids, arrays, shapes, scratch, flops, after)

    def codes(kind, base, width, rows, grads, arrays, after=()):
        return run(
            "gradient_codes",
            lambda *a: codes_body(kind, base, width, grads, *a),
            both_t + arrays,
            [((2, 4, 4, rows, width), BF)] * 2,
            [pltpu.VMEM((SHARD, width), F32)],
            flops=SMALL if base == 0 else COVER,
            after=after,
        )

    def add2(keep, first, after=()):
        gains = keep.shape[-2] > 80
        body = lambda *a: add2_body(gains, *a)
        return run("add_two", body, [keep, first], [(keep.shape[1:], BF)], after=after)[0]

    def add3(keep, first, second, after=()):
        gains = keep.shape[-2] > 80
        body = lambda *a: add3_body(gains, *a)
        shape = (2,) + keep.shape[2:]
        return run("add_three", body, [keep, first, second], [(shape, BF)] * 2, after=after)

    def direct(axis, slots):
        return [
            slots[0],
            swap(slots[1], axis, 1),
            swap(slots[2], axis, 0),
            swap(slots[3], axis + "_far"),
        ]

    w_mine, w_send = run("dequantize", dequant_body, [w_codes, w_scale], [((ROWS, KV), BF)] * 2)
    w_came = swap(w_send, "core")
    t_oth = swap(tokens, "core")
    both_t = [tokens, t_oth]
    gain2 = gain.reshape(1, KV)
    factors = 1.0 / jnp.concatenate(
        [
            lax.dynamic_slice_in_dim(grad_scale, core * 4, 4, axis=1),
            lax.dynamic_slice_in_dim(grad_scale, 8 + core * 4, 4, axis=1),
        ],
        axis=1,
    )
    cots = swap(run("halves", half_body, [value_cot, key_cot], [((2, TOK, HALF), BF)])[0], "core")

    def stack(a, b, after):
        return run("stack_shards", stack_body, [a, b], [((2, SHARD, QUART), BF)], after=after)[0]

    join = lambda own, oth: run("join_halves", halves_body, [own, oth], [((TOK, KV), BF)])[0]

    ka, kb = run("assemble", assemble_body, [w_mine, w_came], [((SHARD, QUART), BF)] * 2)
    k_g = swap(ka, "zb")
    k_x = swap(kb, "x", 0)
    k_s2 = stack(kb, k_x, [cots])
    k_q2 = swap(k_s2, "x", 1)
    k_za = swap(k_s2, "zb")
    k_s1 = stack(ka, k_g, [t_oth])
    k_r1 = swap(k_s1, "x", 0)
    k_q1 = swap(k_s1, "x", 1)
    v_cols = lambda ids, own, oth: (cot_columns(own, ids[CORE]), oth[0])
    v_keep, v_send = codes("y", 4, HALF, 80, v_cols, [value_cot, cots, factors])
    v_first = swap(v_send, "y", 0)
    k_q2 = run("pass_shards", pass_body, [k_q2], [((2, SHARD, QUART), BF)])[0]
    k_zc = swap(k_q2, "zb")
    k_p1 = swap(k_r1, "x", 1)
    k_early, k_late = [k_s1, k_r1, k_s2, k_q2], [k_q1, k_p1, k_za, k_zc]
    raw = run(
        "key_projection_early",
        early_body,
        both_t + k_early,
        [((2 * TOK, HALF), F32)],
        flops=3 * SMALL,
        after=[k_za],
    )[0]
    vw = run(
        "assemble", assemble_body, [w_mine, w_came], [((SHARD, HALF), BF)], after=[k_q1]
    )[0]
    v_x = swap(vw, "x", 0)
    raw, stats = run(
        "key_projection_late",
        late_body,
        both_t + k_late + [raw, key_cot, cots, gain2],
        [((2 * TOK, HALF), F32), ((2 * TOK, GROUP), F32)],
        flops=SMALL,
    )
    stats_oth = swap(stats, "core")
    v_s2, v_h2 = run(
        "stack_shards",
        stack_half_body,
        [vw, v_x],
        [((2, SHARD, HALF), BF), ((2, SHARD, QUART), BF)],
    )
    v_q2 = swap(v_s2, "x", 1)
    v_zs = swap(v_h2, "zb")
    k_own, k_oth, g_own, g_oth, gsum = run(
        "key_norm",
        norm_body,
        [raw, stats, stats_oth, key_cot, cots, gain2],
        [((TOK, HALF), BF)] * 4 + [((8, HALF), F32)],
    )
    a_cols = lambda ids, own, oth: (own[:, :QUART], oth[:, :QUART])
    a_keep, a_send = codes("y", 0, QUART, 96, a_cols, [g_own, g_oth, factors, gsum])
    a_first = swap(a_send, "y", 0)
    v_second = swap(add2(v_keep, v_first), "y", 1)
    v_os = swap(v_zs, "za")
    b_cols = lambda ids, own, oth: (own[:, QUART:], oth[:, QUART:])
    b_keep, b_send = codes("x", 2, QUART, 96, b_cols, [g_own, g_oth, factors, gsum], [v_zs, v_q2])
    b_first = swap(b_send, "x", 0)
    v_zq = swap(v_q2, "zb")
    a_second = swap(add2(a_keep, a_first), "y", 1)
    v_weights = [v_s2, v_q2, v_zs, v_os, v_zq]
    k_weights = k_early + k_late
    sent_near = run(
        "token_gradient",
        lambda *a: back_body(0, *a),
        [g_oth, cots] + k_weights + v_weights[:2],
        [((TOK, D // 2), BF)],
        flops=EARLY,
    )[0]
    v_part = run(
        "value_projection",
        lambda *a: value_body(0, *a),
        both_t + v_weights[:2],
        [((2 * TOK, HALF), F32)],
        flops=EARLY,
    )[0]
    b_second = swap(add2(b_keep, b_first), "x", 1)
    keys = join(k_own, swap(k_oth, "core"))
    a_keep, a_send = add3(a_keep, a_first, a_second)
    a_first = swap(a_send, "x", 0)
    v_keep, v_send = add3(v_keep, v_first, v_second)
    v_first = swap(v_send, "x", 0)
    b_keep, b_send = add3(b_keep, b_first, b_second)
    b_first = swap(b_send, "y", 0)
    sent = run(
        "token_gradient",
        lambda *a: back_body(1, *a),
        [g_oth, cots] + k_weights + v_weights[2:] + [sent_near],
        [((TOK, D), BF)],
        flops=COVER,
    )[0]
    received = swap(sent, "core")
    a_second = swap(add2(a_keep, a_first), "x", 1)
    b_second = swap(add2(b_keep, b_first), "y", 1)
    v_second = swap(add2(v_keep, v_first), "x", 1)
    v_own, v_oth = run(
        "value_projection",
        lambda *a: value_body(1, *a),
        both_t + v_weights[2:] + [v_part],
        [((TOK, HALF), BF)] * 2,
        [pltpu.VMEM((2 * TOK, HALF), F32)],
        flops=COVER,
    )
    z_slots = run(
        "merge_sums",
        merge_body,
        [a_keep, a_first, a_second, b_keep, b_first, b_second, v_keep, v_first, v_second],
        [((96, KV), BF)] * 4,
    )
    z_parts = direct("z", z_slots)
    grad_tokens, _ = run(
        "token_gradient_sum",
        lambda *a: back_body(2, *a),
        [g_own, value_cot] + k_weights + v_weights + [received],
        [((TOK, D), BF), ((8, GROUP), F32)],
        flops=COVER,
    )
    values = join(v_own, swap(v_oth, "core"))
    mine, theirs = run(
        "last_sum", last_body, z_parts, [((48, KV), F32)] * 2, [pltpu.VMEM((96, KV), F32)]
    )
    theirs = swap(theirs, "core")
    grad_codes, grad_gain = run(
        "place_codes", place_body, [mine, theirs], [((40, 2 * KV), F32), ((1, KV), F32)]
    )
    return (keys, values, grad_tokens, grad_codes, grad_gain.reshape(KV))


def solution(mesh):
    rows = P(("node", "group"), None)
    in_specs = (rows, P("node", None), P("node", None), P(), rows, rows, P())
    out_specs = (rows, rows, rows, rows, P())
    return jax.shard_map(
        on_device, mesh=mesh, in_specs=in_specs, out_specs=out_specs, check_vma=False
    )
```

```python
import jax
import jax.numpy as jnp
from jax import lax
from jax.experimental import pallas as pl
from jax.experimental.pallas import tpu as pltpu
from jax.sharding import PartitionSpec as P

BF = jnp.bfloat16
F32 = jnp.float32
GROUP = 128
AXES = ("node", "group")
TOK = 384
ROWS = 320
SHARD = 640
D = 5120
KV = 1024
HALF = 512
QUART = 256
VMEM_LIMIT = 20 * 2**20
COVER = 10**11
SMALL = 6 * 10**9
EARLY = 2 * 10**9
NT = (((1,), (1,)), ((), ()))
TN = (((0,), (0,)), ((), ()))


def coords(i):
    y, z_lo, core, x, z_hi = i % 4, (i // 4) % 2, (i // 8) % 2, (i // 16) % 4, i // 64
    return z_hi * 2 + z_lo, x, core, y


def flat(z, x, core, y):
    return (((z // 2 * 4 + x) * 2 + core) * 2 + z % 2) * 4 + y


def near(n, which):
    return n ^ 1 if which == 0 else 3 - n


def pairs_of(axis, step):
    out = []
    for i in range(128):
        z, x, core, y = coords(i)
        which = step ^ core
        if axis == "core":
            out.append((i, flat(z, x, 1 - core, y)))
        if axis == "x":
            out.append((i, flat(z, near(x, which), core, y)))
        if axis == "y":
            out.append((i, flat(z, x, core, near(y, which))))
        if axis == "z":
            out.append((i, flat(near(z, which), x, core, y)))
        if axis == "zb":
            out.append((i, flat(3 - z, x, core, y)))
        if axis == "za":
            out.append((i, flat(z ^ 1, x, core, y)))
        if axis == "x_far":
            out.append((i, flat(z, (x + 2) % 4, core, y)))
        if axis == "y_far":
            out.append((i, flat(z, x, core, (y + 2) % 4)))
        if axis == "z_far":
            out.append((i, flat((z + 2) % 4, x, core, y)))
    return out


def swap(v, axis, step=0):
    return lax.ppermute(v, AXES, pairs_of(axis, step))


def dot(a, b, dims=(((1,), (0,)), ((), ()))):
    return lax.dot_general(a, b, dims, preferred_element_type=F32)


def f32(v):
    return v.astype(F32)


def columns(n):
    return pl.ds(pl.multiple_of(n * SHARD, GROUP), SHARD)


class Chain:
    def __init__(self):
        self.last = None

    def __call__(self, name, body, ids, arrays, shapes, scratch, flops, after):
        vm = pl.BlockSpec(memory_space=pltpu.VMEM)
        n_in = len(arrays)
        extra = ([] if self.last is None else [self.last]) + list(after)

        def kernel(*refs):
            body(refs[0], refs[1 : 1 + n_in], refs[1 + n_in + len(extra) :])

        out = pl.pallas_call(
            kernel,
            in_specs=[pl.BlockSpec(memory_space=pltpu.SMEM)]
            + [vm] * n_in
            + [pl.BlockSpec(memory_space=pl.ANY)] * len(extra),
            out_specs=[vm] * len(shapes),
            out_shape=[jax.ShapeDtypeStruct(s, t) for s, t in shapes],
            scratch_shapes=list(scratch),
            compiler_params=pltpu.CompilerParams(vmem_limit_bytes=VMEM_LIMIT),
            cost_estimate=pl.CostEstimate(flops=flops, bytes_accessed=1000, transcendentals=0),
            name=name,
        )(ids, *arrays, *extra)
        self.last = out[-1]
        return out


CORE = 8
Z_LO = 21


def dequant_body(ids, ins, outs):
    codes, scale = ins
    for c in (0, 1):

        @pl.when(ids[CORE] == c)
        def _():
            for n, out in enumerate(outs):
                for j in range(8):
                    b = j // 4 * 8 + (c ^ n) * 4 + j % 4
                    out[:, j * GROUP : (j + 1) * GROUP] = (
                        f32(codes[:, b * GROUP : (b + 1) * GROUP]) * f32(scale[:, b : b + 1])
                    ).astype(BF)


def assemble_body(ids, ins, outs):
    for c in (0, 1):

        @pl.when(ids[CORE] == c)
        def _():
            for r in (0, 1):
                rows = slice(r * ROWS, (r + 1) * ROWS)
                source = ins[r ^ c]
                if len(outs) == 2:
                    outs[0][rows, :] = source[:, :QUART]
                    outs[1][rows, :] = source[:, QUART:HALF]
                else:
                    outs[0][rows, :] = source[:, HALF:]


def stack_body(ids, ins, outs):
    outs[0][0] = ins[0][...]
    outs[0][1] = ins[1][...]


def pass_body(ids, ins, outs):
    outs[0][...] = ins[0][...]


def stack_half_body(ids, ins, outs):
    outs[0][0] = ins[0][...]
    outs[0][1] = ins[1][...]
    cols = pl.ds(pl.multiple_of((1 - ids[Z_LO]) * QUART, GROUP), QUART)
    outs[1][0] = ins[0][:, cols]
    outs[1][1] = ins[1][:, cols]


def half_body(ids, ins, outs):
    outs[0][0] = cot_columns(ins[0], 1 - ids[CORE])
    outs[0][1] = cot_columns(ins[1], 1 - ids[CORE])


def cot_columns(ref, core):
    return ref[:, pl.ds(pl.multiple_of(core * HALF, GROUP), HALF)]


def add_products(ids, tokens, out, pieces, first):
    fresh = [first, first]
    for ref, n, shard, half in pieces:
        cols = slice(half * QUART, (half + 1) * QUART)
        for t, tok in enumerate(tokens):
            here = slice(t * TOK, (t + 1) * TOK)
            value = dot(tok[:, columns(ids[shard])], ref[n])
            if fresh[half]:
                out[here, cols] = value
            else:
                out[here, cols] += value
        fresh[half] = False


def early_pieces(s1, r1, s2, q2):
    return [(s1, 0, 0, 0), (s1, 1, 4, 0), (r1, 0, 1, 0), (r1, 1, 5, 0)] + [
        (s2, 0, 0, 1), (s2, 1, 1, 1), (q2, 0, 2, 1), (q2, 1, 3, 1)
    ]


def late_pieces(q1, p1, za, zc):
    return [(q1, 0, 2, 0), (q1, 1, 6, 0), (p1, 0, 3, 0), (p1, 1, 7, 0)] + [
        (za, 0, 4, 1), (za, 1, 5, 1), (zc, 0, 6, 1), (zc, 1, 7, 1)
    ]


def value_shard(ids, refs, shard):
    s2, q2, zs, os, zq = refs
    x_slot = shard % 4
    if shard < 4:
        return (s2 if x_slot < 2 else q2)[x_slot % 2]
    if x_slot > 1:
        return zq[x_slot % 2]
    mine, other = zs[x_slot], os[x_slot]
    even = ids[Z_LO] == 0
    return jnp.concatenate([jnp.where(even, mine, other), jnp.where(even, other, mine)], axis=1)


def early_body(ids, ins, outs):
    add_products(ids, ins[:2], outs[0], early_pieces(*ins[2:6]), True)


def late_body(ids, ins, outs):
    raw, cot_own, cot_oth, gain = ins[6:10]
    out, stats = outs
    out[...] = raw[...]
    add_products(ids, ins[:2], out, late_pieces(*ins[2:6]), False)
    lane = lax.broadcasted_iota(jnp.int32, (TOK, GROUP), 1)
    gains = cot_columns(gain, ids[CORE])
    for n, cot in enumerate((cot_columns(cot_own, ids[CORE]), cot_oth[1])):
        here = slice(n * TOK, (n + 1) * TOK)
        part = out[here, :]
        square = jnp.sum(part * part, axis=1, keepdims=True)
        cross = jnp.sum(part * (f32(cot) * gains), axis=1, keepdims=True)
        stats[here, :] = jnp.where(lane == 0, square, jnp.where(lane == 1, cross, 0.0))


def norm_body(ids, ins, outs):
    raw, mine, theirs, cot_own, cot_oth, gain = ins
    gsum = outs[4]
    weight = cot_columns(gain, ids[CORE])
    total = jnp.zeros((8, HALF), F32)
    for n, cot in enumerate((cot_columns(cot_own, ids[CORE]), cot_oth[1])):
        here = slice(n * TOK, (n + 1) * TOK)
        there = slice((1 - n) * TOK, (2 - n) * TOK)
        square = mine[here, 0:1] + theirs[there, 0:1]
        cross = mine[here, 1:2] + theirs[there, 1:2]
        inverse = lax.rsqrt(square * (1.0 / KV) + 1e-06)
        normed = raw[here, :] * inverse
        cotangent = f32(cot)
        outs[n][...] = (normed * weight).astype(BF)
        mean = cross * inverse * (1.0 / KV)
        outs[2 + n][...] = (inverse * (cotangent * weight - normed * mean)).astype(BF)
        total += jnp.sum((cotangent * normed).reshape(TOK // 8, 8, HALF), axis=0)
    gsum[...] = jnp.broadcast_to(jnp.sum(total, axis=0, keepdims=True), (8, HALF))


def value_body(part, ids, ins, outs):
    refs = (*ins[2:4], None, None, None) if part == 0 else (None, None, *ins[2:5])
    total = outs[2 * part]
    for shard in range(4 * part, 4 * part + 4):
        weight = value_shard(ids, refs, shard)
        for n in (0, 1):
            here = slice(n * TOK, (n + 1) * TOK)
            value = dot(ins[n][:, columns(ids[shard])], weight)
            if shard == 0:
                total[here, :] = value
            elif shard == 4:
                total[here, :] = ins[5][here, :] + value
            else:
                total[here, :] += value
    if part == 1:
        outs[0][...] = total[:TOK, :].astype(BF)
        outs[1][...] = total[TOK:, :].astype(BF)


def back_body(part, ids, ins, outs):
    g_key, g_val = ins[:2]
    own = part == 2
    refs = [(*ins[10:12], None, None, None), (None, None, *ins[10:13]), ins[10:15]][part]
    grad = jnp.concatenate([g_key[...], cot_columns(g_val, ids[CORE]) if own else g_val[0]], axis=1)
    where = {}
    for ref, n, shard, half in early_pieces(*ins[2:6]) + late_pieces(*ins[6:10]):
        where[shard, half] = (ref, n)
    for shard in range(8) if own else range(4 * part, 4 * part + 4):
        parts = [where[shard, h][0][where[shard, h][1]] for h in (0, 1)]
        parts.append(value_shard(ids, refs, shard))
        value = dot(grad, jnp.concatenate(parts, axis=1), NT)
        cols = columns(lax.rem(ids[shard], 4) if part == 0 else ids[shard])
        if own:
            value += f32(ins[15][:, cols])
        outs[0][:, cols] = value.astype(BF)
    if part == 1:
        near_cols = pl.ds(pl.multiple_of((ids[0] // 4) * (D // 2), GROUP), D // 2)
        outs[0][:, near_cols] = ins[13][...]
    if own:
        outs[1][...] = jnp.zeros_like(outs[1])


def piece(prod, offset, extra):
    low = prod[pl.ds(pl.multiple_of(offset, 8), 40), :]
    high = prod[pl.ds(pl.multiple_of(offset + ROWS, 8), 40), :]
    return jnp.concatenate([low, high] + extra, axis=0).astype(BF)


def two_rows(total):
    row = lax.broadcasted_iota(jnp.int32, (16, total.shape[1]), 0)
    high = f32(total.astype(BF))
    return jnp.where(row == 0, high, jnp.where(row == 1, total - high, 0.0))


def with_gain(total):
    return jnp.concatenate(
        [total[:80], two_rows(jnp.sum(total[80:], axis=0, keepdims=True))], axis=0
    ).astype(BF)


def codes_body(kind, base, width, grads, ids, ins, outs):
    t_own, t_oth, g_own, g_oth, scale = ins[:5]
    keep, send, prod = outs
    g_own, g_oth = grads(ids, g_own, g_oth)
    extra = [two_rows(ins[5][0:1, base * GROUP : base * GROUP + width])] if len(ins) > 5 else []

    def block_codes(near_half, pair, k):
        sx = pair + (0 if near_half else 2)
        block = ids[9 + sx * 2 + k]
        total = dot(t_own[:, columns(block)], g_own, TN) + dot(t_oth[:, columns(block)], g_oth, TN)
        rows = pl.ds(pl.multiple_of(block * SHARD, SHARD), SHARD)
        factor = scale[rows, base : base + width // GROUP]
        for j in range(width // GROUP):
            cols = slice(j * GROUP, (j + 1) * GROUP)
            prod[:, cols] = total[:, cols] * factor[:, j : j + 1]
        for m in (0, 1):
            z_slot = ids[17 + k * 2 + m]
            for s in range(4):
                value = piece(prod, ids[21 + m] * 160 + ids[23 + s] * 40, extra)
                if kind == "y":
                    (keep if s < 2 else send)[s % 2, sx, z_slot] = value
                else:
                    (keep if near_half else send)[pair, s, z_slot] = value

    for near_half in (False, True):

        @pl.loop(0, 2)
        def _(pair):
            block_codes(near_half, pair, 0)
            block_codes(near_half, pair, 1)


def summed(parts, at, gains):
    total = f32(parts[0][at])
    for part in parts[1:]:
        total += f32(part[at])
    return with_gain(total) if gains else total.astype(BF)


def add2_body(gains, ids, ins, outs):
    keep, first = ins[0].at[1], ins[1].at[1]
    for i in range(4):
        if keep.shape[0] == 4 and len(keep.shape) == 4:
            for j in range(4):
                outs[0][i, j] = summed([keep, first], (i, j), gains)
        else:
            outs[0][i] = summed([keep, first], i, gains)


def add3_body(gains, ids, ins, outs):
    keep, first, second = ins[0].at[0], ins[1].at[0], ins[2]
    for i in range(4):
        for j in range(4):
            outs[i // 2][i % 2, j] = summed([keep, first, second], (i, j), gains)


def merge_body(ids, ins, outs):
    for n, (at, width) in enumerate(((0, QUART), (QUART, QUART), (HALF, HALF))):
        keep, first, second = ins[3 * n].at[0], ins[3 * n + 1].at[0], ins[3 * n + 2]
        rows = 80 if n == 2 else 96
        for s in range(4):
            outs[s][:rows, at : at + width] = summed([keep, first, second], s, n < 2)
            if n == 2:
                outs[s][80:, at : at + width] = jnp.zeros((16, width), BF)


def last_body(ids, ins, outs):
    mine, theirs, total = outs
    total[...] = f32(ins[0][...]) + f32(ins[1][...]) + f32(ins[2][...]) + f32(ins[3][...])
    gain = jnp.broadcast_to(jnp.sum(total[80:, :], axis=0, keepdims=True), (8, KV))
    for out, core in ((mine, ids[CORE]), (theirs, 1 - ids[CORE])):
        out[:40, :] = total[pl.ds(pl.multiple_of(core * 40, 8), 40), :]
        out[40:, :] = gain


def halves_body(ids, ins, outs):
    for c in (0, 1):

        @pl.when(ids[CORE] == c)
        def _():
            outs[0][:, c * HALF : (c + 1) * HALF] = ins[0][...]
            outs[0][:, (1 - c) * HALF : (2 - c) * HALF] = ins[1][...]


def place_body(ids, ins, outs):
    mine, theirs = ins
    for c in (0, 1):

        @pl.when(ids[CORE] == c)
        def _():
            for n in range(4):
                source = mine if n % 2 == c else theirs
                outs[0][:, n * HALF : (n + 1) * HALF] = source[:40, n // 2 * HALF : (n // 2 + 1) * HALF]
            for n in range(2):
                source = mine if n == c else theirs
                outs[1][:, n * HALF : (n + 1) * HALF] = source[40:41, :HALF]


def on_device(tokens, w_codes, w_scale, gain, key_cot, value_cot, grad_scale):
    node, group = lax.axis_index("node"), lax.axis_index("group")
    z_hi, x, core = node // 8, (node // 2) % 4, node % 2
    z_lo, y = group // 4, group % 4
    z = z_hi * 2 + z_lo

    def ring(n):
        a, b = n ^ 1, 3 - n
        first, second = jnp.where(core == 0, a, b), jnp.where(core == 0, b, a)
        return [n, second, first, (n + 2) % 4]

    x_of, y_of, z_of = ring(x), ring(y), ring(z)
    slot_of = lambda places, n: sum(jnp.where(places[s] == n, s, 0) for s in range(4))
    ids = jnp.stack(
        [
            jnp.asarray(v, jnp.int32)
            for v in [(z_hi ^ dz) * 4 + x_of[s] for dz in (0, 1) for s in (0, 2, 1, 3)]
            + [core]
            + [(z_hi ^ k) * 4 + x_of[s] for s in range(4) for k in (0, 1)]
            + [slot_of(z_of, (z_hi ^ k) * 2 + (z_lo ^ m)) for k in (0, 1) for m in (0, 1)]
            + [z_lo, z_lo ^ 1]
            + y_of
        ]
    )
    chain = Chain()

    def run(name, body, arrays, shapes, scratch=(), flops=1000, after=()):
        return chain(name, body, ids, arrays, shapes, scratch, flops, after)

    def codes(kind, base, width, rows, grads, arrays, after=()):
        return run(
            "gradient_codes",
            lambda *a: codes_body(kind, base, width, grads, *a),
            both_t + arrays,
            [((2, 4, 4, rows, width), BF)] * 2,
            [pltpu.VMEM((SHARD, width), F32)],
            flops=SMALL if base == 0 else COVER,
            after=after,
        )

    def add2(keep, first, after=()):
        gains = keep.shape[-2] > 80
        body = lambda *a: add2_body(gains, *a)
        return run("add_two", body, [keep, first], [(keep.shape[1:], BF)], after=after)[0]

    def add3(keep, first, second, after=()):
        gains = keep.shape[-2] > 80
        body = lambda *a: add3_body(gains, *a)
        shape = (2,) + keep.shape[2:]
        return run("add_three", body, [keep, first, second], [(shape, BF)] * 2, after=after)

    def direct(axis, slots):
        return [
            slots[0],
            swap(slots[1], axis, 1),
            swap(slots[2], axis, 0),
            swap(slots[3], axis + "_far"),
        ]

    w_mine, w_send = run("dequantize", dequant_body, [w_codes, w_scale], [((ROWS, KV), BF)] * 2)
    w_came = swap(w_send, "core")
    t_oth = swap(tokens, "core")
    both_t = [tokens, t_oth]
    gain2 = gain.reshape(1, KV)
    factors = 1.0 / jnp.concatenate(
        [
            lax.dynamic_slice_in_dim(grad_scale, core * 4, 4, axis=1),
            lax.dynamic_slice_in_dim(grad_scale, 8 + core * 4, 4, axis=1),
        ],
        axis=1,
    )
    cots = swap(run("halves", half_body, [value_cot, key_cot], [((2, TOK, HALF), BF)])[0], "core")

    def stack(a, b, after):
        return run("stack_shards", stack_body, [a, b], [((2, SHARD, QUART), BF)], after=after)[0]

    join = lambda own, oth: run("join_halves", halves_body, [own, oth], [((TOK, KV), BF)])[0]

    ka, kb = run("assemble", assemble_body, [w_mine, w_came], [((SHARD, QUART), BF)] * 2)
    k_g = swap(ka, "zb")
    k_x = swap(kb, "x", 0)
    k_s2 = stack(kb, k_x, [cots])
    k_q2 = swap(k_s2, "x", 1)
    k_za = swap(k_s2, "zb")
    k_s1 = stack(ka, k_g, [t_oth])
    k_r1 = swap(k_s1, "x", 0)
    k_q1 = swap(k_s1, "x", 1)
    v_cols = lambda ids, own, oth: (cot_columns(own, ids[CORE]), oth[0])
    v_keep, v_send = codes("y", 4, HALF, 80, v_cols, [value_cot, cots, factors])
    v_first = swap(v_send, "y", 0)
    k_q2 = run("pass_shards", pass_body, [k_q2], [((2, SHARD, QUART), BF)])[0]
    k_zc = swap(k_q2, "zb")
    k_p1 = swap(k_r1, "x", 1)
    k_early, k_late = [k_s1, k_r1, k_s2, k_q2], [k_q1, k_p1, k_za, k_zc]
    raw = run(
        "key_projection_early",
        early_body,
        both_t + k_early,
        [((2 * TOK, HALF), F32)],
        flops=3 * SMALL,
        after=[k_za],
    )[0]
    vw = run(
        "assemble", assemble_body, [w_mine, w_came], [((SHARD, HALF), BF)], after=[k_q1]
    )[0]
    v_x = swap(vw, "x", 0)
    raw, stats = run(
        "key_projection_late",
        late_body,
        both_t + k_late + [raw, key_cot, cots, gain2],
        [((2 * TOK, HALF), F32), ((2 * TOK, GROUP), F32)],
        flops=SMALL,
    )
    stats_oth = swap(stats, "core")
    v_s2, v_h2 = run(
        "stack_shards",
        stack_half_body,
        [vw, v_x],
        [((2, SHARD, HALF), BF), ((2, SHARD, QUART), BF)],
    )
    v_q2 = swap(v_s2, "x", 1)
    v_zs = swap(v_h2, "zb")
    k_own, k_oth, g_own, g_oth, gsum = run(
        "key_norm",
        norm_body,
        [raw, stats, stats_oth, key_cot, cots, gain2],
        [((TOK, HALF), BF)] * 4 + [((8, HALF), F32)],
    )
    a_cols = lambda ids, own, oth: (own[:, :QUART], oth[:, :QUART])
    a_keep, a_send = codes("y", 0, QUART, 96, a_cols, [g_own, g_oth, factors, gsum])
    a_first = swap(a_send, "y", 0)
    v_second = swap(add2(v_keep, v_first), "y", 1)
    v_os = swap(v_zs, "za")
    b_cols = lambda ids, own, oth: (own[:, QUART:], oth[:, QUART:])
    b_keep, b_send = codes("x", 2, QUART, 96, b_cols, [g_own, g_oth, factors, gsum], [v_zs, v_q2])
    b_first = swap(b_send, "x", 0)
    v_zq = swap(v_q2, "zb")
    a_second = swap(add2(a_keep, a_first), "y", 1)
    v_weights = [v_s2, v_q2, v_zs, v_os, v_zq]
    k_weights = k_early + k_late
    sent_near = run(
        "token_gradient",
        lambda *a: back_body(0, *a),
        [g_oth, cots] + k_weights + v_weights[:2],
        [((TOK, D // 2), BF)],
        flops=EARLY,
    )[0]
    v_part = run(
        "value_projection",
        lambda *a: value_body(0, *a),
        both_t + v_weights[:2],
        [((2 * TOK, HALF), F32)],
        flops=EARLY,
    )[0]
    b_second = swap(add2(b_keep, b_first), "x", 1)
    keys = join(k_own, swap(k_oth, "core"))
    a_keep, a_send = add3(a_keep, a_first, a_second)
    a_first = swap(a_send, "x", 0)
    v_keep, v_send = add3(v_keep, v_first, v_second)
    v_first = swap(v_send, "x", 0)
    b_keep, b_send = add3(b_keep, b_first, b_second)
    b_first = swap(b_send, "y", 0)
    sent = run(
        "token_gradient",
        lambda *a: back_body(1, *a),
        [g_oth, cots] + k_weights + v_weights[2:] + [sent_near],
        [((TOK, D), BF)],
        flops=COVER,
    )[0]
    received = swap(sent, "core")
    a_second = swap(add2(a_keep, a_first), "x", 1)
    b_second = swap(add2(b_keep, b_first), "y", 1)
    v_second = swap(add2(v_keep, v_first), "x", 1)
    v_own, v_oth = run(
        "value_projection",
        lambda *a: value_body(1, *a),
        both_t + v_weights[2:] + [v_part],
        [((TOK, HALF), BF)] * 2,
        [pltpu.VMEM((2 * TOK, HALF), F32)],
        flops=COVER,
    )
    z_slots = run(
        "merge_sums",
        merge_body,
        [a_keep, a_first, a_second, b_keep, b_first, b_second, v_keep, v_first, v_second],
        [((96, KV), BF)] * 4,
    )
    z_parts = direct("z", z_slots)
    grad_tokens, _ = run(
        "token_gradient_sum",
        lambda *a: back_body(2, *a),
        [g_own, value_cot] + k_weights + v_weights + [received],
        [((TOK, D), BF), ((8, GROUP), F32)],
        flops=COVER,
    )
    mine, theirs = run(
        "last_sum", last_body, z_parts, [((48, KV), F32)] * 2, [pltpu.VMEM((96, KV), F32)]
    )
    theirs = swap(theirs, "core")
    values = join(v_own, swap(v_oth, "core"))
    grad_codes, grad_gain = run(
        "place_codes", place_body, [mine, theirs], [((40, 2 * KV), F32), ((1, KV), F32)]
    )
    return (keys, values, grad_tokens, grad_codes, grad_gain.reshape(KV))


def solution(mesh):
    rows = P(("node", "group"), None)
    in_specs = (rows, P("node", None), P("node", None), P(), rows, rows, P())
    out_specs = (rows, rows, rows, rows, P())
    return jax.shard_map(
        on_device, mesh=mesh, in_specs=in_specs, out_specs=out_specs, check_vma=False
    )
```
